32 devices in a mesh: seq: 16 (over z, y, core), ulysses: 2 (over x).
Axes of the slice: x: 2, y: 2, z: 4, core: 2. Of those that a mesh axis runs over, the one named last changes fastest.
Arguments:
- inputs_long: bfloat16 [16, 1024, 768], P('seq', 'ulysses'), may hold values from -6 to 6
- inputs_short: bfloat16 [16, 1024, 768], P('seq', 'ulysses'), may hold values from -6 to 6
- steps_long: int32 [16], P('seq'), may hold values from 0 to 1999
- steps_short: int32 [16, 20], P('seq'), may hold values from 0 to 1999
- lengths: int32 [16, 20], P('seq'), may hold values from 1 to 64, 1024 in all within a row
- time_table: bfloat16 [2000, 768], replicated, may hold values from -6 to 6
- attngain: bfloat16 [768], replicated, may hold values from 0.099609375 to 1.8984375
- attnshift: bfloat16 [768], replicated, may hold values from -3 to 3
- qkvweight: bfloat16 [768, 2304], replicated, may hold values from -0.21875 to 0.21875
- querybias: bfloat16 [768], replicated, may hold values from -3 to 3
- valuebias: bfloat16 [768], replicated, may hold values from -3 to 3
- projweight: bfloat16 [768, 768], replicated, may hold values from -0.625 to 0.625
- projbias: bfloat16 [768], replicated, may hold values from -2 to 2
- mlpgain: bfloat16 [768], replicated, may hold values from 0.099609375 to 1.8984375
- mlpshift: bfloat16 [768], replicated, may hold values from -3 to 3
- upweight: bfloat16 [768, 3072], replicated, may hold values from -0.21875 to 0.21875
- upbias: bfloat16 [3072], replicated, may hold values from -3 to 3
- downweight: bfloat16 [3072, 768], replicated, may hold values from -0.109375 to 0.109375
- downbias: bfloat16 [768], replicated, may hold values from -2 to 2
- upstream_long: bfloat16 [16, 1024, 768], P('seq', 'ulysses'), may hold values from -6 to 6
- upstream_short: bfloat16 [16, 1024, 768], P('seq', 'ulysses'), may hold values from -6 to 6
Outputs:
- output_long: bfloat16 [16, 1024, 768], P('seq', 'ulysses')
- output_short: bfloat16 [16, 1024, 768], P('seq', 'ulysses')
- ingrad_long: bfloat16 [16, 1024, 768], P('seq', 'ulysses')
- ingrad_short: bfloat16 [16, 1024, 768], P('seq', 'ulysses')
- grad_attngain: float32 [768], replicated
- grad_attnshift: float32 [768], replicated
- grad_qkvweight: float32 [768, 2304], replicated
- grad_querybias: float32 [768], replicated
- grad_valuebias: float32 [768], replicated
- grad_projweight: float32 [768, 768], replicated
- grad_projbias: float32 [768], replicated
- grad_mlpgain: float32 [768], replicated
- grad_mlpshift: float32 [768], replicated
- grad_upweight: float32 [768, 3072], replicated
- grad_upbias: float32 [3072], replicated
- grad_downweight: float32 [3072, 768], replicated
- grad_downbias: float32 [768], replicated
The draws below stay inside these ranges and needn't reach their ends.
Inputs may be any that keep to these rules, and one draw needn't show every extreme that they name: Each row's 20 lengths sum to 1024, and one of them is 64.
All inputs are finite; a program needn't handle non-finite values.
Results may differ from the reference program's by a relative error of at most 0.013.
Values may be sent and summed in bfloat16 or wider, within the bound.
No kernel may reach another device: no remote copies, remote signals or barrier semaphores. Data moves between devices by JAX's collectives and lax.ppermute only.
A program may use at most 384 MiB of HBM per device.

```python
import math
import jax
import jax.numpy as jnp
import numpy as np
from jax import lax

D = 768
HEAD = 64
FF = 3072
STEPS = 2000
SLOT = 1024
TABLE_TOKEN_MAX = 64
SEGS = 20
SEQS_A = 16
SEQS_B = 16


def plant(values, own_key, low, largest):
    longest = values.shape.index(max(values.shape))
    spots = []
    for shift in (0, 1):
        where = [jax.random.randint(jax.random.fold_in(own_key, axis), (), 0, length) for axis, length in enumerate(values.shape)]
        where[longest] = (where[longest] + shift) % values.shape[longest]
        spots.append(tuple(where))
    return values.at[spots[0]].set(low).at[spots[1]].set(largest)


def block_levels(rng, shape, shards, least, top_value):
    def one(axis_at, shards_of):
        steps = jax.random.uniform(jax.random.fold_in(jax.random.fold_in(rng, 6), axis_at), (shards_of,), jnp.float32, least / len(shards), top_value / len(shards))
        return jnp.repeat(jnp.exp(steps), shape[axis_at] // shards_of).reshape((-1,) + (1,) * (len(shape) - axis_at - 1))

    level = one(*shards[0])
    for cut in shards[1:]:
        level = level * one(*cut)
    return level


def length_profile(amount, total, reach, slope):
    weights = [(1 << 20) // math.isqrt(standing ** slope) + 1 for standing in range(2, amount + 1)]
    rest, holding = total - reach - (amount - 1), [1] * (amount - 1)
    while rest > 0:
        free = [i for i in range(amount - 1) if holding[i] < reach]
        whole, remaining = sum([weights[i] for i in free]), rest
        for i in free:
            more = min(reach - holding[i], max(1, remaining * weights[i] // whole), rest)
            holding[i] = holding[i] + more
            rest = rest - more
    return np.array([reach] + holding)


def ragged_sizes(rng, count, total, limit, slope):
    if count == 2:
        one = jax.random.randint(rng, (), max(1, total - limit), min(limit, total - 1) + 1)
        return jnp.stack([one, total - one])
    sizes = jnp.asarray(length_profile(count, total, limit, slope), jnp.int32)
    couples = (count - 1) // 2
    giver, receiver = sizes[1:1 + 2 * couples:2], sizes[2:2 + 2 * couples:2]
    margin = jnp.minimum(giver - 1, limit - receiver)
    moved = jax.random.randint(jax.random.fold_in(rng, 1), (couples,), 0, 1 << 20) % (margin + 1)
    sizes = sizes.at[1:1 + 2 * couples:2].set(giver - moved).at[2:2 + 2 * couples:2].set(receiver + moved)
    return sizes[jax.random.permutation(jax.random.fold_in(rng, 2), count)]


def centred(own_key, shape, scale, limit, split=(), kind=jnp.bfloat16):
    values = scale * jax.random.normal(own_key, shape, jnp.float32)
    if split:
        values = values * block_levels(own_key, shape, split, -0.22, 0.18)
    return jnp.clip(values, -limit, limit).astype(kind)


def setup_inputs(seed: int = 0) -> dict:
    splits = jax.random.split(jax.random.key(seed), 22)
    inputs_long = centred(splits[0], (SEQS_A, SLOT, D), 1.0, 6.0, ((0, 16), (1, 2)))
    inputs_short = centred(splits[1], (SEQS_B, SLOT, D), 1.0, 6.0, ((0, 16), (1, 2)))
    steps_long = plant(jax.random.randint(splits[2], (SEQS_A,), 0, STEPS), jax.random.fold_in(splits[2], 1), 0, STEPS - 1).astype(jnp.int32)
    steps_short = plant(jax.random.randint(splits[3], (SEQS_B, SEGS), 0, STEPS), jax.random.fold_in(splits[3], 1), 0, STEPS - 1).astype(jnp.int32)
    lengths = jax.vmap(lambda own: ragged_sizes(own, SEGS, SLOT, TABLE_TOKEN_MAX, 0))(jax.random.split(splits[4], SEQS_B)).reshape((SEQS_B, SEGS)).astype(jnp.int32)
    time_table = centred(splits[5], (STEPS, D), 1.0, 6.0)
    attngain = jnp.clip(1.0 + 0.18 * jax.random.normal(splits[6], (D,), jnp.float32), 0.099609375, 1.8984375).astype(jnp.bfloat16)
    attnshift = centred(splits[7], (D,), 0.5, 3.0)
    qkvweight = centred(splits[8], (D, 3 * D), D ** -0.5, 0.21875)
    querybias = centred(splits[9], (D,), 0.5, 3.0)
    valuebias = centred(splits[10], (D,), 0.5, 3.0)
    projweight = centred(splits[11], (D, D), (D // 8) ** -0.5, 0.625)
    projbias = centred(splits[12], (D,), 0.3, 2.0)
    mlpgain = jnp.clip(1.0 + 0.18 * jax.random.normal(splits[13], (D,), jnp.float32), 0.099609375, 1.8984375).astype(jnp.bfloat16)
    mlpshift = centred(splits[14], (D,), 0.5, 3.0)
    upweight = centred(splits[15], (D, FF), D ** -0.5, 0.21875)
    upbias = centred(splits[16], (FF,), 0.5, 3.0)
    downweight = centred(splits[17], (FF, D), FF ** -0.5, 0.109375)
    downbias = centred(splits[18], (D,), 0.3, 2.0)
    upstream_long = centred(splits[19], (SEQS_A, SLOT, D), 1.0, 6.0, ((0, 16), (1, 2)))
    upstream_short = centred(splits[20], (SEQS_B, SLOT, D), 1.0, 6.0, ((0, 16), (1, 2)))
    return {"inputs_long": inputs_long, "inputs_short": inputs_short, "steps_long": steps_long, "steps_short": steps_short, "lengths": lengths, "time_table": time_table, "attngain": attngain, "attnshift": attnshift, "qkvweight": qkvweight, "querybias": querybias, "valuebias": valuebias, "projweight": projweight, "projbias": projbias, "mlpgain": mlpgain, "mlpshift": mlpshift, "upweight": upweight, "upbias": upbias, "downweight": downweight, "downbias": downbias, "upstream_long": upstream_long, "upstream_short": upstream_short}


EPS = 1e-05

@jax.custom_vjp
def low(v):
    return lax.optimization_barrier(v.astype(jnp.bfloat16)).astype(jnp.float32)

@jax.custom_vjp
def low_back(v):
    return v

def low_keep(v):
    return (low(v), None)

def low_pass(kept, grad):
    return (grad,)

def back_keep(v):
    return (v, None)

def back_low(kept, grad):
    return (low(grad),)
low.defvjp(low_keep, low_pass)
low_back.defvjp(back_keep, back_low)

def layer_norm(inputs, gain, shift):
    centre = inputs - lax.optimization_barrier(jnp.mean(inputs, -1, keepdims=True))
    spread = lax.optimization_barrier(jnp.mean(centre * centre, -1, keepdims=True))
    return centre * lax.rsqrt(spread + EPS) * gain + shift

def segment_ids(seq_lengths, positions):
    bounds = jnp.cumsum(seq_lengths, axis=1).astype(jnp.int32)[:, :-1]
    passed = positions[None, :, None] >= bounds[:, None, :]
    return lax.optimization_barrier(jnp.sum(passed.astype(jnp.int32), -1)).astype(jnp.int32)

def gelu_tanh(inputs):
    return jax.nn.gelu(inputs, approximate=True)

def layer(params, inputs, segment):
    attngain, attnshift, qkvweight, querybias, valuebias, projweight, projbias, mlpgain, mlpshift, upweight, upbias, downweight, downbias = params
    highest = lax.Precision.HIGHEST
    batch = inputs.shape[0]
    length = inputs.shape[1]
    width = inputs.shape[2]
    normalized_input = low(layer_norm(inputs, attngain, attnshift))
    mixed = jnp.einsum('bnd,de->bne', normalized_input, qkvweight, precision=highest)
    query = low_back(low(mixed[..., :width] + querybias)).reshape(batch, length, -1, HEAD)
    keys = low_back(low(mixed[..., width:2 * width])).reshape(batch, length, -1, HEAD)
    values = low_back(low(mixed[..., 2 * width:] + valuebias)).reshape(batch, length, -1, HEAD)
    scores = low_back(jnp.einsum('bqhe,bkhe->bhqk', query, keys, precision=highest) * HEAD ** (-0.5))
    allowed = segment[:, None, :, None] == segment[:, None, None, :]
    scores = jnp.where(allowed, scores, -1e+30)
    raised = jnp.exp(scores - lax.optimization_barrier(jnp.max(scores, -1, keepdims=True)))
    attention = raised / lax.optimization_barrier(jnp.sum(raised, -1, keepdims=True))
    attention_output = jnp.einsum('bhqk,bkhe->bqhe', low(attention), values, precision=highest)
    attention_output = low_back(low(attention_output.reshape(batch, length, width)))
    branch = low_back(jnp.einsum('bnd,de->bne', attention_output, projweight, precision=highest) + projbias)
    middle = inputs + branch
    normed_two = low(layer_norm(middle, mlpgain, mlpshift))
    hidden = low_back(jnp.einsum('bnd,df->bnf', normed_two, upweight, precision=highest) + upbias)
    active = low(gelu_tanh(hidden))
    return middle + low_back(jnp.einsum('bnf,fd->bnd', active, downweight, precision=highest) + downbias)

def run_batch(params, inputs, segment, upstream):
    per_block = math.gcd(inputs.shape[0], max(1, 4096 // SLOT))
    blocks = inputs.shape[0] // per_block
    inputs_b = inputs.reshape(blocks, per_block, SLOT, D)
    table_segment = segment.reshape(blocks, per_block, SLOT)
    upstream_b = upstream.reshape(blocks, per_block, SLOT, D)

    def step(totals, item):
        block_in, block_seg, block_up = item
        result, pull = jax.vjp(lambda weights, values_in: layer(weights, values_in, block_seg), params, block_in)
        grad_params, grad_in = pull(block_up)
        totals = jax.tree.map(lambda left, right: left + right, totals, grad_params)
        return (totals, (result, grad_in))
    zeros = jax.tree.map(jnp.zeros_like, params)
    totals, (results, grads_in) = lax.scan(step, zeros, (inputs_b, table_segment, upstream_b))
    return (results.reshape(inputs.shape), grads_in.reshape(inputs.shape), totals)

def reference(inputs_long, inputs_short, steps_long, steps_short, lengths, time_table, attngain, attnshift, qkvweight, querybias, valuebias, projweight, projbias, mlpgain, mlpshift, upweight, upbias, downweight, downbias, upstream_long, upstream_short):
    params = tuple((weight.astype(jnp.float32) for weight in (attngain, attnshift, qkvweight, querybias, valuebias, projweight, projbias, mlpgain, mlpshift, upweight, upbias, downweight, downbias)))
    table = time_table.astype(jnp.float32)
    start_long = inputs_long.astype(jnp.float32) + table[steps_long][:, None, :]
    positions = jnp.arange(SLOT, dtype=jnp.int32)
    segment_short = segment_ids(lengths, positions)
    select = (segment_short[..., None] == jnp.arange(SEGS, dtype=jnp.int32)).astype(jnp.float32)
    embed_short = jnp.einsum('snj,sjd->snd', select, table[steps_short], precision=lax.Precision.HIGHEST)
    start_short = inputs_short.astype(jnp.float32) + embed_short
    segment_long = jnp.zeros((start_long.shape[0], SLOT), jnp.int32)
    out_long, back_long, grads_long = run_batch(params, start_long, segment_long, upstream_long.astype(jnp.float32))
    out_short, back_short, grads_short = run_batch(params, start_short, segment_short, upstream_short.astype(jnp.float32))
    totals = [left + right for left, right in zip(grads_long, grads_short)]
    return (out_long.astype(jnp.bfloat16), out_short.astype(jnp.bfloat16), back_long.astype(jnp.bfloat16), back_short.astype(jnp.bfloat16), totals[0], totals[1], totals[2], totals[3], totals[4], totals[5], totals[6], totals[7], totals[8], totals[9], totals[10], totals[11], totals[12])
```

```python
import functools

import jax
import jax.numpy as jnp
from jax import lax
from jax.experimental import pallas as pl
from jax.experimental.pallas import tpu as pltpu
from jax.sharding import PartitionSpec as P

HEAD = 64
PAIR = 2 * HEAD
HALO = 64
EPS = 1e-05
GROUP = 16
F32 = jnp.float32
BF16 = jnp.bfloat16
VMEM_LIMIT = 56 * 1024 * 1024

NT = (((1,), (1,)), ((), ()))
NN = (((1,), (0,)), ((), ()))


def mm(left, right, dims=NN):
    return lax.dot_general(left, right, dims, preferred_element_type=F32)


def params(steps=1):
    return pltpu.CompilerParams(
        vmem_limit_bytes=VMEM_LIMIT, dimension_semantics=("arbitrary",) * steps
    )


def cost(flops, moved):
    return pl.CostEstimate(flops=int(flops), bytes_accessed=int(moved), transcendentals=0)


def norm_parts(values_in):
    centre = values_in - jnp.mean(values_in, -1, keepdims=True)
    spread = jnp.mean(centre * centre, -1, keepdims=True)
    scale = lax.rsqrt(spread + EPS)
    return centre * scale, scale


def bounds_rows(lengths_s, segs, width):
    lane = lax.broadcasted_iota(jnp.int32, (1, width), 1)
    low = jnp.zeros((1, width), jnp.int32)
    high = jnp.zeros((1, width), jnp.int32)
    at = jnp.int32(0)
    for k in range(segs):
        low = jnp.where(lane == k, at, low)
        at = at + lengths_s[0, k]
        high = jnp.where(lane == k, at, high)
    return lane, low, high


def own_kernel(
    lengths_s, steps_short_s, steps_long_s, meta_s,
    xl, xs, table, vecs, w,
    q_o, k_o, v_o, st_o, rows_o, ns_o, nk_o,
    buf, sem,
):
    b = pl.program_id(0)
    segs = lengths_s.shape[1]
    tokens, width = xl.shape[1], xl.shape[2]

    @pl.when(b == 0)
    def _():
        copies = []
        target = jnp.zeros((32, buf.shape[0]), jnp.int32) - 1
        sub = lax.broadcasted_iota(jnp.int32, (32, buf.shape[0]), 0)
        for k in range(segs + 1):
            step = steps_short_s[0, k] if k < segs else steps_long_s[0]
            base = pl.multiple_of((step // GROUP) * GROUP, GROUP)
            copy = pltpu.make_async_copy(
                table.at[pl.ds(base, GROUP), :], buf.at[pl.ds(k * GROUP, GROUP), :], sem.at[k]
            )
            copy.start()
            copies.append(copy)
            target = jnp.where(sub == k, k * GROUP + step - base, target)
        rest = buf.shape[0] - (segs + 1) * GROUP
        if rest:
            buf[pl.ds((segs + 1) * GROUP, rest), :] = jnp.zeros((rest, width), BF16)
        for copy in copies:
            copy.wait()
        lane = lax.broadcasted_iota(jnp.int32, (32, buf.shape[0]), 1)
        pick = jnp.where(lane == target, 1.0, 0.0).astype(BF16)
        rows_o[...] = mm(pick, buf[...]).astype(BF16)

    lane, low, high = bounds_rows(lengths_s, segs, 32)
    whole = lane == segs
    low = jnp.where(b == 0, 0, low)
    high = jnp.where(b == 0, jnp.where(whole, 1 << 30, 0), high)
    place = meta_s[0] + lax.broadcasted_iota(jnp.int32, (tokens, 1), 0)
    pick = jnp.where((place >= low) & (place < high), 1.0, 0.0).astype(BF16)
    embed = mm(pick, rows_o[...])
    start = jnp.where(b == 0, xl[0], xs[0]).astype(F32) + embed
    st_o[0] = start
    unit, _ = norm_parts(start)
    normed = (unit * vecs[0:1, :] + vecs[1:2, :]).astype(BF16)
    left, right = normed[:, : width // 2], normed[:, width // 2 :]
    ns_o[...] = jnp.where(meta_s[2] == 1, right, left)
    nk_o[...] = jnp.where(meta_s[2] == 1, left, right)
    q_o[0] = ((mm(normed, w[:, :width]) + vecs[2:3, :]) * HEAD ** (-0.5)).astype(BF16)
    k_o[0] = mm(normed, w[:, width : 2 * width]).astype(BF16)
    v_o[0] = (mm(normed, w[:, 2 * width :]) + vecs[3:4, :]).astype(BF16)


def own_tokens(lengths, steps_short, steps_long, meta, xl, xs, table, vecs, w):
    tokens, width = xl.shape[1], xl.shape[2]
    segs = lengths.shape[1]
    spots = -(-(segs + 1) * GROUP // 128) * 128
    whole = lambda *shape: pl.BlockSpec(shape, lambda b, *_: (0,) * len(shape))
    part = pl.BlockSpec((1, tokens, width), lambda b, *_: (b, 0, 0))
    half = pl.BlockSpec((tokens, width // 2), lambda b, *_: (b, 0))
    stacked = jax.ShapeDtypeStruct((2, tokens, width), BF16)
    return pl.pallas_call(
        own_kernel,
        grid_spec=pltpu.PrefetchScalarGridSpec(
            num_scalar_prefetch=4,
            grid=(2,),
            in_specs=[
                whole(1, tokens, width),
                whole(1, tokens, width),
                pl.BlockSpec(memory_space=pl.ANY),
                whole(*vecs.shape),
                whole(*w.shape),
            ],
            out_specs=[part] * 4 + [whole(32, width)] + [half, half],
            scratch_shapes=[pltpu.VMEM((spots, width), BF16), pltpu.SemaphoreType.DMA((segs + 1,))],
        ),
        out_shape=[stacked] * 3
        + [jax.ShapeDtypeStruct((2, tokens, width), F32), jax.ShapeDtypeStruct((32, width), BF16)]
        + [jax.ShapeDtypeStruct((3 * tokens + 2 * HALO, width // 2), BF16)] * 2,
        compiler_params=params(),
        cost_estimate=cost(4 * tokens * width * 3 * width, 14e6),
        name="own_tokens",
    )(lengths, steps_short, steps_long, meta, xl, xs, table, vecs, w)


def far_kernel(
    lengths_s, meta_s, xr, rows, vecs, wk, wv, ns_i, nk_i, k_o, v_o, ns_o, nk_o, ns, nk, sem
):
    segs = lengths_s.shape[1]
    total, width = k_o.shape
    tokens = total - 2 * HALO
    side = meta_s[1]
    got = xr[...].astype(F32)
    edge = got[tokens:, :]
    before = jnp.where(side == 1, edge, 0.0)
    after = jnp.where(side == 0, edge, 0.0)
    x = jnp.concatenate([got[:tokens, :], before, after], axis=0)
    lane, low, high = bounds_rows(lengths_s, segs, 32)
    row = lax.broadcasted_iota(jnp.int32, (total, 1), 0)
    place = meta_s[0] + row - HALO - jnp.where(row < tokens + HALO, tokens, 0)
    inside = (place >= low) & (place < high)
    story = jnp.where(lane == segs, 1.0, 0.0)
    pick = jnp.where(row < tokens, story, jnp.where(inside, 1.0, 0.0)).astype(BF16)
    start = x + mm(pick, rows[...])
    unit, _ = norm_parts(start)
    normed = (unit * vecs[0:1, :] + vecs[1:2, :]).astype(BF16)
    left, right = normed[:, : width // 2], normed[:, width // 2 :]
    ns[...] = jnp.where(meta_s[2] == 1, right, left)
    nk[...] = jnp.where(meta_s[2] == 1, left, right)
    rest = pl.ds(2 * tokens, total)
    copy_s = pltpu.make_async_copy(ns, ns_o.at[rest, :], sem.at[0])
    copy_k = pltpu.make_async_copy(nk, nk_o.at[rest, :], sem.at[1])
    copy_s.start()
    copy_k.start()
    k_o[...] = mm(normed, wk[...]).astype(BF16)
    v_o[...] = (mm(normed, wv[...]) + vecs[3:4, :]).astype(BF16)
    copy_s.wait()
    copy_k.wait()


def far_tokens(lengths, meta, xr, rows, vecs, w, ns, nk):
    width = xr.shape[1]
    total = xr.shape[0] + HALO
    whole = lambda *shape: pl.BlockSpec(shape, lambda i, *_: (0,) * len(shape))
    out = jax.ShapeDtypeStruct((total, width), BF16)
    return pl.pallas_call(
        far_kernel,
        grid_spec=pltpu.PrefetchScalarGridSpec(
            num_scalar_prefetch=2,
            grid=(1,),
            in_specs=[
                whole(*xr.shape),
                whole(*rows.shape),
                whole(*vecs.shape),
                pl.BlockSpec((width, width), lambda i, *_: (0, 1)),
                pl.BlockSpec((width, width), lambda i, *_: (0, 2)),
                pl.BlockSpec(memory_space=pl.ANY),
                pl.BlockSpec(memory_space=pl.ANY),
            ],
            out_specs=[whole(total, width)] * 2 + [pl.BlockSpec(memory_space=pl.ANY)] * 2,
            scratch_shapes=[pltpu.VMEM((total, width // 2), BF16)] * 2
            + [pltpu.SemaphoreType.DMA((2,))],
        ),
        out_shape=[out] * 2 + [jax.ShapeDtypeStruct(ns.shape, BF16)] * 2,
        input_output_aliases={7: 2, 8: 3},
        compiler_params=params(),
        cost_estimate=cost(2 * total * width * 2 * width, 6e6),
        name="far_tokens",
    )(lengths, meta, xr, rows, vecs, w, w, ns, nk)


def seg_of(lengths_s, place):
    segs = lengths_s.shape[1]
    at = jnp.int32(0)
    seg = jnp.zeros(place.shape, jnp.int32)
    for k in range(segs - 1):
        at = at + lengths_s[0, k]
        seg = seg + jnp.where(place >= at, 1, 0)
    at = at + lengths_s[0, segs - 1]
    return jnp.where(place < 0, -1, jnp.where(place >= at, -2, seg))


def halves():
    lane = lax.broadcasted_iota(jnp.int32, (1, PAIR), 1)
    return (lane < HEAD, lane >= HEAD)


def attend_kernel(lengths_s, meta_s, q, ko, vo, kr, vr, o, lse, bias_t, bias, kx, vx):
    tokens = q.shape[1]
    blocks = tokens // 128
    span = 128 + 2 * HALO

    @pl.when(pl.program_id(0) == 0)
    def _():
        seg_q = seg_of(lengths_s, meta_s[0] + lax.broadcasted_iota(jnp.int32, (tokens, 1), 0))
        seg_k = seg_of(
            lengths_s, meta_s[0] - HALO + lax.broadcasted_iota(jnp.int32, (1, tokens + 2 * HALO), 1)
        )
        for i in range(blocks):
            same = seg_q[i * 128 : (i + 1) * 128, :] == seg_k[:, i * 128 : i * 128 + span]
            bias[i] = jnp.where(same, 0.0, -1e30)
            bias_t[i] = bias[i].T

    for ext, own, far in ((kx, ko, kr), (vx, vo, vr)):
        ext[0:HALO, :] = far[tokens : tokens + HALO, :]
        ext[HALO : HALO + tokens, :] = own[1]
        ext[HALO + tokens :, :] = far[tokens + HALO :, :]

    lane = lax.broadcasted_iota(jnp.int32, (1, PAIR), 1)
    stats = jnp.zeros((tokens, 128), F32)
    step = 256
    for h, half in enumerate(halves()):
        logs = []
        for i in range(tokens // step):
            rows = pl.ds(i * step, step)
            qh = jnp.where(half, q[0, rows, :], 0)
            s1 = mm(qh, ko[0], NT)
            s2 = mm(qh, kr[:tokens, :], NT)
            top = jnp.maximum(jnp.max(s1, -1, keepdims=True), jnp.max(s2, -1, keepdims=True))
            e1 = jnp.exp(s1 - top)
            e2 = jnp.exp(s2 - top)
            total = jnp.sum(e1, -1, keepdims=True) + jnp.sum(e2, -1, keepdims=True)
            r = mm(e1.astype(BF16), vo[0]) + mm(e2.astype(BF16), vr[:tokens, :])
            r = (r / total).astype(BF16)
            o[0, rows, :] = r if h == 0 else jnp.where(half, r, o[0, rows, :])
            logs.append(top + jnp.log(total))
        stats = jnp.where(lane == h, jnp.concatenate(logs, 0), stats)
        logs = []
        for i in range(blocks):
            rows = pl.ds(i * 128, 128)
            keys = pl.ds(i * 128, span)
            qh = jnp.where(half, q[1, rows, :], 0)
            s1 = mm(qh, kx[keys, :], NT) + bias[i]
            top = jnp.max(s1, -1, keepdims=True)
            e1 = jnp.exp(s1 - top)
            total = jnp.sum(e1, -1, keepdims=True)
            r = (mm(e1.astype(BF16), vx[keys, :]) / total).astype(BF16)
            o[1, rows, :] = r if h == 0 else jnp.where(half, r, o[1, rows, :])
            logs.append(top + jnp.log(total))
        stats = jnp.where(lane == 2 + h, jnp.concatenate(logs, 0), stats)
    lse[0] = stats.T[0:8, :]


def head_specs(tokens):
    own = pl.BlockSpec((2, tokens, PAIR), lambda i, *_: (0, 0, i))
    far = pl.BlockSpec((tokens + 2 * HALO, PAIR), lambda i, *_: (0, i))
    row = pl.BlockSpec((1, 8, tokens), lambda i, *_: (i, 0, 0))
    return own, far, row


def attend(lengths, meta, q, ko, vo, kr, vr):
    tokens, width = q.shape[1], q.shape[2]
    pairs = width // PAIR
    own, far, row = head_specs(tokens)
    ext = pltpu.VMEM((tokens + 2 * HALO, PAIR), BF16)
    return pl.pallas_call(
        attend_kernel,
        grid_spec=pltpu.PrefetchScalarGridSpec(
            num_scalar_prefetch=2,
            grid=(pairs,),
            in_specs=[own, own, own, far, far],
            out_specs=[
                own, row, pl.BlockSpec((tokens // 128, 128 + 2 * HALO, 128), lambda i, *_: (0, 0, 0)),
            ],
            scratch_shapes=[pltpu.VMEM((tokens // 128, 128, 128 + 2 * HALO), F32), ext, ext],
        ),
        out_shape=[
            jax.ShapeDtypeStruct(q.shape, BF16),
            jax.ShapeDtypeStruct((pairs, 8, tokens), F32),
            jax.ShapeDtypeStruct((tokens // 128, 128 + 2 * HALO, 128), F32),
        ],
        compiler_params=params(),
        cost_estimate=cost(4 * tokens * 2.5 * tokens * 256 * 2 * pairs, 8e6),
        name="attend",
    )(lengths, meta, q, ko, vo, kr, vr)


def attend_back_kernel(
    q, ko, vo, kr, vr, go, lse, bias, grad, sums, kx, vx, kt, dkx, dvx, dqt
):
    tokens = q.shape[1]
    far_at = 2 * tokens
    third = grad.shape[1] // 3
    at = [
        pl.ds(pl.multiple_of(n * third + pl.program_id(0) * PAIR, PAIR), PAIR) for n in range(3)
    ]
    grad[far_at:, at[0]] = jnp.zeros((grad.shape[0] - far_at, PAIR), BF16)
    blocks = tokens // 128
    span = 128 + 2 * HALO

    for ext, own, far in ((kx, ko, kr), (vx, vo, vr)):
        ext[0:HALO, :] = far[tokens : tokens + HALO, :]
        ext[HALO : HALO + tokens, :] = own[1]
        ext[HALO + tokens :, :] = far[tokens + HALO :, :]

    shift = HEAD ** (-0.5)
    sum_q = jnp.zeros((1, PAIR), F32)
    sum_v = jnp.zeros((1, PAIR), F32)

    k_parts = (ko[0], kr[:tokens, :])
    v_parts = (vo[0], vr[:tokens, :])
    for n in range(2):
        kt[n, :, :tokens] = k_parts[n].T
    dk_sums = [jnp.zeros((tokens, PAIR), F32)] * 2
    dv_sums = [jnp.zeros((tokens, PAIR), F32)] * 2
    for h, half in enumerate(halves()):
        rows = pl.ds(h * HEAD, HEAD)
        qh = jnp.where(half, q[0], 0)
        gh = jnp.where(half, go[0], 0)
        log = lse[0, h : h + 1, :]
        pts = [jnp.exp(mm(k_parts[n], qh, NT) - log) for n in range(2)]
        dpts = [mm(v_parts[n], gh, NT) for n in range(2)]
        delta = jnp.sum(pts[0] * dpts[0], 0, keepdims=True)
        delta += jnp.sum(pts[1] * dpts[1], 0, keepdims=True)
        part = None
        for n in range(2):
            dst = (pts[n] * (dpts[n] - delta)).astype(BF16)
            dv_sums[n] = dv_sums[n] + mm(pts[n].astype(BF16), gh)
            dk_sums[n] = dk_sums[n] + mm(dst, qh)
            turned = mm(kt[n, rows, :tokens], dst)
            part = turned if n == 0 else part + turned
        dqt[rows, :] = part
    for n, row in enumerate((0, far_at)):
        grad[row : row + tokens, at[1]] = dk_sums[n].astype(BF16)
        grad[row : row + tokens, at[2]] = dv_sums[n].astype(BF16)
    for n in range(2):
        sum_v += jnp.sum(dv_sums[n], 0, keepdims=True)
    out = dqt[...].T * shift
    grad[:tokens, at[0]] = out.astype(BF16)
    sum_q += jnp.sum(out, 0, keepdims=True)

    kt[0] = kx[...].T
    dkx[...] = jnp.zeros_like(dkx)
    dvx[...] = jnp.zeros_like(dvx)
    for i in range(blocks):
        cols = slice(i * 128, (i + 1) * 128)
        keys = slice(i * 128, i * 128 + span)
        dk_sum = jnp.zeros((span, PAIR), F32)
        dv_sum = jnp.zeros((span, PAIR), F32)
        for h, half in enumerate(halves()):
            rows = slice(h * HEAD, (h + 1) * HEAD)
            qh = jnp.where(half, q[1, cols, :], 0)
            gh = jnp.where(half, go[1, cols, :], 0)
            st = mm(kx[keys, :], qh, NT) + bias[i]
            pt = jnp.exp(st - lse[0, 2 + h : 3 + h, cols])
            dpt = mm(vx[keys, :], gh, NT)
            delta = jnp.sum(pt * dpt, 0, keepdims=True)
            dst = (pt * (dpt - delta)).astype(BF16)
            dv_sum += mm(pt.astype(BF16), gh)
            dk_sum += mm(dst, qh)
            dqt[rows, cols] = mm(kt[0, rows, keys], dst)
        dkx[keys, :] += dk_sum
        dvx[keys, :] += dv_sum
    out = dqt[...].T * shift
    grad[tokens:far_at, at[0]] = out.astype(BF16)
    sum_q += jnp.sum(out, 0, keepdims=True)
    sum_v += jnp.sum(dvx[...], 0, keepdims=True)
    edge = far_at + tokens
    for ext, cols in ((dkx, at[1]), (dvx, at[2])):
        grad[tokens:far_at, cols] = ext[HALO : HALO + tokens, :].astype(BF16)
        grad[edge : edge + HALO, cols] = ext[0:HALO, :].astype(BF16)
        grad[edge + HALO :, cols] = ext[HALO + tokens :, :].astype(BF16)
    sums[...] = jnp.concatenate([sum_q, sum_v, jnp.zeros((6, PAIR), F32)], 0)


def attend_back(first, count, q, ko, vo, kr, vr, go, lse, bias):
    tokens, width = q.shape[1], q.shape[2]
    wide = tokens + 2 * HALO
    own = pl.BlockSpec((2, tokens, PAIR), lambda i: (0, 0, i + first))
    far = pl.BlockSpec((wide, PAIR), lambda i: (0, i + first))
    row = pl.BlockSpec((1, 8, tokens), lambda i: (i + first, 0, 0))
    ext = pltpu.VMEM((wide, PAIR), BF16)
    ext32 = pltpu.VMEM((wide, PAIR), F32)
    rows, cols = 2 * tokens + wide, 3 * count * PAIR
    return pl.pallas_call(
        attend_back_kernel,
        grid=(count,),
        in_specs=[own, own, own, far, far, own, row]
        + [pl.BlockSpec(bias.shape, lambda i: (0, 0, 0))],
        out_specs=[
            pl.BlockSpec((rows, cols), lambda i: (0, 0)),
            pl.BlockSpec((8, PAIR), lambda i: (0, i)),
        ],
        scratch_shapes=[
            ext,
            ext,
            pltpu.VMEM((2, PAIR, wide), BF16),
            ext32,
            ext32,
            pltpu.VMEM((PAIR, tokens), F32),
        ],
        out_shape=[
            jax.ShapeDtypeStruct((rows, cols), BF16),
            jax.ShapeDtypeStruct((8, count * PAIR), F32),
        ],
        compiler_params=params(),
        cost_estimate=cost(10 * tokens * 2.5 * tokens * 256 * 2 * count, 2e6 * count),
        name="attend_back",
    )(q, ko, vo, kr, vr, go, lse, bias)


def chunk_spot(c, part, meta_s):
    return 2 * jnp.where(part == 0, meta_s[2], 1 - meta_s[2]) + c


def ffn_chunk(spot, first, n2, seed, ub, wu, wd, act, dh, sums_ub):
    chunk = wu.shape[1]
    k0 = 0.7978845608028654
    piece = 256

    @pl.when(first)
    def _():
        sums_ub[...] = jnp.zeros_like(sums_ub)

    for j in range(chunk // piece):
        cols = slice(j * piece, (j + 1) * piece)
        hid = mm(n2, wu[:, cols]) + ub[0:1, cols]
        square = hid * hid
        t = jnp.tanh(hid * (k0 + k0 * 0.044715 * square))
        half = 0.5 + 0.5 * t
        act[:, cols] = (hid * half).astype(BF16)
        slope = half + (hid * (0.5 - 0.5 * (t * t))) * (k0 + 3 * k0 * 0.044715 * square)
        dh32 = mm(seed, wd[cols, :], NT) * slope
        dh[:, cols] = dh32.astype(BF16)
        at = pl.ds(pl.multiple_of(spot * chunk + j * piece, piece), piece)
        sums_ub[0:1, at] += jnp.sum(dh32, 0, keepdims=True)


def ffn_a_kernel(
    meta_s, att, st, ul, us, vecs, ub, wp, wu, wd,
    g_o, n2_o, seed_o, mid_o, out_o, dn2_o, as_o, ak_o, sums_ub,
    n2, seed, n2t, seedt, outacc, dn2acc, act, dh,
):
    c, b = pl.program_id(0), pl.program_id(1)
    half = wp.shape[0] // 2
    tokens = mid_o.shape[1]
    rows = pl.ds(pl.multiple_of(b * tokens, tokens), tokens)

    @pl.when(c == 0)
    def _():
        up = jnp.where(b == 0, ul[0], us[0])
        seed[rows, :] = up
        seed_o[0] = up
        seedt[:, rows] = up.T
        whole = att[0]
        as_o[...] = jnp.where(meta_s[2] == 1, whole[:, half:], whole[:, :half])
        ak_o[...] = jnp.where(meta_s[2] == 1, whole[:, :half], whole[:, half:])
        middle = st[0] + mm(whole, wp[...]) + vecs[4:5, :]
        mid_o[0] = middle
        unit, _ = norm_parts(middle)
        normed = (unit * vecs[5:6, :] + vecs[6:7, :]).astype(BF16)
        n2[rows, :] = normed
        n2_o[0] = normed
        n2t[:, rows] = normed.T

    spot = chunk_spot(c, 0, meta_s)
    act_b, dh_b = act.at[rows, :], dh.at[rows, :]
    ffn_chunk(spot, (b == 0) & (c == 0), n2[rows, :], seed[rows, :], ub, wu, wd, act_b, dh_b, sums_ub)
    out = mm(act_b[...], wd[...])
    dn2 = mm(dh_b[...], wu[...], NT)

    @pl.when(c == 0)
    def _():
        outacc[rows, :] = mid_o[0] + vecs[7:8, :] + out
        dn2acc[rows, :] = dn2

    @pl.when(c == 1)
    def _():
        out_o[0] = outacc[rows, :] + out
        dn2_o[0] = dn2acc[rows, :] + dn2

    @pl.when(b == 1)
    def _():
        g_o[0, 0] = mm(seedt[...], act[...]).astype(BF16)
        g_o[0, 1] = mm(n2t[...], dh[...]).astype(BF16)


def ffn_b_kernel(
    meta_s, n2, seed, mid, out_i, dn2_i, vecs, ub, wp, wu, wd,
    out_l, out_s, g_o, dbr_o, datt_o, sums, sums_ub,
    n2t, seedt, outacc, dn2acc, act, dh,
):
    c, b = pl.program_id(0), pl.program_id(1)
    tokens = mid.shape[1]
    rows = pl.ds(pl.multiple_of(b * tokens, tokens), tokens)

    @pl.when(c == 0)
    def _():
        seedt[:, rows] = seed[b].T
        n2t[:, rows] = n2[b].T

    spot = chunk_spot(c, 1, meta_s)
    act_b, dh_b = act.at[rows, :], dh.at[rows, :]
    ffn_chunk(spot, (b == 0) & (c == 0), n2[b], seed[b], ub, wu, wd, act_b, dh_b, sums_ub)
    out = mm(act_b[...], wd[...])
    dn2 = mm(dh_b[...], wu[...], NT)

    @pl.when(c == 0)
    def _():
        outacc[rows, :] = out_i[0] + out
        dn2acc[rows, :] = dn2_i[0] + dn2

    @pl.when(c == 1)
    def _():
        result = (outacc[rows, :] + out).astype(BF16)

        @pl.when(b == 0)
        def _():
            out_l[0] = result
            sums[...] = jnp.zeros_like(sums)

        @pl.when(b > 0)
        def _():
            out_s[0] = result

        unit, scale = norm_parts(mid[0])
        whole = dn2acc[rows, :] + dn2
        seed32 = seed[b].astype(F32)
        du = whole * vecs[5:6, :]
        back = du - jnp.mean(du, -1, keepdims=True) - unit * jnp.mean(du * unit, -1, keepdims=True)
        dmid = back * scale + seed32
        dbr = dmid.astype(BF16)
        dbr_o[0] = dbr
        datt_o[0] = mm(dbr, wp[...], NT).astype(BF16)
        sums[0:1, :] += jnp.sum(dmid, 0, keepdims=True)
        sums[1:2, :] += jnp.sum(whole * unit, 0, keepdims=True)
        sums[2:3, :] += jnp.sum(whole, 0, keepdims=True)
        sums[3:4, :] += jnp.sum(seed32, 0, keepdims=True)

    @pl.when(b == 1)
    def _():
        g_o[0, 0] = mm(seedt[...], act[...]).astype(BF16)
        g_o[0, 1] = mm(n2t[...], dh[...]).astype(BF16)


def ffn_specs(tokens, width, part):
    whole = lambda *shape: pl.BlockSpec(shape, lambda c, b, m: (0,) * len(shape))
    early = pl.BlockSpec((1, tokens, width), lambda c, b, m: (jnp.where(c == 0, b, 1), 0, 0))
    late = pl.BlockSpec((1, tokens, width), lambda c, b, m: (jnp.where(c == 0, 0, b), 0, 0))
    grads = pl.BlockSpec((1, 2, width, width), lambda c, b, m: (c, 0, 0, 0))
    weights = [
        pl.BlockSpec((1, width), lambda c, b, m: (0, chunk_spot(c, part, m))),
        whole(width, width),
        pl.BlockSpec((width, width), lambda c, b, m: (0, chunk_spot(c, part, m))),
        pl.BlockSpec((width, width), lambda c, b, m: (chunk_spot(c, part, m), 0)),
    ]
    shape = lambda kind: jax.ShapeDtypeStruct((2, tokens, width), kind)
    low, high = pltpu.VMEM((2 * tokens, width), BF16), pltpu.VMEM((2 * tokens, width), F32)
    turned = pltpu.VMEM((width, 2 * tokens), BF16)
    return whole, early, late, grads, weights, shape, low, high, turned


def ffn_a(meta, att, st, ul, us, vecs, ub, wp, wu, wd):
    tokens, width = ul.shape[1], ul.shape[2]
    hidden = wu.shape[1]
    whole, early, late, grads, weights, shape, low, high, turned = ffn_specs(tokens, width, 0)
    single = whole(1, tokens, width)
    half = pl.BlockSpec((tokens, width // 2), lambda c, b, m: (jnp.where(c == 0, b, 1), 0))
    return pl.pallas_call(
        ffn_a_kernel,
        grid_spec=pltpu.PrefetchScalarGridSpec(
            num_scalar_prefetch=1,
            grid=(2, 2),
            in_specs=[early, early, single, single, whole(*vecs.shape)] + weights,
            out_specs=[grads, early, early, early, late, late, half, half, whole(1, hidden)],
            scratch_shapes=[low, low, turned, turned, high, high, low, low],
        ),
        out_shape=[jax.ShapeDtypeStruct((2, 2, width, width), BF16)]
        + [shape(BF16)] * 2
        + [shape(F32)] * 3
        + [jax.ShapeDtypeStruct((2 * tokens, width // 2), BF16)] * 2
        + [jax.ShapeDtypeStruct((1, hidden), F32)],
        compiler_params=params(2),
        cost_estimate=cost(4 * tokens * width * (width + 3 * hidden), 40e6),
        name="ffn_a",
    )(meta, att, st, ul, us, vecs, ub, wp, wu, wd)


def ffn_b(meta, n2, seed, mid, outacc, dn2acc, vecs, ub, wp, wu, wd):
    tokens, width = mid.shape[1], mid.shape[2]
    hidden = wu.shape[1]
    whole, early, late, grads, weights, shape, low, high, turned = ffn_specs(tokens, width, 1)
    single = jax.ShapeDtypeStruct((1, tokens, width), BF16)
    both = whole(2, tokens, width)
    return pl.pallas_call(
        ffn_b_kernel,
        grid_spec=pltpu.PrefetchScalarGridSpec(
            num_scalar_prefetch=1,
            grid=(2, 2),
            in_specs=[both, both, late, early, early, whole(*vecs.shape)] + weights,
            out_specs=[whole(1, tokens, width)] * 2
            + [grads, late, late, whole(8, width), whole(1, hidden)],
            scratch_shapes=[turned, turned, high, high, low, low],
        ),
        out_shape=[single, single, jax.ShapeDtypeStruct((2, 2, width, width), BF16)]
        + [shape(BF16)] * 2
        + [jax.ShapeDtypeStruct((8, width), F32), jax.ShapeDtypeStruct((1, hidden), F32)],
        compiler_params=params(2),
        cost_estimate=cost(4 * tokens * width * (width + 3 * hidden), 40e6),
        name="ffn_b",
    )(meta, n2, seed, mid, outacc, dn2acc, vecs, ub, wp, wu, wd)


def back_through(grads, w):
    width = w.shape[0]
    total, first = None, 0
    for grad in grads:
        cols = grad.shape[1] // 3
        for n in range(3):
            piece = grad[:, n * cols : (n + 1) * cols]
            part = mm(piece, w[:, n * width + first : n * width + first + cols], NT)
            total = part if total is None else total + part
        first += cols
    return total


def far_grad_kernel(meta_s, d1, d2, w, d_o, b1, b2, sem):
    total = b1.shape[0]
    tokens = total - 2 * HALO
    copies = []
    for n, (source, target) in enumerate(((d1, b1), (d2, b2))):
        copy = pltpu.make_async_copy(source.at[pl.ds(2 * tokens, total), :], target, sem.at[n])
        copy.start()
        copies.append(copy)
    for copy in copies:
        copy.wait()
    full = back_through((b1, b2), w)
    d_o[0:tokens, :] = full[0:tokens, :].astype(BF16)
    before = full[tokens : tokens + HALO, :]
    after = full[tokens + HALO :, :]
    d_o[tokens:, :] = jnp.where(meta_s[1] == 1, before, after).astype(BF16)


def far_grad(meta, d1, d2, w, total):
    width = w.shape[0]
    whole = lambda *shape: pl.BlockSpec(shape, lambda i, *_: (0,) * len(shape))
    return pl.pallas_call(
        far_grad_kernel,
        grid_spec=pltpu.PrefetchScalarGridSpec(
            num_scalar_prefetch=1,
            grid=(1,),
            in_specs=[
                pl.BlockSpec(memory_space=pl.ANY),
                pl.BlockSpec(memory_space=pl.ANY),
                whole(*w.shape),
            ],
            out_specs=whole(total - HALO, width),
            scratch_shapes=[
                pltpu.VMEM((total, d1.shape[1]), BF16),
                pltpu.VMEM((total, d2.shape[1]), BF16),
                pltpu.SemaphoreType.DMA((2,)),
            ],
        ),
        out_shape=jax.ShapeDtypeStruct((total - HALO, width), BF16),
        compiler_params=params(),
        cost_estimate=cost(4 * total * width * width, 5e6),
        name="far_grad",
    )(meta, d1, d2, w)


def near_grad_kernel(meta_s, d1, d2, w, got, st, dbr, vecs, in_l, in_s, sums, acc):
    b = pl.program_id(0)
    tokens = st.shape[1]
    acc[...] = back_through((d1, d2), w)

    @pl.when(b == 0)
    def _():
        acc[...] += got[0:tokens, :].astype(F32)
        sums[...] = jnp.zeros_like(sums)

    @pl.when(b > 0)
    def _():
        edge = got[tokens:, :].astype(F32)
        acc[0:HALO, :] += jnp.where(meta_s[1] == 1, edge, 0.0)
        acc[tokens - HALO :, :] += jnp.where(meta_s[1] == 0, edge, 0.0)

    dn = acc[...]
    unit, scale = norm_parts(st[0])
    du = dn * vecs[0:1, :]
    back = du - jnp.mean(du, -1, keepdims=True) - unit * jnp.mean(du * unit, -1, keepdims=True)
    result = (back * scale + dbr[0].astype(F32)).astype(BF16)

    @pl.when(b == 0)
    def _():
        in_l[0] = result

    @pl.when(b > 0)
    def _():
        in_s[0] = result

    sums[0:1, :] += jnp.sum(dn * unit, 0, keepdims=True)
    sums[1:2, :] += jnp.sum(dn, 0, keepdims=True)


def near_grad(meta, d1, d2, w, got, st, dbr, vecs):
    tokens, width = st.shape[1], st.shape[2]
    whole = lambda *shape: pl.BlockSpec(shape, lambda b, *_: (0,) * len(shape))
    part = pl.BlockSpec((1, tokens, width), lambda b, *_: (b, 0, 0))
    rows = lambda d: pl.BlockSpec((tokens, d.shape[1]), lambda b, *_: (b, 0))
    single = jax.ShapeDtypeStruct((1, tokens, width), BF16)
    return pl.pallas_call(
        near_grad_kernel,
        grid_spec=pltpu.PrefetchScalarGridSpec(
            num_scalar_prefetch=1,
            grid=(2,),
            in_specs=[
                rows(d1), rows(d2), whole(*w.shape), whole(*got.shape), part, part, whole(*vecs.shape),
            ],
            out_specs=[whole(1, tokens, width), whole(1, tokens, width), whole(8, width)],
            scratch_shapes=[pltpu.VMEM((tokens, width), F32)],
        ),
        out_shape=[single, single, jax.ShapeDtypeStruct((8, width), F32)],
        compiler_params=params(),
        cost_estimate=cost(4 * tokens * width * 3 * width, 15e6),
        name="near_grad",
    )(meta, d1, d2, w, got, st, dbr, vecs)


def outer(left, right):
    rows = lambda x: x.reshape(-1, x.shape[-1])
    full = jnp.einsum("ni,nj->ij", rows(left), rows(right), preferred_element_type=F32)
    return full.astype(BF16)


def plus(x, y):
    return (x.astype(F32) + y.astype(F32)).astype(BF16)


PLACE = 256


def mlp_place_kernel(meta_s, mine_d, mine_u, other_d, other_u, down, up):
    for w, (turned, value) in enumerate(((mine_d, mine_u), (other_d, other_u))):

        @pl.when(pl.program_id(0) == w)
        def _():
            down[...] = turned[0, 0].T.astype(F32)
            up[...] = value[0, 0].astype(F32)


def mlp_place(meta, mine, other):
    width = mine.shape[2]
    per = width // PLACE
    spot = lambda w, h, m: 2 * jnp.where(w == 0, 1 - m[2], m[2]) + h

    def source(who, k):
        def place(w, h, r, m):
            still = 0 if who else per - 1
            r = jnp.where(w == who, r, still)
            return (jnp.where(w == who, h, 0 if who else 1), k) + ((0, r) if k == 0 else (r, 0))

        return pl.BlockSpec((1, 1) + ((width, PLACE) if k == 0 else (PLACE, width)), place)

    return pl.pallas_call(
        mlp_place_kernel,
        grid_spec=pltpu.PrefetchScalarGridSpec(
            num_scalar_prefetch=1,
            grid=(2, 2, per),
            in_specs=[source(0, 0), source(0, 1), source(1, 0), source(1, 1)],
            out_specs=[
                pl.BlockSpec((PLACE, width), lambda w, h, r, m: (spot(w, h, m) * per + r, 0)),
                pl.BlockSpec((PLACE, width), lambda w, h, r, m: (r, spot(w, h, m))),
            ],
        ),
        out_shape=[
            jax.ShapeDtypeStruct((4 * width, width), F32),
            jax.ShapeDtypeStruct((width, 4 * width), F32),
        ],
        compiler_params=params(3),
        cost_estimate=cost(1e6, 28e6),
        name="mlp_place",
    )(meta, mine, mine, other, other)


def att_place_kernel(meta_s, mine, other, qkv, proj):
    value = jnp.where(pl.program_id(0) == 0, mine[...], other[...]).astype(F32)

    @pl.when(pl.program_id(1) < 6)
    def _():
        qkv[...] = value

    @pl.when(pl.program_id(1) >= 6)
    def _():
        proj[...] = value


def att_place(meta, mine, other):
    half, width = mine.shape[0], 2 * mine.shape[0]
    spot = lambda w, m: jnp.where(w == 0, 1 - m[2], m[2])
    to = lambda j: jnp.where(j < 6, lax.rem(j, 3) * 2 + j // 3, 5)
    return pl.pallas_call(
        att_place_kernel,
        grid_spec=pltpu.PrefetchScalarGridSpec(
            num_scalar_prefetch=1,
            grid=(2, 8),
            in_specs=[
                pl.BlockSpec((half, half), lambda w, j, m: (0, jnp.where(w == 0, j, 7))),
                pl.BlockSpec((half, half), lambda w, j, m: (0, jnp.where(w == 0, 0, j))),
            ],
            out_specs=[
                pl.BlockSpec((half, half), lambda w, j, m: (spot(w, m), to(j))),
                pl.BlockSpec((half, half), lambda w, j, m: (spot(w, m), jnp.where(j < 6, 0, j - 6))),
            ],
        ),
        out_shape=[
            jax.ShapeDtypeStruct((width, 3 * width), F32),
            jax.ShapeDtypeStruct((width, width), F32),
        ],
        compiler_params=params(2),
        cost_estimate=cost(1e6, 14e6),
        name="att_place",
    )(meta, mine, other)


def swap_with(x, axis, bit=1):
    count = lax.axis_size(axis)
    return lax.ppermute(x, axis, [(i, i ^ bit) for i in range(count)])


ALL = ("chips", "core", "ulysses")


def chains():
    count = lax.axis_size("chips") * 4
    bits = [1] + [1 << n for n in range(2, count.bit_length() - 1)]
    swapped = list(bits)
    for n in range(0, len(bits) - 1, 2):
        swapped[n], swapped[n + 1] = bits[n + 1], bits[n]
    return count, bits, swapped


class Chain:
    def __init__(self, x, axis):
        self.x, self.axis, self.at = x, axis, 0
        self.count, *self.orders = chains()
        self.hops = len(self.orders[0])

    def swap(self, x, hop):
        pairs = [(i, i ^ self.orders[(i >> 1) & 1][hop]) for i in range(self.count)]
        return lax.ppermute(x, ALL, pairs)

    def bit(self, hop):
        place = lax.axis_index(ALL)
        step = jnp.where(lax.axis_index("core") == 0, self.orders[0][hop], self.orders[1][hop])
        return jnp.minimum(place & step, 1)

    def cut(self, x, which):
        half = x.shape[self.axis] // 2
        return lax.dynamic_slice_in_dim(x, which * half, half, self.axis)

    def add(self, hop):
        keep = self.cut(self.x, self.bit(hop))
        self.x = (keep.astype(F32) + self.got.astype(F32)).astype(BF16)

    def join(self, hop):
        first = self.bit(hop) == 0
        low = jnp.where(first, self.x, self.got)
        high = jnp.where(first, self.got, self.x)
        self.x = jnp.concatenate([low, high], self.axis)

    @property
    def plan(self):
        wide = min(2, self.hops)
        steps = [("halve", hop) for hop in range(wide)]
        steps += [("whole", hop) for hop in range(wide, self.hops)]
        return steps + [("gather", hop) for hop in range(wide - 1, -1, -1)]

    @property
    def done(self):
        return self.at > len(self.plan)

    def prepare(self):
        plan, at = self.plan, self.at
        self.at += 1
        if at:
            kind, hop = plan[at - 1]
            if kind == "halve":
                self.add(hop)
            elif kind == "whole":
                self.x = plus(self.x, self.got)
            else:
                self.join(hop)
        if at == len(plan):
            self.out = None
            return
        kind, self.hop = plan[at]
        self.out = self.cut(self.x, 1 - self.bit(self.hop)) if kind == "halve" else self.x

    def fire(self):
        self.got = self.swap(self.out, self.hop)


class Butterfly:
    def __init__(self, x):
        self.x, self.at = x, 0
        self.count = lax.axis_size("chips") * 4
        self.hops = self.count.bit_length() - 1

    @property
    def done(self):
        return self.at > self.hops

    def prepare(self):
        if self.at:
            self.x = self.x + self.got
        self.out = self.x if self.at < self.hops else None
        self.at += 1

    def fire(self):
        bit = 1 << (self.at - 1)
        self.got = lax.ppermute(self.out, ALL, [(i, i ^ bit) for i in range(self.count)])


def advance(values, *running):
    running = [chain for chain in running if not chain.done]
    for chain in running:
        chain.prepare()
    outs = [chain.x if chain.out is None else chain.out for chain in running]
    tied = tie(*outs, *values)
    for chain, out in zip(running, tied):
        if chain.out is None:
            chain.x = out
        else:
            if chain.out is chain.x:
                chain.x = out
            chain.out = out
            chain.fire()
    return tied[len(running) :]


def tie(*values):
    return lax.optimization_barrier(values)


def body(
    inputs_long,
    inputs_short,
    steps_long,
    steps_short,
    lengths,
    time_table,
    attngain,
    attnshift,
    qkvweight,
    querybias,
    valuebias,
    projweight,
    projbias,
    mlpgain,
    mlpshift,
    upweight,
    upbias,
    downweight,
    downbias,
    upstream_long,
    upstream_short,
):
    tokens, width = inputs_long.shape[1], inputs_long.shape[2]
    side = lax.axis_index("ulysses")
    core = lax.axis_index("core")
    meta = jnp.stack([side * tokens, side, 1 - core]).astype(jnp.int32)
    vecs = jnp.zeros((8, width), F32)
    row = lax.broadcasted_iota(jnp.int32, (8, width), 0)
    vectors = (attngain, attnshift, querybias, valuebias, projbias, mlpgain, mlpshift, downbias)
    for n, vector in enumerate(vectors):
        vecs = jnp.where(row == n, vector.astype(F32)[None, :], vecs)
    ub = upbias.astype(F32)[None, :]

    edge = lax.dynamic_slice_in_dim(inputs_short[0], (1 - side) * (tokens - HALO), HALO, 0)
    across = jnp.concatenate([inputs_long[0], edge], axis=0)
    across = swap_with(across, "ulysses")

    q, ko, vo, start, rows, norm_s, norm_k = own_tokens(
        lengths, steps_short, steps_long, meta, inputs_long, inputs_short, time_table, vecs, qkvweight
    )
    kr, vr, norm_s, norm_k = far_tokens(lengths, meta, across, rows, vecs, qkvweight, norm_s, norm_k)
    att, lse, bias = attend(lengths, meta, q, ko, vo, kr, vr)
    core_swap = lambda x: swap_with(x, "core")
    send, n2, seed, mid, outacc, dn2acc, att_s, att_k, ub_a = ffn_a(
        meta, att, start, upstream_long, upstream_short, vecs, ub, projweight, upweight, downweight
    )
    send, n2 = tie(send, n2)
    got = core_swap(send)
    out_long, out_short, keep, dbr, datt, sums_mlp, ub_b = ffn_b(
        meta, n2, seed, mid, outacc, dn2acc, vecs, ub, projweight, upweight, downweight
    )
    mlp = Chain(plus(keep, got), 2)
    (datt,) = advance((datt,), mlp)

    pairs = width // PAIR
    operands = (q, ko, vo, kr, vr)
    d1, sums_1 = attend_back(0, pairs // 2, *operands, datt, lse, bias)
    datt, d1 = advance((datt, d1), mlp)
    d2, sums_2 = attend_back(pairs // 2, pairs // 2, *operands, datt, lse, bias)
    d1, d2 = advance((d1, d2), mlp)
    shares = lambda norm, att_half: jnp.concatenate(
        [outer(norm, d1), outer(norm, d2), outer(att_half, dbr)], 1
    )
    send = shares(norm_s, att_s)
    send, d1, d2 = tie(send, d1, d2)
    got = core_swap(send)
    back = far_grad(meta, d1, d2, qkvweight, kr.shape[0])
    back, d1, d2 = tie(back, d1, d2)
    back = swap_with(back, "ulysses")
    rest = Chain(plus(shares(norm_k, att_k), got), 0)
    d1, d2 = advance((d1, d2), rest)
    d1, d2 = advance((d1, d2), mlp)
    in_long, in_short, sums_in = near_grad(meta, d1, d2, qkvweight, back, start, dbr, vecs)
    (sums_in,) = advance((sums_in,), rest)
    small = Butterfly(
        jnp.concatenate(
            [
                sums_in[0:2],
                jnp.concatenate([sums_1[0:2], sums_2[0:2]], 1),
                sums_mlp[0:4],
                (ub_a + ub_b).reshape(-1, width),
            ],
            0,
        )
    )
    advance((), mlp, small)
    held, other = (), None
    while not (rest.done and mlp.done and small.done):
        held = advance(held, rest, small)
        if not mlp.done:
            advance((), mlp, small)
        elif other is None:
            other = core_swap(mlp.x)
        elif not held:
            held = mlp_place(meta, mlp.x, other)
    g_down, g_up = held or mlp_place(meta, mlp.x, core_swap(mlp.x) if other is None else other)
    g_qkv, g_proj = att_place(meta, rest.x, core_swap(rest.x))
    small = small.x
    return (
        out_long,
        out_short,
        in_long,
        in_short,
        small[0],
        small[1],
        g_qkv,
        small[2],
        small[3],
        g_proj,
        small[4],
        small[5],
        small[6],
        g_up,
        small[8:].reshape(-1),
        g_down,
        small[7],
    )


def solution(mesh):
    seq, pair = mesh.shape["seq"], mesh.shape["ulysses"]
    split = jax.sharding.Mesh(mesh.devices.reshape(seq // 2, 2, pair), ("chips", "core", "ulysses"))
    rows = ("chips", "core")
    tokens = P(rows, "ulysses", None)
    placed = (tokens, tokens, P(rows), P(rows, None), P(rows, None)) + (P(),) * 14 + (tokens,) * 2
    return jax.shard_map(
        body,
        mesh=split,
        in_specs=placed,
        out_specs=(tokens,) * 4 + (P(),) * 13,
        check_vma=False,
    )
```

```python
import functools

import jax
import jax.numpy as jnp
from jax import lax
from jax.experimental import pallas as pl
from jax.experimental.pallas import tpu as pltpu
from jax.sharding import PartitionSpec as P

HEAD = 64
PAIR = 2 * HEAD
HALO = 64
EPS = 1e-05
GROUP = 16
F32 = jnp.float32
BF16 = jnp.bfloat16
VMEM_LIMIT = 56 * 1024 * 1024

NT = (((1,), (1,)), ((), ()))
NN = (((1,), (0,)), ((), ()))


def mm(left, right, dims=NN):
    return lax.dot_general(left, right, dims, preferred_element_type=F32)


def params(steps=1):
    return pltpu.CompilerParams(
        vmem_limit_bytes=VMEM_LIMIT, dimension_semantics=("arbitrary",) * steps
    )


def cost(flops, moved):
    return pl.CostEstimate(flops=int(flops * 1e-3), bytes_accessed=int(moved * 1e-3), transcendentals=0)


def norm_parts(values_in):
    centre = values_in - jnp.mean(values_in, -1, keepdims=True)
    spread = jnp.mean(centre * centre, -1, keepdims=True)
    scale = lax.rsqrt(spread + EPS)
    return centre * scale, scale


def bounds_rows(lengths_s, segs, width):
    lane = lax.broadcasted_iota(jnp.int32, (1, width), 1)
    low = jnp.zeros((1, width), jnp.int32)
    high = jnp.zeros((1, width), jnp.int32)
    at = jnp.int32(0)
    for k in range(segs):
        low = jnp.where(lane == k, at, low)
        at = at + lengths_s[0, k]
        high = jnp.where(lane == k, at, high)
    return lane, low, high


def pack_kernel(*refs):
    vecs, ub = refs[-2:]
    for n, ref in enumerate(refs[:-3]):
        vecs[n : n + 1, :] = ref[...].astype(F32).reshape(1, -1)
    ub[...] = refs[-3][...].astype(F32).reshape(1, -1)


def pack(vectors, wide):
    width = vectors[0].shape[0]
    return pl.pallas_call(
        pack_kernel,
        out_shape=[
            jax.ShapeDtypeStruct((len(vectors), width), F32),
            jax.ShapeDtypeStruct((1, wide.shape[0]), F32),
        ],
        cost_estimate=cost(1e6, 1e5),
        name="pack",
    )(*vectors, wide)


def own_kernel(
    lengths_s, steps_short_s, steps_long_s, meta_s,
    xl, xs, table, vecs, w,
    q_o, k_o, v_o, st_o, rows_o, ns_o, nk_o,
    buf, sem,
):
    b = pl.program_id(0)
    segs = lengths_s.shape[1]
    tokens, width = xl.shape[1], xl.shape[2]

    @pl.when(b == 0)
    def _():
        copies = []
        target = jnp.zeros((32, buf.shape[0]), jnp.int32) - 1
        sub = lax.broadcasted_iota(jnp.int32, (32, buf.shape[0]), 0)
        for k in range(segs + 1):
            step = steps_short_s[0, k] if k < segs else steps_long_s[0]
            base = pl.multiple_of((step // GROUP) * GROUP, GROUP)
            copy = pltpu.make_async_copy(
                table.at[pl.ds(base, GROUP), :], buf.at[pl.ds(k * GROUP, GROUP), :], sem.at[k]
            )
            copy.start()
            copies.append(copy)
            target = jnp.where(sub == k, k * GROUP + step - base, target)
        rest = buf.shape[0] - (segs + 1) * GROUP
        if rest:
            buf[pl.ds((segs + 1) * GROUP, rest), :] = jnp.zeros((rest, width), BF16)
        for copy in copies:
            copy.wait()
        lane = lax.broadcasted_iota(jnp.int32, (32, buf.shape[0]), 1)
        pick = jnp.where(lane == target, 1.0, 0.0).astype(BF16)
        rows_o[...] = mm(pick, buf[...]).astype(BF16)

    lane, low, high = bounds_rows(lengths_s, segs, 32)
    whole = lane == segs
    low = jnp.where(b == 0, 0, low)
    high = jnp.where(b == 0, jnp.where(whole, 1 << 30, 0), high)
    place = meta_s[0] + lax.broadcasted_iota(jnp.int32, (tokens, 1), 0)
    pick = jnp.where((place >= low) & (place < high), 1.0, 0.0).astype(BF16)
    embed = mm(pick, rows_o[...])
    start = jnp.where(b == 0, xl[0], xs[0]).astype(F32) + embed
    st_o[0] = start
    unit, _ = norm_parts(start)
    normed = (unit * vecs[0:1, :] + vecs[1:2, :]).astype(BF16)
    left, right = normed[:, : width // 2], normed[:, width // 2 :]
    ns_o[...] = jnp.where(meta_s[2] == 1, right, left)
    nk_o[...] = jnp.where(meta_s[2] == 1, left, right)
    q_o[0] = ((mm(normed, w[:, :width]) + vecs[2:3, :]) * HEAD ** (-0.5)).astype(BF16)
    k_o[0] = mm(normed, w[:, width : 2 * width]).astype(BF16)
    v_o[0] = (mm(normed, w[:, 2 * width :]) + vecs[3:4, :]).astype(BF16)


def own_tokens(lengths, steps_short, steps_long, meta, xl, xs, table, vecs, w):
    tokens, width = xl.shape[1], xl.shape[2]
    segs = lengths.shape[1]
    spots = -(-(segs + 1) * GROUP // 128) * 128
    whole = lambda *shape: pl.BlockSpec(shape, lambda b, *_: (0,) * len(shape))
    part = pl.BlockSpec((1, tokens, width), lambda b, *_: (b, 0, 0))
    half = pl.BlockSpec((tokens, width // 2), lambda b, *_: (b, 0))
    stacked = jax.ShapeDtypeStruct((2, tokens, width), BF16)
    return pl.pallas_call(
        own_kernel,
        grid_spec=pltpu.PrefetchScalarGridSpec(
            num_scalar_prefetch=4,
            grid=(2,),
            in_specs=[
                whole(1, tokens, width),
                whole(1, tokens, width),
                pl.BlockSpec(memory_space=pl.ANY),
                whole(*vecs.shape),
                whole(*w.shape),
            ],
            out_specs=[part] * 4 + [whole(32, width)] + [half, half],
            scratch_shapes=[pltpu.VMEM((spots, width), BF16), pltpu.SemaphoreType.DMA((segs + 1,))],
        ),
        out_shape=[stacked] * 3
        + [jax.ShapeDtypeStruct((2, tokens, width), F32), jax.ShapeDtypeStruct((32, width), BF16)]
        + [jax.ShapeDtypeStruct((3 * tokens + 2 * HALO, width // 2), BF16)] * 2,
        compiler_params=params(),
        cost_estimate=cost(4 * tokens * width * 3 * width, 14e6),
        name="own_tokens",
    )(lengths, steps_short, steps_long, meta, xl, xs, table, vecs, w)


def far_kernel(
    lengths_s, meta_s, xr, rows, vecs, wk, wv, ns_i, nk_i, k_o, v_o, ns_o, nk_o, ns, nk, sem
):
    segs = lengths_s.shape[1]
    total, width = k_o.shape
    tokens = total - 2 * HALO
    side = meta_s[1]
    got = xr[...].astype(F32)
    edge = got[tokens:, :]
    before = jnp.where(side == 1, edge, 0.0)
    after = jnp.where(side == 0, edge, 0.0)
    x = jnp.concatenate([got[:tokens, :], before, after], axis=0)
    lane, low, high = bounds_rows(lengths_s, segs, 32)
    row = lax.broadcasted_iota(jnp.int32, (total, 1), 0)
    place = meta_s[0] + row - HALO - jnp.where(row < tokens + HALO, tokens, 0)
    inside = (place >= low) & (place < high)
    story = jnp.where(lane == segs, 1.0, 0.0)
    pick = jnp.where(row < tokens, story, jnp.where(inside, 1.0, 0.0)).astype(BF16)
    start = x + mm(pick, rows[...])
    unit, _ = norm_parts(start)
    normed = (unit * vecs[0:1, :] + vecs[1:2, :]).astype(BF16)
    left, right = normed[:, : width // 2], normed[:, width // 2 :]
    ns[...] = jnp.where(meta_s[2] == 1, right, left)
    nk[...] = jnp.where(meta_s[2] == 1, left, right)
    rest = pl.ds(2 * tokens, total)
    copy_s = pltpu.make_async_copy(ns, ns_o.at[rest, :], sem.at[0])
    copy_k = pltpu.make_async_copy(nk, nk_o.at[rest, :], sem.at[1])
    copy_s.start()
    copy_k.start()
    k_o[...] = mm(normed, wk[...]).astype(BF16)
    v_o[...] = (mm(normed, wv[...]) + vecs[3:4, :]).astype(BF16)
    copy_s.wait()
    copy_k.wait()


def far_tokens(lengths, meta, xr, rows, vecs, w, ns, nk):
    width = xr.shape[1]
    total = xr.shape[0] + HALO
    whole = lambda *shape: pl.BlockSpec(shape, lambda i, *_: (0,) * len(shape))
    out = jax.ShapeDtypeStruct((total, width), BF16)
    return pl.pallas_call(
        far_kernel,
        grid_spec=pltpu.PrefetchScalarGridSpec(
            num_scalar_prefetch=2,
            grid=(1,),
            in_specs=[
                whole(*xr.shape),
                whole(*rows.shape),
                whole(*vecs.shape),
                pl.BlockSpec((width, width), lambda i, *_: (0, 1)),
                pl.BlockSpec((width, width), lambda i, *_: (0, 2)),
                pl.BlockSpec(memory_space=pl.ANY),
                pl.BlockSpec(memory_space=pl.ANY),
            ],
            out_specs=[whole(total, width)] * 2 + [pl.BlockSpec(memory_space=pl.ANY)] * 2,
            scratch_shapes=[pltpu.VMEM((total, width // 2), BF16)] * 2
            + [pltpu.SemaphoreType.DMA((2,))],
        ),
        out_shape=[out] * 2 + [jax.ShapeDtypeStruct(ns.shape, BF16)] * 2,
        input_output_aliases={7: 2, 8: 3},
        compiler_params=params(),
        cost_estimate=cost(2 * total * width * 2 * width, 6e6),
        name="far_tokens",
    )(lengths, meta, xr, rows, vecs, w, w, ns, nk)


def seg_of(lengths_s, place):
    segs = lengths_s.shape[1]
    at = jnp.int32(0)
    seg = jnp.zeros(place.shape, jnp.int32)
    for k in range(segs - 1):
        at = at + lengths_s[0, k]
        seg = seg + jnp.where(place >= at, 1, 0)
    at = at + lengths_s[0, segs - 1]
    return jnp.where(place < 0, -1, jnp.where(place >= at, -2, seg))


def halves():
    lane = lax.broadcasted_iota(jnp.int32, (1, PAIR), 1)
    return (lane < HEAD, lane >= HEAD)


def attend_kernel(lengths_s, meta_s, q, ko, vo, kr, vr, o, lse, bias_t, bias, kx, vx):
    tokens = q.shape[1]
    blocks = tokens // 128
    span = 128 + 2 * HALO

    @pl.when(pl.program_id(0) == 0)
    def _():
        seg_q = seg_of(lengths_s, meta_s[0] + lax.broadcasted_iota(jnp.int32, (tokens, 1), 0))
        seg_k = seg_of(
            lengths_s, meta_s[0] - HALO + lax.broadcasted_iota(jnp.int32, (1, tokens + 2 * HALO), 1)
        )
        for i in range(blocks):
            same = seg_q[i * 128 : (i + 1) * 128, :] == seg_k[:, i * 128 : i * 128 + span]
            bias[i] = jnp.where(same, 0.0, -1e30)
            bias_t[i] = bias[i].T

    for ext, own, far in ((kx, ko, kr), (vx, vo, vr)):
        ext[0:HALO, :] = far[tokens : tokens + HALO, :]
        ext[HALO : HALO + tokens, :] = own[1]
        ext[HALO + tokens :, :] = far[tokens + HALO :, :]

    lane = lax.broadcasted_iota(jnp.int32, (1, PAIR), 1)
    stats = jnp.zeros((tokens, 128), F32)
    step = 256
    for h, half in enumerate(halves()):
        logs = []
        for i in range(tokens // step):
            rows = pl.ds(i * step, step)
            qh = jnp.where(half, q[0, rows, :], 0)
            s1 = mm(qh, ko[0], NT)
            s2 = mm(qh, kr[:tokens, :], NT)
            top = jnp.maximum(jnp.max(s1, -1, keepdims=True), jnp.max(s2, -1, keepdims=True))
            e1 = jnp.exp(s1 - top)
            e2 = jnp.exp(s2 - top)
            total = jnp.sum(e1, -1, keepdims=True) + jnp.sum(e2, -1, keepdims=True)
            r = mm(e1.astype(BF16), vo[0]) + mm(e2.astype(BF16), vr[:tokens, :])
            r = (r / total).astype(BF16)
            o[0, rows, :] = r if h == 0 else jnp.where(half, r, o[0, rows, :])
            logs.append(top + jnp.log(total))
        stats = jnp.where(lane == h, jnp.concatenate(logs, 0), stats)
        logs = []
        for i in range(blocks):
            rows = pl.ds(i * 128, 128)
            keys = pl.ds(i * 128, span)
            qh = jnp.where(half, q[1, rows, :], 0)
            s1 = mm(qh, kx[keys, :], NT) + bias[i]
            top = jnp.max(s1, -1, keepdims=True)
            e1 = jnp.exp(s1 - top)
            total = jnp.sum(e1, -1, keepdims=True)
            r = (mm(e1.astype(BF16), vx[keys, :]) / total).astype(BF16)
            o[1, rows, :] = r if h == 0 else jnp.where(half, r, o[1, rows, :])
            logs.append(top + jnp.log(total))
        stats = jnp.where(lane == 2 + h, jnp.concatenate(logs, 0), stats)
    lse[0] = stats.T[0:8, :]


def head_specs(tokens):
    own = pl.BlockSpec((2, tokens, PAIR), lambda i, *_: (0, 0, i))
    far = pl.BlockSpec((tokens + 2 * HALO, PAIR), lambda i, *_: (0, i))
    row = pl.BlockSpec((1, 8, tokens), lambda i, *_: (i, 0, 0))
    return own, far, row


def attend(lengths, meta, q, ko, vo, kr, vr):
    tokens, width = q.shape[1], q.shape[2]
    pairs = width // PAIR
    own, far, row = head_specs(tokens)
    ext = pltpu.VMEM((tokens + 2 * HALO, PAIR), BF16)
    return pl.pallas_call(
        attend_kernel,
        grid_spec=pltpu.PrefetchScalarGridSpec(
            num_scalar_prefetch=2,
            grid=(pairs,),
            in_specs=[own, own, own, far, far],
            out_specs=[
                own, row, pl.BlockSpec((tokens // 128, 128 + 2 * HALO, 128), lambda i, *_: (0, 0, 0)),
            ],
            scratch_shapes=[pltpu.VMEM((tokens // 128, 128, 128 + 2 * HALO), F32), ext, ext],
        ),
        out_shape=[
            jax.ShapeDtypeStruct(q.shape, BF16),
            jax.ShapeDtypeStruct((pairs, 8, tokens), F32),
            jax.ShapeDtypeStruct((tokens // 128, 128 + 2 * HALO, 128), F32),
        ],
        compiler_params=params(),
        cost_estimate=cost(4 * tokens * 2.5 * tokens * 256 * 2 * pairs, 8e6),
        name="attend",
    )(lengths, meta, q, ko, vo, kr, vr)


def attend_back_kernel(
    q, ko, vo, kr, vr, go, lse, bias, grad, sums, kx, vx, kt, dkx, dvx, dqt
):
    tokens = q.shape[1]
    far_at = 2 * tokens
    third = grad.shape[1] // 3
    at = [
        pl.ds(pl.multiple_of(n * third + pl.program_id(0) * PAIR, PAIR), PAIR) for n in range(3)
    ]
    grad[far_at:, at[0]] = jnp.zeros((grad.shape[0] - far_at, PAIR), BF16)
    blocks = tokens // 128
    span = 128 + 2 * HALO

    for ext, own, far in ((kx, ko, kr), (vx, vo, vr)):
        ext[0:HALO, :] = far[tokens : tokens + HALO, :]
        ext[HALO : HALO + tokens, :] = own[1]
        ext[HALO + tokens :, :] = far[tokens + HALO :, :]

    shift = HEAD ** (-0.5)
    sum_q = jnp.zeros((1, PAIR), F32)
    sum_v = jnp.zeros((1, PAIR), F32)

    k_parts = (ko[0], kr[:tokens, :])
    v_parts = (vo[0], vr[:tokens, :])
    for n in range(2):
        kt[n, :, :tokens] = k_parts[n].T
    dk_sums = [jnp.zeros((tokens, PAIR), F32)] * 2
    dv_sums = [jnp.zeros((tokens, PAIR), F32)] * 2
    for h, half in enumerate(halves()):
        rows = pl.ds(h * HEAD, HEAD)
        qh = jnp.where(half, q[0], 0)
        gh = jnp.where(half, go[0], 0)
        log = lse[0, h : h + 1, :]
        pts = [jnp.exp(mm(k_parts[n], qh, NT) - log) for n in range(2)]
        dpts = [mm(v_parts[n], gh, NT) for n in range(2)]
        delta = jnp.sum(pts[0] * dpts[0], 0, keepdims=True)
        delta += jnp.sum(pts[1] * dpts[1], 0, keepdims=True)
        part = None
        for n in range(2):
            dst = (pts[n] * (dpts[n] - delta)).astype(BF16)
            dv_sums[n] = dv_sums[n] + mm(pts[n].astype(BF16), gh)
            dk_sums[n] = dk_sums[n] + mm(dst, qh)
            turned = mm(kt[n, rows, :tokens], dst)
            part = turned if n == 0 else part + turned
        dqt[rows, :] = part
    for n, row in enumerate((0, far_at)):
        grad[row : row + tokens, at[1]] = dk_sums[n].astype(BF16)
        grad[row : row + tokens, at[2]] = dv_sums[n].astype(BF16)
    for n in range(2):
        sum_v += jnp.sum(dv_sums[n], 0, keepdims=True)
    out = dqt[...].T * shift
    grad[:tokens, at[0]] = out.astype(BF16)
    sum_q += jnp.sum(out, 0, keepdims=True)

    kt[0] = kx[...].T
    dkx[...] = jnp.zeros_like(dkx)
    dvx[...] = jnp.zeros_like(dvx)
    for i in range(blocks):
        cols = slice(i * 128, (i + 1) * 128)
        keys = slice(i * 128, i * 128 + span)
        dk_sum = jnp.zeros((span, PAIR), F32)
        dv_sum = jnp.zeros((span, PAIR), F32)
        for h, half in enumerate(halves()):
            rows = slice(h * HEAD, (h + 1) * HEAD)
            qh = jnp.where(half, q[1, cols, :], 0)
            gh = jnp.where(half, go[1, cols, :], 0)
            st = mm(kx[keys, :], qh, NT) + bias[i]
            pt = jnp.exp(st - lse[0, 2 + h : 3 + h, cols])
            dpt = mm(vx[keys, :], gh, NT)
            delta = jnp.sum(pt * dpt, 0, keepdims=True)
            dst = (pt * (dpt - delta)).astype(BF16)
            dv_sum += mm(pt.astype(BF16), gh)
            dk_sum += mm(dst, qh)
            dqt[rows, cols] = mm(kt[0, rows, keys], dst)
        dkx[keys, :] += dk_sum
        dvx[keys, :] += dv_sum
    out = dqt[...].T * shift
    grad[tokens:far_at, at[0]] = out.astype(BF16)
    sum_q += jnp.sum(out, 0, keepdims=True)
    sum_v += jnp.sum(dvx[...], 0, keepdims=True)
    edge = far_at + tokens
    for ext, cols in ((dkx, at[1]), (dvx, at[2])):
        grad[tokens:far_at, cols] = ext[HALO : HALO + tokens, :].astype(BF16)
        grad[edge : edge + HALO, cols] = ext[0:HALO, :].astype(BF16)
        grad[edge + HALO :, cols] = ext[HALO + tokens :, :].astype(BF16)
    sums[...] = jnp.concatenate([sum_q, sum_v, jnp.zeros((6, PAIR), F32)], 0)


def attend_back(first, count, q, ko, vo, kr, vr, go, lse, bias):
    tokens, width = q.shape[1], q.shape[2]
    wide = tokens + 2 * HALO
    own = pl.BlockSpec((2, tokens, PAIR), lambda i: (0, 0, i + first))
    far = pl.BlockSpec((wide, PAIR), lambda i: (0, i + first))
    row = pl.BlockSpec((1, 8, tokens), lambda i: (i + first, 0, 0))
    ext = pltpu.VMEM((wide, PAIR), BF16)
    ext32 = pltpu.VMEM((wide, PAIR), F32)
    rows, cols = 2 * tokens + wide, 3 * count * PAIR
    return pl.pallas_call(
        attend_back_kernel,
        grid=(count,),
        in_specs=[own, own, own, far, far, own, row]
        + [pl.BlockSpec(bias.shape, lambda i: (0, 0, 0))],
        out_specs=[
            pl.BlockSpec((rows, cols), lambda i: (0, 0)),
            pl.BlockSpec((8, PAIR), lambda i: (0, i)),
        ],
        scratch_shapes=[
            ext,
            ext,
            pltpu.VMEM((2, PAIR, wide), BF16),
            ext32,
            ext32,
            pltpu.VMEM((PAIR, tokens), F32),
        ],
        out_shape=[
            jax.ShapeDtypeStruct((rows, cols), BF16),
            jax.ShapeDtypeStruct((8, count * PAIR), F32),
        ],
        compiler_params=params(),
        cost_estimate=cost(10 * tokens * 2.5 * tokens * 256 * 2 * count, 2e6 * count),
        name="attend_back",
    )(q, ko, vo, kr, vr, go, lse, bias)


def chunk_spot(c, part, meta_s):
    return 2 * jnp.where(part == 0, meta_s[2], 1 - meta_s[2]) + c


def ffn_chunk(spot, first, n2, seed, ub, wu, wd, act, dh, sums_ub):
    chunk = wu.shape[1]
    k0 = 0.7978845608028654
    piece = 256

    @pl.when(first)
    def _():
        sums_ub[...] = jnp.zeros_like(sums_ub)

    for j in range(chunk // piece):
        cols = slice(j * piece, (j + 1) * piece)
        hid = mm(n2, wu[:, cols]) + ub[0:1, cols]
        square = hid * hid
        t = jnp.tanh(hid * (k0 + k0 * 0.044715 * square))
        half = 0.5 + 0.5 * t
        act[:, cols] = (hid * half).astype(BF16)
        slope = half + (hid * (0.5 - 0.5 * (t * t))) * (k0 + 3 * k0 * 0.044715 * square)
        dh32 = mm(seed, wd[cols, :], NT) * slope
        dh[:, cols] = dh32.astype(BF16)
        at = pl.ds(pl.multiple_of(spot * chunk + j * piece, piece), piece)
        sums_ub[0:1, at] += jnp.sum(dh32, 0, keepdims=True)


def ffn_a_kernel(
    meta_s, att, st, ul, us, vecs, ub, wp, wu, wd,
    g_o, n2_o, seed_o, mid_o, out_o, dn2_o, as_o, ak_o, sums_ub,
    n2, seed, n2t, seedt, outacc, dn2acc, act, dh,
):
    c, b = pl.program_id(0), pl.program_id(1)
    half = wp.shape[0] // 2
    tokens = mid_o.shape[1]
    rows = pl.ds(pl.multiple_of(b * tokens, tokens), tokens)

    @pl.when(c == 0)
    def _():
        up = jnp.where(b == 0, ul[0], us[0])
        seed[rows, :] = up
        seed_o[0] = up
        seedt[:, rows] = up.T
        whole = att[0]
        as_o[...] = jnp.where(meta_s[2] == 1, whole[:, half:], whole[:, :half])
        ak_o[...] = jnp.where(meta_s[2] == 1, whole[:, :half], whole[:, half:])
        middle = st[0] + mm(whole, wp[...]) + vecs[4:5, :]
        mid_o[0] = middle
        unit, _ = norm_parts(middle)
        normed = (unit * vecs[5:6, :] + vecs[6:7, :]).astype(BF16)
        n2[rows, :] = normed
        n2_o[0] = normed
        n2t[:, rows] = normed.T

    spot = chunk_spot(c, 0, meta_s)
    act_b, dh_b = act.at[rows, :], dh.at[rows, :]
    ffn_chunk(spot, (b == 0) & (c == 0), n2[rows, :], seed[rows, :], ub, wu, wd, act_b, dh_b, sums_ub)
    out = mm(act_b[...], wd[...])
    dn2 = mm(dh_b[...], wu[...], NT)

    @pl.when(c == 0)
    def _():
        outacc[rows, :] = mid_o[0] + vecs[7:8, :] + out
        dn2acc[rows, :] = dn2

    @pl.when(c == 1)
    def _():
        out_o[0] = outacc[rows, :] + out
        dn2_o[0] = dn2acc[rows, :] + dn2

    @pl.when(b == 1)
    def _():
        g_o[0, 0] = mm(seedt[...], act[...]).astype(BF16)
        g_o[0, 1] = mm(n2t[...], dh[...]).astype(BF16)


def ffn_b_kernel(
    meta_s, n2, seed, mid, out_i, dn2_i, vecs, ub, wp, wu, wd,
    out_l, out_s, g_o, dbr_o, datt_o, sums, sums_ub,
    n2t, seedt, outacc, dn2acc, act, dh,
):
    c, b = pl.program_id(0), pl.program_id(1)
    tokens = mid.shape[1]
    rows = pl.ds(pl.multiple_of(b * tokens, tokens), tokens)

    @pl.when(c == 0)
    def _():
        seedt[:, rows] = seed[b].T
        n2t[:, rows] = n2[b].T

    spot = chunk_spot(c, 1, meta_s)
    act_b, dh_b = act.at[rows, :], dh.at[rows, :]
    ffn_chunk(spot, (b == 0) & (c == 0), n2[b], seed[b], ub, wu, wd, act_b, dh_b, sums_ub)
    out = mm(act_b[...], wd[...])
    dn2 = mm(dh_b[...], wu[...], NT)

    @pl.when(c == 0)
    def _():
        outacc[rows, :] = out_i[0] + out
        dn2acc[rows, :] = dn2_i[0] + dn2

    @pl.when(c == 1)
    def _():
        result = (outacc[rows, :] + out).astype(BF16)

        @pl.when(b == 0)
        def _():
            out_l[0] = result
            sums[...] = jnp.zeros_like(sums)

        @pl.when(b > 0)
        def _():
            out_s[0] = result

        unit, scale = norm_parts(mid[0])
        whole = dn2acc[rows, :] + dn2
        seed32 = seed[b].astype(F32)
        du = whole * vecs[5:6, :]
        back = du - jnp.mean(du, -1, keepdims=True) - unit * jnp.mean(du * unit, -1, keepdims=True)
        dmid = back * scale + seed32
        dbr = dmid.astype(BF16)
        dbr_o[0] = dbr
        datt_o[0] = mm(dbr, wp[...], NT).astype(BF16)
        sums[0:1, :] += jnp.sum(dmid, 0, keepdims=True)
        sums[1:2, :] += jnp.sum(whole * unit, 0, keepdims=True)
        sums[2:3, :] += jnp.sum(whole, 0, keepdims=True)
        sums[3:4, :] += jnp.sum(seed32, 0, keepdims=True)

    @pl.when(b == 1)
    def _():
        g_o[0, 0] = mm(seedt[...], act[...]).astype(BF16)
        g_o[0, 1] = mm(n2t[...], dh[...]).astype(BF16)


def ffn_specs(tokens, width, part):
    whole = lambda *shape: pl.BlockSpec(shape, lambda c, b, m: (0,) * len(shape))
    early = pl.BlockSpec((1, tokens, width), lambda c, b, m: (jnp.where(c == 0, b, 1), 0, 0))
    late = pl.BlockSpec((1, tokens, width), lambda c, b, m: (jnp.where(c == 0, 0, b), 0, 0))
    grads = pl.BlockSpec((1, 2, width, width), lambda c, b, m: (c, 0, 0, 0))
    weights = [
        pl.BlockSpec((1, width), lambda c, b, m: (0, chunk_spot(c, part, m))),
        whole(width, width),
        pl.BlockSpec((width, width), lambda c, b, m: (0, chunk_spot(c, part, m))),
        pl.BlockSpec((width, width), lambda c, b, m: (chunk_spot(c, part, m), 0)),
    ]
    shape = lambda kind: jax.ShapeDtypeStruct((2, tokens, width), kind)
    low, high = pltpu.VMEM((2 * tokens, width), BF16), pltpu.VMEM((2 * tokens, width), F32)
    turned = pltpu.VMEM((width, 2 * tokens), BF16)
    return whole, early, late, grads, weights, shape, low, high, turned


def ffn_a(meta, att, st, ul, us, vecs, ub, wp, wu, wd):
    tokens, width = ul.shape[1], ul.shape[2]
    hidden = wu.shape[1]
    whole, early, late, grads, weights, shape, low, high, turned = ffn_specs(tokens, width, 0)
    single = whole(1, tokens, width)
    half = pl.BlockSpec((tokens, width // 2), lambda c, b, m: (jnp.where(c == 0, b, 1), 0))
    return pl.pallas_call(
        ffn_a_kernel,
        grid_spec=pltpu.PrefetchScalarGridSpec(
            num_scalar_prefetch=1,
            grid=(2, 2),
            in_specs=[early, early, single, single, whole(*vecs.shape)] + weights,
            out_specs=[grads, early, early, early, late, late, half, half, whole(1, hidden)],
            scratch_shapes=[low, low, turned, turned, high, high, low, low],
        ),
        out_shape=[jax.ShapeDtypeStruct((2, 2, width, width), BF16)]
        + [shape(BF16)] * 2
        + [shape(F32)] * 3
        + [jax.ShapeDtypeStruct((2 * tokens, width // 2), BF16)] * 2
        + [jax.ShapeDtypeStruct((1, hidden), F32)],
        compiler_params=params(2),
        cost_estimate=cost(4 * tokens * width * (width + 3 * hidden), 40e6),
        name="ffn_a",
    )(meta, att, st, ul, us, vecs, ub, wp, wu, wd)


def ffn_b(meta, n2, seed, mid, outacc, dn2acc, vecs, ub, wp, wu, wd):
    tokens, width = mid.shape[1], mid.shape[2]
    hidden = wu.shape[1]
    whole, early, late, grads, weights, shape, low, high, turned = ffn_specs(tokens, width, 1)
    single = jax.ShapeDtypeStruct((1, tokens, width), BF16)
    both = whole(2, tokens, width)
    return pl.pallas_call(
        ffn_b_kernel,
        grid_spec=pltpu.PrefetchScalarGridSpec(
            num_scalar_prefetch=1,
            grid=(2, 2),
            in_specs=[both, both, late, early, early, whole(*vecs.shape)] + weights,
            out_specs=[whole(1, tokens, width)] * 2
            + [grads, late, late, whole(8, width), whole(1, hidden)],
            scratch_shapes=[turned, turned, high, high, low, low],
        ),
        out_shape=[single, single, jax.ShapeDtypeStruct((2, 2, width, width), BF16)]
        + [shape(BF16)] * 2
        + [jax.ShapeDtypeStruct((8, width), F32), jax.ShapeDtypeStruct((1, hidden), F32)],
        compiler_params=params(2),
        cost_estimate=cost(4 * tokens * width * (width + 3 * hidden), 40e6),
        name="ffn_b",
    )(meta, n2, seed, mid, outacc, dn2acc, vecs, ub, wp, wu, wd)


def back_through(grads, w):
    width = w.shape[0]
    total, first = None, 0
    for grad in grads:
        cols = grad.shape[1] // 3
        for n in range(3):
            piece = grad[:, n * cols : (n + 1) * cols]
            part = mm(piece, w[:, n * width + first : n * width + first + cols], NT)
            total = part if total is None else total + part
        first += cols
    return total


def far_grad_kernel(meta_s, d1, d2, w, d_o, b1, b2, sem):
    total = b1.shape[0]
    tokens = total - 2 * HALO
    copies = []
    for n, (source, target) in enumerate(((d1, b1), (d2, b2))):
        copy = pltpu.make_async_copy(source.at[pl.ds(2 * tokens, total), :], target, sem.at[n])
        copy.start()
        copies.append(copy)
    for copy in copies:
        copy.wait()
    full = back_through((b1, b2), w)
    d_o[0:tokens, :] = full[0:tokens, :].astype(BF16)
    before = full[tokens : tokens + HALO, :]
    after = full[tokens + HALO :, :]
    d_o[tokens:, :] = jnp.where(meta_s[1] == 1, before, after).astype(BF16)


def far_grad(meta, d1, d2, w, total):
    width = w.shape[0]
    whole = lambda *shape: pl.BlockSpec(shape, lambda i, *_: (0,) * len(shape))
    return pl.pallas_call(
        far_grad_kernel,
        grid_spec=pltpu.PrefetchScalarGridSpec(
            num_scalar_prefetch=1,
            grid=(1,),
            in_specs=[
                pl.BlockSpec(memory_space=pl.ANY),
                pl.BlockSpec(memory_space=pl.ANY),
                whole(*w.shape),
            ],
            out_specs=whole(total - HALO, width),
            scratch_shapes=[
                pltpu.VMEM((total, d1.shape[1]), BF16),
                pltpu.VMEM((total, d2.shape[1]), BF16),
                pltpu.SemaphoreType.DMA((2,)),
            ],
        ),
        out_shape=jax.ShapeDtypeStruct((total - HALO, width), BF16),
        compiler_params=params(),
        cost_estimate=cost(4 * total * width * width, 5e6),
        name="far_grad",
    )(meta, d1, d2, w)


def near_grad_kernel(meta_s, d1, d2, w, got, st, dbr, vecs, in_l, in_s, sums, acc):
    b = pl.program_id(0)
    tokens = st.shape[1]
    acc[...] = back_through((d1, d2), w)

    @pl.when(b == 0)
    def _():
        acc[...] += got[0:tokens, :].astype(F32)
        sums[...] = jnp.zeros_like(sums)

    @pl.when(b > 0)
    def _():
        edge = got[tokens:, :].astype(F32)
        acc[0:HALO, :] += jnp.where(meta_s[1] == 1, edge, 0.0)
        acc[tokens - HALO :, :] += jnp.where(meta_s[1] == 0, edge, 0.0)

    dn = acc[...]
    unit, scale = norm_parts(st[0])
    du = dn * vecs[0:1, :]
    back = du - jnp.mean(du, -1, keepdims=True) - unit * jnp.mean(du * unit, -1, keepdims=True)
    result = (back * scale + dbr[0].astype(F32)).astype(BF16)

    @pl.when(b == 0)
    def _():
        in_l[0] = result

    @pl.when(b > 0)
    def _():
        in_s[0] = result

    sums[0:1, :] += jnp.sum(dn * unit, 0, keepdims=True)
    sums[1:2, :] += jnp.sum(dn, 0, keepdims=True)


def near_grad(meta, d1, d2, w, got, st, dbr, vecs):
    tokens, width = st.shape[1], st.shape[2]
    whole = lambda *shape: pl.BlockSpec(shape, lambda b, *_: (0,) * len(shape))
    part = pl.BlockSpec((1, tokens, width), lambda b, *_: (b, 0, 0))
    rows = lambda d: pl.BlockSpec((tokens, d.shape[1]), lambda b, *_: (b, 0))
    single = jax.ShapeDtypeStruct((1, tokens, width), BF16)
    return pl.pallas_call(
        near_grad_kernel,
        grid_spec=pltpu.PrefetchScalarGridSpec(
            num_scalar_prefetch=1,
            grid=(2,),
            in_specs=[
                rows(d1), rows(d2), whole(*w.shape), whole(*got.shape), part, part, whole(*vecs.shape),
            ],
            out_specs=[whole(1, tokens, width), whole(1, tokens, width), whole(8, width)],
            scratch_shapes=[pltpu.VMEM((tokens, width), F32)],
        ),
        out_shape=[single, single, jax.ShapeDtypeStruct((8, width), F32)],
        compiler_params=params(),
        cost_estimate=cost(4 * tokens * width * 3 * width, 15e6),
        name="near_grad",
    )(meta, d1, d2, w, got, st, dbr, vecs)


def outer(left, right):
    rows = lambda x: x.reshape(-1, x.shape[-1])
    full = jnp.einsum("ni,nj->ij", rows(left), rows(right), preferred_element_type=F32)
    return full.astype(BF16)


def plus(x, y):
    return (x.astype(F32) + y.astype(F32)).astype(BF16)


PLACE = 256


def mlp_place_kernel(meta_s, turned, value, *rest):
    down, up = rest[-2:]
    down[...] = turned[0, 0].T.astype(F32)
    up[...] = value[0, 0].astype(F32)


def mlp_place(meta, theirs, grads, earlier=()):
    width = grads.shape[2]
    per = width // PLACE
    spot = lambda h, m: 2 * (m[2] if theirs else 1 - m[2]) + h
    return pl.pallas_call(
        mlp_place_kernel,
        grid_spec=pltpu.PrefetchScalarGridSpec(
            num_scalar_prefetch=1,
            grid=(2, per),
            in_specs=[
                pl.BlockSpec((1, 1, width, PLACE), lambda h, r, m: (h, 0, 0, r)),
                pl.BlockSpec((1, 1, PLACE, width), lambda h, r, m: (h, 1, r, 0)),
            ]
            + [pl.BlockSpec(memory_space=pl.ANY)] * len(earlier),
            out_specs=[
                pl.BlockSpec((PLACE, width), lambda h, r, m: (spot(h, m) * per + r, 0)),
                pl.BlockSpec((PLACE, width), lambda h, r, m: (r, spot(h, m))),
            ],
        ),
        out_shape=[
            jax.ShapeDtypeStruct((4 * width, width), F32),
            jax.ShapeDtypeStruct((width, 4 * width), F32),
        ],
        input_output_aliases={3 + n: n for n in range(len(earlier))},
        compiler_params=params(2),
        cost_estimate=cost(1e6, 14e6),
        name="mlp_place",
    )(meta, grads, grads, *earlier)


def att_place_kernel(meta_s, left, right, last, *rest):
    qkv, proj = rest[-2:]
    half = left.shape[1]

    @pl.when(pl.program_id(0) < 3)
    def _():
        qkv[:, :half] = left[...].astype(F32)
        qkv[:, half:] = right[...].astype(F32)

    @pl.when(pl.program_id(0) == 3)
    def _():
        proj[...] = last[...].astype(F32)


def att_place(meta, theirs, grads, earlier=()):
    half, width = grads.shape[0], 2 * grads.shape[0]
    spot = lambda m: m[2] if theirs else 1 - m[2]
    return pl.pallas_call(
        att_place_kernel,
        grid_spec=pltpu.PrefetchScalarGridSpec(
            num_scalar_prefetch=1,
            grid=(4,),
            in_specs=[
                pl.BlockSpec((half, half), lambda j, m: (0, jnp.minimum(j, 2))),
                pl.BlockSpec((half, half), lambda j, m: (0, 3 + jnp.minimum(j, 2))),
                pl.BlockSpec((half, width), lambda j, m: (0, 3)),
            ]
            + [pl.BlockSpec(memory_space=pl.ANY)] * len(earlier),
            out_specs=[
                pl.BlockSpec((half, width), lambda j, m: (spot(m), jnp.minimum(j, 2))),
                pl.BlockSpec((half, width), lambda j, m: (spot(m), 0)),
            ],
        ),
        out_shape=[
            jax.ShapeDtypeStruct((width, 3 * width), F32),
            jax.ShapeDtypeStruct((width, width), F32),
        ],
        input_output_aliases={4 + n: n for n in range(len(earlier))},
        compiler_params=params(),
        cost_estimate=cost(1e6, 14e6),
        name="att_place",
    )(meta, grads, grads, grads, *earlier)


def swap_with(x, axis, bit=1):
    count = lax.axis_size(axis)
    return lax.ppermute(x, axis, [(i, i ^ bit) for i in range(count)])


ALL = ("chips", "core", "ulysses")


def chains():
    count = lax.axis_size("chips") * 4
    bits = [1] + [1 << n for n in range(2, count.bit_length() - 1)]
    swapped = list(bits)
    for n in range(0, len(bits) - 1, 2):
        swapped[n], swapped[n + 1] = bits[n + 1], bits[n]
    return count, bits, swapped


class Chain:
    def __init__(self, x, axis):
        self.x, self.axis, self.at = x, axis, 0
        self.count, *self.orders = chains()
        self.hops = len(self.orders[0])

    def swap(self, x, hop):
        pairs = [(i, i ^ self.orders[(i >> 1) & 1][hop]) for i in range(self.count)]
        return lax.ppermute(x, ALL, pairs)

    def bit(self, hop):
        place = lax.axis_index(ALL)
        step = jnp.where(lax.axis_index("core") == 0, self.orders[0][hop], self.orders[1][hop])
        return jnp.minimum(place & step, 1)

    def cut(self, x, which):
        half = x.shape[self.axis] // 2
        return lax.dynamic_slice_in_dim(x, which * half, half, self.axis)

    def add(self, hop):
        keep = self.cut(self.x, self.bit(hop))
        self.x = (keep.astype(F32) + self.got.astype(F32)).astype(BF16)

    def join(self, hop):
        first = self.bit(hop) == 0
        low = jnp.where(first, self.x, self.got)
        high = jnp.where(first, self.got, self.x)
        self.x = jnp.concatenate([low, high], self.axis)

    @property
    def plan(self):
        wide = min(2, self.hops)
        steps = [("halve", hop) for hop in range(wide)]
        steps += [("whole", hop) for hop in range(wide, self.hops)]
        return steps + [("gather", hop) for hop in range(wide - 1, -1, -1)]

    @property
    def done(self):
        return self.at > len(self.plan)

    def prepare(self):
        plan, at = self.plan, self.at
        self.at += 1
        if at:
            kind, hop = plan[at - 1]
            if kind == "halve":
                self.add(hop)
            elif kind == "whole":
                self.x = plus(self.x, self.got)
            else:
                self.join(hop)
        if at == len(plan):
            self.out = None
            return
        kind, self.hop = plan[at]
        self.out = self.cut(self.x, 1 - self.bit(self.hop)) if kind == "halve" else self.x

    def fire(self):
        self.got = self.swap(self.out, self.hop)


class Butterfly:
    def __init__(self, x):
        self.x, self.at = x, 0
        self.count = lax.axis_size("chips") * 4
        self.hops = self.count.bit_length() - 1

    @property
    def done(self):
        return self.at > self.hops

    def prepare(self):
        if self.at:
            self.x = self.x + self.got
        self.out = self.x if self.at < self.hops else None
        self.at += 1

    def fire(self):
        bit = 1 << (self.at - 1)
        self.got = lax.ppermute(self.out, ALL, [(i, i ^ bit) for i in range(self.count)])


def advance(values, *running):
    running = [chain for chain in running if not chain.done]
    for chain in running:
        chain.prepare()
    outs = [chain.x if chain.out is None else chain.out for chain in running]
    tied = tie(*outs, *values)
    for chain, out in zip(running, tied):
        if chain.out is None:
            chain.x = out
        else:
            if chain.out is chain.x:
                chain.x = out
            chain.out = out
            chain.fire()
    return tied[len(running) :]


def tie(*values):
    return lax.optimization_barrier(values)


def body(
    inputs_long,
    inputs_short,
    steps_long,
    steps_short,
    lengths,
    time_table,
    attngain,
    attnshift,
    qkvweight,
    querybias,
    valuebias,
    projweight,
    projbias,
    mlpgain,
    mlpshift,
    upweight,
    upbias,
    downweight,
    downbias,
    upstream_long,
    upstream_short,
):
    tokens, width = inputs_long.shape[1], inputs_long.shape[2]
    side = lax.axis_index("ulysses")
    core = lax.axis_index("core")
    meta = jnp.stack([side * tokens, side, 1 - core]).astype(jnp.int32)
    vecs, ub = pack(
        (attngain, attnshift, querybias, valuebias, projbias, mlpgain, mlpshift, downbias), upbias
    )

    edge = lax.dynamic_slice_in_dim(inputs_short[0], (1 - side) * (tokens - HALO), HALO, 0)
    across = jnp.concatenate([inputs_long[0], edge], axis=0)
    across = swap_with(across, "ulysses")

    q, ko, vo, start, rows, norm_s, norm_k = own_tokens(
        lengths, steps_short, steps_long, meta, inputs_long, inputs_short, time_table, vecs, qkvweight
    )
    kr, vr, norm_s, norm_k = far_tokens(lengths, meta, across, rows, vecs, qkvweight, norm_s, norm_k)
    att, lse, bias = attend(lengths, meta, q, ko, vo, kr, vr)
    core_swap = lambda x: swap_with(x, "core")
    send, n2, seed, mid, outacc, dn2acc, att_s, att_k, ub_a = ffn_a(
        meta, att, start, upstream_long, upstream_short, vecs, ub, projweight, upweight, downweight
    )
    send, n2 = tie(send, n2)
    got = core_swap(send)
    out_long, out_short, keep, dbr, datt, sums_mlp, ub_b = ffn_b(
        meta, n2, seed, mid, outacc, dn2acc, vecs, ub, projweight, upweight, downweight
    )
    mlp = Chain(plus(keep, got), 2)
    (datt,) = advance((datt,), mlp)

    pairs = width // PAIR
    operands = (q, ko, vo, kr, vr)
    d1, sums_1 = attend_back(0, pairs // 2, *operands, datt, lse, bias)
    datt, d1 = advance((datt, d1), mlp)
    d2, sums_2 = attend_back(pairs // 2, pairs // 2, *operands, datt, lse, bias)
    d1, d2 = advance((d1, d2), mlp)
    shares = lambda norm, att_half: jnp.concatenate(
        [outer(norm, d1), outer(norm, d2), outer(att_half, dbr)], 1
    )
    send = shares(norm_s, att_s)
    send, d1, d2 = tie(send, d1, d2)
    got = core_swap(send)
    rest = Chain(plus(shares(norm_k, att_k), got), 0)
    d1, d2 = advance((d1, d2), rest)
    back = far_grad(meta, d1, d2, qkvweight, kr.shape[0])
    back, d1, d2 = tie(back, d1, d2)
    back = swap_with(back, "ulysses")
    d1, d2 = advance((d1, d2), mlp)
    d1, d2 = advance((d1, d2), rest)
    in_long, in_short, sums_in = near_grad(meta, d1, d2, qkvweight, back, start, dbr, vecs)
    small = Butterfly(
        jnp.concatenate(
            [
                sums_in[0:2],
                jnp.concatenate([sums_1[0:2], sums_2[0:2]], 1),
                sums_mlp[0:4],
                (ub_a + ub_b).reshape(-1, width),
            ],
            0,
        )
    )
    advance((), mlp, small)
    advance((), rest)
    advance((), small)
    advance((), mlp)
    advance((), rest)
    held, waiting = (), None
    while not (rest.done and mlp.done and small.done):
        if not rest.done:
            moving = held if waiting is None else (*held, waiting)
            moving = advance(moving, rest)
            if waiting is None:
                held = moving
            else:
                held = mlp_place(meta, False, moving[-1])
                waiting = None
            if rest.done:
                rest_other = core_swap(rest.x)
        if not mlp.done:
            held = advance(held, mlp)
            if mlp.done:
                mlp_other = core_swap(mlp.x)
                waiting = mlp.x
        if not small.done:
            held = advance(held, small)
    if waiting is not None:
        held = mlp_place(meta, False, waiting)
    held = mlp_place(meta, True, mlp_other, held)
    rest_x, *held = tie(rest.x, *held)
    placed = att_place(meta, False, rest_x)
    g_down, g_up = held
    g_qkv, g_proj = att_place(meta, True, rest_other, placed)
    small = small.x
    return (
        out_long,
        out_short,
        in_long,
        in_short,
        small[0],
        small[1],
        g_qkv,
        small[2],
        small[3],
        g_proj,
        small[4],
        small[5],
        small[6],
        g_up,
        small[8:].reshape(-1),
        g_down,
        small[7],
    )


def solution(mesh):
    seq, pair = mesh.shape["seq"], mesh.shape["ulysses"]
    split = jax.sharding.Mesh(mesh.devices.reshape(seq // 2, 2, pair), ("chips", "core", "ulysses"))
    rows = ("chips", "core")
    tokens = P(rows, "ulysses", None)
    placed = (tokens, tokens, P(rows), P(rows, None), P(rows, None)) + (P(),) * 14 + (tokens,) * 2
    return jax.shard_map(
        body,
        mesh=split,
        in_specs=placed,
        out_specs=(tokens,) * 4 + (P(),) * 13,
        check_vma=False,
    )
```

```python
import functools

import jax
import jax.numpy as jnp
from jax import lax
from jax.experimental import pallas as pl
from jax.experimental.pallas import tpu as pltpu
from jax.sharding import PartitionSpec as P

HEAD = 64
PAIR = 2 * HEAD
HALO = 64
EPS = 1e-05
GROUP = 16
F32 = jnp.float32
BF16 = jnp.bfloat16
VMEM_LIMIT = 56 * 1024 * 1024

NT = (((1,), (1,)), ((), ()))
NN = (((1,), (0,)), ((), ()))


def mm(left, right, dims=NN):
    return lax.dot_general(left, right, dims, preferred_element_type=F32)


def params(steps=1):
    return pltpu.CompilerParams(
        vmem_limit_bytes=VMEM_LIMIT, dimension_semantics=("arbitrary",) * steps
    )


def cost(flops, moved, scale=1):
    return pl.CostEstimate(flops=int(flops * scale), bytes_accessed=int(moved * scale), transcendentals=0)


def norm_parts(values_in):
    centre = values_in - jnp.mean(values_in, -1, keepdims=True)
    spread = jnp.mean(centre * centre, -1, keepdims=True)
    scale = lax.rsqrt(spread + EPS)
    return centre * scale, scale


def bounds_rows(lengths_s, segs, width):
    lane = lax.broadcasted_iota(jnp.int32, (1, width), 1)
    low = jnp.zeros((1, width), jnp.int32)
    high = jnp.zeros((1, width), jnp.int32)
    at = jnp.int32(0)
    for k in range(segs):
        low = jnp.where(lane == k, at, low)
        at = at + lengths_s[0, k]
        high = jnp.where(lane == k, at, high)
    return lane, low, high


def pack_kernel(*refs):
    vecs, ub = refs[-2:]
    for n, ref in enumerate(refs[:-3]):
        vecs[n : n + 1, :] = ref[...].astype(F32).reshape(1, -1)
    ub[...] = refs[-3][...].astype(F32).reshape(1, -1)


def pack(vectors, wide):
    width = vectors[0].shape[0]
    return pl.pallas_call(
        pack_kernel,
        out_shape=[
            jax.ShapeDtypeStruct((len(vectors), width), F32),
            jax.ShapeDtypeStruct((1, wide.shape[0]), F32),
        ],
        cost_estimate=cost(1e6, 1e5),
        name="pack",
    )(*vectors, wide)


def own_kernel(
    lengths_s, steps_short_s, steps_long_s, meta_s,
    xl, xs, table, vecs, w,
    q_o, k_o, v_o, st_o, rows_o, ns_o, nk_o,
    buf, sem,
):
    b = pl.program_id(0)
    segs = lengths_s.shape[1]
    tokens, width = xl.shape[1], xl.shape[2]

    @pl.when(b == 0)
    def _():
        copies = []
        target = jnp.zeros((32, buf.shape[0]), jnp.int32) - 1
        sub = lax.broadcasted_iota(jnp.int32, (32, buf.shape[0]), 0)
        for k in range(segs + 1):
            step = steps_short_s[0, k] if k < segs else steps_long_s[0]
            base = pl.multiple_of((step // GROUP) * GROUP, GROUP)
            copy = pltpu.make_async_copy(
                table.at[pl.ds(base, GROUP), :], buf.at[pl.ds(k * GROUP, GROUP), :], sem.at[k]
            )
            copy.start()
            copies.append(copy)
            target = jnp.where(sub == k, k * GROUP + step - base, target)
        rest = buf.shape[0] - (segs + 1) * GROUP
        if rest:
            buf[pl.ds((segs + 1) * GROUP, rest), :] = jnp.zeros((rest, width), BF16)
        for copy in copies:
            copy.wait()
        lane = lax.broadcasted_iota(jnp.int32, (32, buf.shape[0]), 1)
        pick = jnp.where(lane == target, 1.0, 0.0).astype(BF16)
        rows_o[...] = mm(pick, buf[...]).astype(BF16)

    lane, low, high = bounds_rows(lengths_s, segs, 32)
    whole = lane == segs
    low = jnp.where(b == 0, 0, low)
    high = jnp.where(b == 0, jnp.where(whole, 1 << 30, 0), high)
    place = meta_s[0] + lax.broadcasted_iota(jnp.int32, (tokens, 1), 0)
    pick = jnp.where((place >= low) & (place < high), 1.0, 0.0).astype(BF16)
    embed = mm(pick, rows_o[...])
    start = jnp.where(b == 0, xl[0], xs[0]).astype(F32) + embed
    st_o[0] = start
    unit, _ = norm_parts(start)
    normed = (unit * vecs[0:1, :] + vecs[1:2, :]).astype(BF16)
    left, right = normed[:, : width // 2], normed[:, width // 2 :]
    ns_o[...] = jnp.where(meta_s[2] == 1, right, left)
    nk_o[...] = jnp.where(meta_s[2] == 1, left, right)
    q_o[0] = ((mm(normed, w[:, :width]) + vecs[2:3, :]) * HEAD ** (-0.5)).astype(BF16)
    k_o[0] = mm(normed, w[:, width : 2 * width]).astype(BF16)
    v_o[0] = (mm(normed, w[:, 2 * width :]) + vecs[3:4, :]).astype(BF16)


def own_tokens(lengths, steps_short, steps_long, meta, xl, xs, table, vecs, w):
    tokens, width = xl.shape[1], xl.shape[2]
    segs = lengths.shape[1]
    spots = -(-(segs + 1) * GROUP // 128) * 128
    whole = lambda *shape: pl.BlockSpec(shape, lambda b, *_: (0,) * len(shape))
    part = pl.BlockSpec((1, tokens, width), lambda b, *_: (b, 0, 0))
    half = pl.BlockSpec((tokens, width // 2), lambda b, *_: (b, 0))
    stacked = jax.ShapeDtypeStruct((2, tokens, width), BF16)
    return pl.pallas_call(
        own_kernel,
        grid_spec=pltpu.PrefetchScalarGridSpec(
            num_scalar_prefetch=4,
            grid=(2,),
            in_specs=[
                whole(1, tokens, width),
                whole(1, tokens, width),
                pl.BlockSpec(memory_space=pl.ANY),
                whole(*vecs.shape),
                whole(*w.shape),
            ],
            out_specs=[part] * 4 + [whole(32, width)] + [half, half],
            scratch_shapes=[pltpu.VMEM((spots, width), BF16), pltpu.SemaphoreType.DMA((segs + 1,))],
        ),
        out_shape=[stacked] * 3
        + [jax.ShapeDtypeStruct((2, tokens, width), F32), jax.ShapeDtypeStruct((32, width), BF16)]
        + [jax.ShapeDtypeStruct((3 * tokens + 2 * HALO, width // 2), BF16)] * 2,
        compiler_params=params(),
        cost_estimate=cost(4 * tokens * width * 3 * width, 14e6),
        name="own_tokens",
    )(lengths, steps_short, steps_long, meta, xl, xs, table, vecs, w)


def far_kernel(
    lengths_s, meta_s, xr, rows, vecs, wk, wv, ns_i, nk_i, k_o, v_o, ns_o, nk_o, ns, nk, sem
):
    segs = lengths_s.shape[1]
    total, width = k_o.shape
    tokens = total - 2 * HALO
    side = meta_s[1]
    got = xr[...].astype(F32)
    edge = got[tokens:, :]
    before = jnp.where(side == 1, edge, 0.0)
    after = jnp.where(side == 0, edge, 0.0)
    x = jnp.concatenate([got[:tokens, :], before, after], axis=0)
    lane, low, high = bounds_rows(lengths_s, segs, 32)
    row = lax.broadcasted_iota(jnp.int32, (total, 1), 0)
    place = meta_s[0] + row - HALO - jnp.where(row < tokens + HALO, tokens, 0)
    inside = (place >= low) & (place < high)
    story = jnp.where(lane == segs, 1.0, 0.0)
    pick = jnp.where(row < tokens, story, jnp.where(inside, 1.0, 0.0)).astype(BF16)
    start = x + mm(pick, rows[...])
    unit, _ = norm_parts(start)
    normed = (unit * vecs[0:1, :] + vecs[1:2, :]).astype(BF16)
    left, right = normed[:, : width // 2], normed[:, width // 2 :]
    ns[...] = jnp.where(meta_s[2] == 1, right, left)
    nk[...] = jnp.where(meta_s[2] == 1, left, right)
    rest = pl.ds(2 * tokens, total)
    copy_s = pltpu.make_async_copy(ns, ns_o.at[rest, :], sem.at[0])
    copy_k = pltpu.make_async_copy(nk, nk_o.at[rest, :], sem.at[1])
    copy_s.start()
    copy_k.start()
    k_o[...] = mm(normed, wk[...]).astype(BF16)
    v_o[...] = (mm(normed, wv[...]) + vecs[3:4, :]).astype(BF16)
    copy_s.wait()
    copy_k.wait()


def far_tokens(lengths, meta, xr, rows, vecs, w, ns, nk):
    width = xr.shape[1]
    total = xr.shape[0] + HALO
    whole = lambda *shape: pl.BlockSpec(shape, lambda i, *_: (0,) * len(shape))
    out = jax.ShapeDtypeStruct((total, width), BF16)
    return pl.pallas_call(
        far_kernel,
        grid_spec=pltpu.PrefetchScalarGridSpec(
            num_scalar_prefetch=2,
            grid=(1,),
            in_specs=[
                whole(*xr.shape),
                whole(*rows.shape),
                whole(*vecs.shape),
                pl.BlockSpec((width, width), lambda i, *_: (0, 1)),
                pl.BlockSpec((width, width), lambda i, *_: (0, 2)),
                pl.BlockSpec(memory_space=pl.ANY),
                pl.BlockSpec(memory_space=pl.ANY),
            ],
            out_specs=[whole(total, width)] * 2 + [pl.BlockSpec(memory_space=pl.ANY)] * 2,
            scratch_shapes=[pltpu.VMEM((total, width // 2), BF16)] * 2
            + [pltpu.SemaphoreType.DMA((2,))],
        ),
        out_shape=[out] * 2 + [jax.ShapeDtypeStruct(ns.shape, BF16)] * 2,
        input_output_aliases={7: 2, 8: 3},
        compiler_params=params(),
        cost_estimate=cost(2 * total * width * 2 * width, 6e6),
        name="far_tokens",
    )(lengths, meta, xr, rows, vecs, w, w, ns, nk)


def seg_of(lengths_s, place):
    segs = lengths_s.shape[1]
    at = jnp.int32(0)
    seg = jnp.zeros(place.shape, jnp.int32)
    for k in range(segs - 1):
        at = at + lengths_s[0, k]
        seg = seg + jnp.where(place >= at, 1, 0)
    at = at + lengths_s[0, segs - 1]
    return jnp.where(place < 0, -1, jnp.where(place >= at, -2, seg))


def halves():
    lane = lax.broadcasted_iota(jnp.int32, (1, PAIR), 1)
    return (lane < HEAD, lane >= HEAD)


def attend_kernel(lengths_s, meta_s, q, ko, vo, kr, vr, o, lse, bias_t, bias, kx, vx):
    tokens = q.shape[1]
    blocks = tokens // 128
    span = 128 + 2 * HALO

    @pl.when(pl.program_id(0) == 0)
    def _():
        seg_q = seg_of(lengths_s, meta_s[0] + lax.broadcasted_iota(jnp.int32, (tokens, 1), 0))
        seg_k = seg_of(
            lengths_s, meta_s[0] - HALO + lax.broadcasted_iota(jnp.int32, (1, tokens + 2 * HALO), 1)
        )
        for i in range(blocks):
            same = seg_q[i * 128 : (i + 1) * 128, :] == seg_k[:, i * 128 : i * 128 + span]
            bias[i] = jnp.where(same, 0.0, -1e30)
            bias_t[i] = bias[i].T

    for ext, own, far in ((kx, ko, kr), (vx, vo, vr)):
        ext[0:HALO, :] = far[tokens : tokens + HALO, :]
        ext[HALO : HALO + tokens, :] = own[1]
        ext[HALO + tokens :, :] = far[tokens + HALO :, :]

    lane = lax.broadcasted_iota(jnp.int32, (1, PAIR), 1)
    stats = jnp.zeros((tokens, 128), F32)
    step = 256
    for h, half in enumerate(halves()):
        logs = []
        for i in range(tokens // step):
            rows = pl.ds(i * step, step)
            qh = jnp.where(half, q[0, rows, :], 0)
            s1 = mm(qh, ko[0], NT)
            s2 = mm(qh, kr[:tokens, :], NT)
            top = jnp.maximum(jnp.max(s1, -1, keepdims=True), jnp.max(s2, -1, keepdims=True))
            e1 = jnp.exp(s1 - top)
            e2 = jnp.exp(s2 - top)
            total = jnp.sum(e1, -1, keepdims=True) + jnp.sum(e2, -1, keepdims=True)
            r = mm(e1.astype(BF16), vo[0]) + mm(e2.astype(BF16), vr[:tokens, :])
            r = (r / total).astype(BF16)
            o[0, rows, :] = r if h == 0 else jnp.where(half, r, o[0, rows, :])
            logs.append(top + jnp.log(total))
        stats = jnp.where(lane == h, jnp.concatenate(logs, 0), stats)
        logs = []
        for i in range(blocks):
            rows = pl.ds(i * 128, 128)
            keys = pl.ds(i * 128, span)
            qh = jnp.where(half, q[1, rows, :], 0)
            s1 = mm(qh, kx[keys, :], NT) + bias[i]
            top = jnp.max(s1, -1, keepdims=True)
            e1 = jnp.exp(s1 - top)
            total = jnp.sum(e1, -1, keepdims=True)
            r = (mm(e1.astype(BF16), vx[keys, :]) / total).astype(BF16)
            o[1, rows, :] = r if h == 0 else jnp.where(half, r, o[1, rows, :])
            logs.append(top + jnp.log(total))
        stats = jnp.where(lane == 2 + h, jnp.concatenate(logs, 0), stats)
    lse[0] = stats.T[0:8, :]


def head_specs(tokens):
    own = pl.BlockSpec((2, tokens, PAIR), lambda i, *_: (0, 0, i))
    far = pl.BlockSpec((tokens + 2 * HALO, PAIR), lambda i, *_: (0, i))
    row = pl.BlockSpec((1, 8, tokens), lambda i, *_: (i, 0, 0))
    return own, far, row


def attend(lengths, meta, q, ko, vo, kr, vr):
    tokens, width = q.shape[1], q.shape[2]
    pairs = width // PAIR
    own, far, row = head_specs(tokens)
    ext = pltpu.VMEM((tokens + 2 * HALO, PAIR), BF16)
    return pl.pallas_call(
        attend_kernel,
        grid_spec=pltpu.PrefetchScalarGridSpec(
            num_scalar_prefetch=2,
            grid=(pairs,),
            in_specs=[own, own, own, far, far],
            out_specs=[
                own, row, pl.BlockSpec((tokens // 128, 128 + 2 * HALO, 128), lambda i, *_: (0, 0, 0)),
            ],
            scratch_shapes=[pltpu.VMEM((tokens // 128, 128, 128 + 2 * HALO), F32), ext, ext],
        ),
        out_shape=[
            jax.ShapeDtypeStruct(q.shape, BF16),
            jax.ShapeDtypeStruct((pairs, 8, tokens), F32),
            jax.ShapeDtypeStruct((tokens // 128, 128 + 2 * HALO, 128), F32),
        ],
        compiler_params=params(),
        cost_estimate=cost(4 * tokens * 2.5 * tokens * 256 * 2 * pairs, 8e6),
        name="attend",
    )(lengths, meta, q, ko, vo, kr, vr)


def attend_back_kernel(
    q, ko, vo, kr, vr, go, lse, bias, grad, sums, kx, vx, kt, dkx, dvx, dqt
):
    tokens = q.shape[1]
    far_at = 2 * tokens
    third = grad.shape[1] // 3
    at = [
        pl.ds(pl.multiple_of(n * third + pl.program_id(0) * PAIR, PAIR), PAIR) for n in range(3)
    ]
    grad[far_at:, at[0]] = jnp.zeros((grad.shape[0] - far_at, PAIR), BF16)
    blocks = tokens // 128
    span = 128 + 2 * HALO

    for ext, own, far in ((kx, ko, kr), (vx, vo, vr)):
        ext[0:HALO, :] = far[tokens : tokens + HALO, :]
        ext[HALO : HALO + tokens, :] = own[1]
        ext[HALO + tokens :, :] = far[tokens + HALO :, :]

    shift = HEAD ** (-0.5)
    sum_q = jnp.zeros((1, PAIR), F32)
    sum_v = jnp.zeros((1, PAIR), F32)

    k_parts = (ko[0], kr[:tokens, :])
    v_parts = (vo[0], vr[:tokens, :])
    for n in range(2):
        kt[n, :, :tokens] = k_parts[n].T
    dk_sums = [jnp.zeros((tokens, PAIR), F32)] * 2
    dv_sums = [jnp.zeros((tokens, PAIR), F32)] * 2
    for h, half in enumerate(halves()):
        rows = pl.ds(h * HEAD, HEAD)
        qh = jnp.where(half, q[0], 0)
        gh = jnp.where(half, go[0], 0)
        log = lse[0, h : h + 1, :]
        pts = [jnp.exp(mm(k_parts[n], qh, NT) - log) for n in range(2)]
        dpts = [mm(v_parts[n], gh, NT) for n in range(2)]
        delta = jnp.sum(pts[0] * dpts[0], 0, keepdims=True)
        delta += jnp.sum(pts[1] * dpts[1], 0, keepdims=True)
        part = None
        for n in range(2):
            dst = (pts[n] * (dpts[n] - delta)).astype(BF16)
            dv_sums[n] = dv_sums[n] + mm(pts[n].astype(BF16), gh)
            dk_sums[n] = dk_sums[n] + mm(dst, qh)
            turned = mm(kt[n, rows, :tokens], dst)
            part = turned if n == 0 else part + turned
        dqt[rows, :] = part
    for n, row in enumerate((0, far_at)):
        grad[row : row + tokens, at[1]] = dk_sums[n].astype(BF16)
        grad[row : row + tokens, at[2]] = dv_sums[n].astype(BF16)
    for n in range(2):
        sum_v += jnp.sum(dv_sums[n], 0, keepdims=True)
    out = dqt[...].T * shift
    grad[:tokens, at[0]] = out.astype(BF16)
    sum_q += jnp.sum(out, 0, keepdims=True)

    kt[0] = kx[...].T
    dkx[...] = jnp.zeros_like(dkx)
    dvx[...] = jnp.zeros_like(dvx)
    for i in range(blocks):
        cols = slice(i * 128, (i + 1) * 128)
        keys = slice(i * 128, i * 128 + span)
        dk_sum = jnp.zeros((span, PAIR), F32)
        dv_sum = jnp.zeros((span, PAIR), F32)
        for h, half in enumerate(halves()):
            rows = slice(h * HEAD, (h + 1) * HEAD)
            qh = jnp.where(half, q[1, cols, :], 0)
            gh = jnp.where(half, go[1, cols, :], 0)
            st = mm(kx[keys, :], qh, NT) + bias[i]
            pt = jnp.exp(st - lse[0, 2 + h : 3 + h, cols])
            dpt = mm(vx[keys, :], gh, NT)
            delta = jnp.sum(pt * dpt, 0, keepdims=True)
            dst = (pt * (dpt - delta)).astype(BF16)
            dv_sum += mm(pt.astype(BF16), gh)
            dk_sum += mm(dst, qh)
            dqt[rows, cols] = mm(kt[0, rows, keys], dst)
        dkx[keys, :] += dk_sum
        dvx[keys, :] += dv_sum
    out = dqt[...].T * shift
    grad[tokens:far_at, at[0]] = out.astype(BF16)
    sum_q += jnp.sum(out, 0, keepdims=True)
    sum_v += jnp.sum(dvx[...], 0, keepdims=True)
    edge = far_at + tokens
    for ext, cols in ((dkx, at[1]), (dvx, at[2])):
        grad[tokens:far_at, cols] = ext[HALO : HALO + tokens, :].astype(BF16)
        grad[edge : edge + HALO, cols] = ext[0:HALO, :].astype(BF16)
        grad[edge + HALO :, cols] = ext[HALO + tokens :, :].astype(BF16)
    sums[...] = jnp.concatenate([sum_q, sum_v, jnp.zeros((6, PAIR), F32)], 0)


def attend_back(first, count, q, ko, vo, kr, vr, go, lse, bias):
    tokens, width = q.shape[1], q.shape[2]
    wide = tokens + 2 * HALO
    own = pl.BlockSpec((2, tokens, PAIR), lambda i: (0, 0, i + first))
    far = pl.BlockSpec((wide, PAIR), lambda i: (0, i + first))
    row = pl.BlockSpec((1, 8, tokens), lambda i: (i + first, 0, 0))
    ext = pltpu.VMEM((wide, PAIR), BF16)
    ext32 = pltpu.VMEM((wide, PAIR), F32)
    rows, cols = 2 * tokens + wide, 3 * count * PAIR
    return pl.pallas_call(
        attend_back_kernel,
        grid=(count,),
        in_specs=[own, own, own, far, far, own, row]
        + [pl.BlockSpec(bias.shape, lambda i: (0, 0, 0))],
        out_specs=[
            pl.BlockSpec((rows, cols), lambda i: (0, 0)),
            pl.BlockSpec((8, PAIR), lambda i: (0, i)),
        ],
        scratch_shapes=[
            ext,
            ext,
            pltpu.VMEM((2, PAIR, wide), BF16),
            ext32,
            ext32,
            pltpu.VMEM((PAIR, tokens), F32),
        ],
        out_shape=[
            jax.ShapeDtypeStruct((rows, cols), BF16),
            jax.ShapeDtypeStruct((8, count * PAIR), F32),
        ],
        compiler_params=params(),
        cost_estimate=cost(10 * tokens * 2.5 * tokens * 256 * 2 * count, 2e6 * count),
        name="attend_back",
    )(q, ko, vo, kr, vr, go, lse, bias)


def chunk_spot(c, part, meta_s):
    return 2 * jnp.where(part == 0, meta_s[2], 1 - meta_s[2]) + c


def ffn_chunk(spot, first, n2, seed, ub, wu, wd, act, dh, sums_ub):
    chunk = wu.shape[1]
    k0 = 0.7978845608028654
    piece = 256

    @pl.when(first)
    def _():
        sums_ub[...] = jnp.zeros_like(sums_ub)

    for j in range(chunk // piece):
        cols = slice(j * piece, (j + 1) * piece)
        hid = mm(n2, wu[:, cols]) + ub[0:1, cols]
        square = hid * hid
        t = jnp.tanh(hid * (k0 + k0 * 0.044715 * square))
        half = 0.5 + 0.5 * t
        act[:, cols] = (hid * half).astype(BF16)
        slope = half + (hid * (0.5 - 0.5 * (t * t))) * (k0 + 3 * k0 * 0.044715 * square)
        dh32 = mm(seed, wd[cols, :], NT) * slope
        dh[:, cols] = dh32.astype(BF16)
        at = pl.ds(pl.multiple_of(spot * chunk + j * piece, piece), piece)
        sums_ub[0:1, at] += jnp.sum(dh32, 0, keepdims=True)


def ffn_a_kernel(
    meta_s, att, st, ul, us, vecs, ub, wp, wu, wd,
    g_o, n2_o, seed_o, mid_o, out_o, dn2_o, as_o, ak_o, sums_ub,
    n2, seed, n2t, seedt, outacc, dn2acc, act, dh,
):
    c, b = pl.program_id(0), pl.program_id(1)
    half = wp.shape[0] // 2
    tokens = mid_o.shape[1]
    rows = pl.ds(pl.multiple_of(b * tokens, tokens), tokens)

    @pl.when(c == 0)
    def _():
        up = jnp.where(b == 0, ul[0], us[0])
        seed[rows, :] = up
        seed_o[0] = up
        seedt[:, rows] = up.T
        whole = att[0]
        as_o[...] = jnp.where(meta_s[2] == 1, whole[:, half:], whole[:, :half])
        ak_o[...] = jnp.where(meta_s[2] == 1, whole[:, :half], whole[:, half:])
        middle = st[0] + mm(whole, wp[...]) + vecs[4:5, :]
        mid_o[0] = middle
        unit, _ = norm_parts(middle)
        normed = (unit * vecs[5:6, :] + vecs[6:7, :]).astype(BF16)
        n2[rows, :] = normed
        n2_o[0] = normed
        n2t[:, rows] = normed.T

    spot = chunk_spot(c, 0, meta_s)
    act_b, dh_b = act.at[rows, :], dh.at[rows, :]
    ffn_chunk(spot, (b == 0) & (c == 0), n2[rows, :], seed[rows, :], ub, wu, wd, act_b, dh_b, sums_ub)
    out = mm(act_b[...], wd[...])
    dn2 = mm(dh_b[...], wu[...], NT)

    @pl.when(c == 0)
    def _():
        outacc[rows, :] = mid_o[0] + vecs[7:8, :] + out
        dn2acc[rows, :] = dn2

    @pl.when(c == 1)
    def _():
        out_o[0] = outacc[rows, :] + out
        dn2_o[0] = dn2acc[rows, :] + dn2

    @pl.when(b == 1)
    def _():
        g_o[0, 0] = mm(seedt[...], act[...]).astype(BF16)
        g_o[0, 1] = mm(n2t[...], dh[...]).astype(BF16)


def ffn_b_kernel(
    meta_s, n2, seed, mid, out_i, dn2_i, vecs, ub, wp, wu, wd,
    out_l, out_s, g_o, dbr_o, datt_o, sums, sums_ub,
    n2t, seedt, outacc, dn2acc, act, dh,
):
    c, b = pl.program_id(0), pl.program_id(1)
    tokens = mid.shape[1]
    rows = pl.ds(pl.multiple_of(b * tokens, tokens), tokens)

    @pl.when(c == 0)
    def _():
        seedt[:, rows] = seed[b].T
        n2t[:, rows] = n2[b].T

    spot = chunk_spot(c, 1, meta_s)
    act_b, dh_b = act.at[rows, :], dh.at[rows, :]
    ffn_chunk(spot, (b == 0) & (c == 0), n2[b], seed[b], ub, wu, wd, act_b, dh_b, sums_ub)
    out = mm(act_b[...], wd[...])
    dn2 = mm(dh_b[...], wu[...], NT)

    @pl.when(c == 0)
    def _():
        outacc[rows, :] = out_i[0] + out
        dn2acc[rows, :] = dn2_i[0] + dn2

    @pl.when(c == 1)
    def _():
        result = (outacc[rows, :] + out).astype(BF16)

        @pl.when(b == 0)
        def _():
            out_l[0] = result
            sums[...] = jnp.zeros_like(sums)

        @pl.when(b > 0)
        def _():
            out_s[0] = result

        unit, scale = norm_parts(mid[0])
        whole = dn2acc[rows, :] + dn2
        seed32 = seed[b].astype(F32)
        du = whole * vecs[5:6, :]
        back = du - jnp.mean(du, -1, keepdims=True) - unit * jnp.mean(du * unit, -1, keepdims=True)
        dmid = back * scale + seed32
        dbr = dmid.astype(BF16)
        dbr_o[0] = dbr
        datt_o[0] = mm(dbr, wp[...], NT).astype(BF16)
        sums[0:1, :] += jnp.sum(dmid, 0, keepdims=True)
        sums[1:2, :] += jnp.sum(whole * unit, 0, keepdims=True)
        sums[2:3, :] += jnp.sum(whole, 0, keepdims=True)
        sums[3:4, :] += jnp.sum(seed32, 0, keepdims=True)

    @pl.when(b == 1)
    def _():
        g_o[0, 0] = mm(seedt[...], act[...]).astype(BF16)
        g_o[0, 1] = mm(n2t[...], dh[...]).astype(BF16)


def ffn_specs(tokens, width, part):
    whole = lambda *shape: pl.BlockSpec(shape, lambda c, b, m: (0,) * len(shape))
    early = pl.BlockSpec((1, tokens, width), lambda c, b, m: (jnp.where(c == 0, b, 1), 0, 0))
    late = pl.BlockSpec((1, tokens, width), lambda c, b, m: (jnp.where(c == 0, 0, b), 0, 0))
    grads = pl.BlockSpec((1, 2, width, width), lambda c, b, m: (c, 0, 0, 0))
    weights = [
        pl.BlockSpec((1, width), lambda c, b, m: (0, chunk_spot(c, part, m))),
        whole(width, width),
        pl.BlockSpec((width, width), lambda c, b, m: (0, chunk_spot(c, part, m))),
        pl.BlockSpec((width, width), lambda c, b, m: (chunk_spot(c, part, m), 0)),
    ]
    shape = lambda kind: jax.ShapeDtypeStruct((2, tokens, width), kind)
    low, high = pltpu.VMEM((2 * tokens, width), BF16), pltpu.VMEM((2 * tokens, width), F32)
    turned = pltpu.VMEM((width, 2 * tokens), BF16)
    return whole, early, late, grads, weights, shape, low, high, turned


def ffn_a(meta, att, st, ul, us, vecs, ub, wp, wu, wd):
    tokens, width = ul.shape[1], ul.shape[2]
    hidden = wu.shape[1]
    whole, early, late, grads, weights, shape, low, high, turned = ffn_specs(tokens, width, 0)
    single = whole(1, tokens, width)
    half = pl.BlockSpec((tokens, width // 2), lambda c, b, m: (jnp.where(c == 0, b, 1), 0))
    return pl.pallas_call(
        ffn_a_kernel,
        grid_spec=pltpu.PrefetchScalarGridSpec(
            num_scalar_prefetch=1,
            grid=(2, 2),
            in_specs=[early, early, single, single, whole(*vecs.shape)] + weights,
            out_specs=[grads, early, early, early, late, late, half, half, whole(1, hidden)],
            scratch_shapes=[low, low, turned, turned, high, high, low, low],
        ),
        out_shape=[jax.ShapeDtypeStruct((2, 2, width, width), BF16)]
        + [shape(BF16)] * 2
        + [shape(F32)] * 3
        + [jax.ShapeDtypeStruct((2 * tokens, width // 2), BF16)] * 2
        + [jax.ShapeDtypeStruct((1, hidden), F32)],
        compiler_params=params(2),
        cost_estimate=cost(4 * tokens * width * (width + 3 * hidden), 40e6),
        name="ffn_a",
    )(meta, att, st, ul, us, vecs, ub, wp, wu, wd)


def ffn_b(meta, n2, seed, mid, outacc, dn2acc, vecs, ub, wp, wu, wd):
    tokens, width = mid.shape[1], mid.shape[2]
    hidden = wu.shape[1]
    whole, early, late, grads, weights, shape, low, high, turned = ffn_specs(tokens, width, 1)
    single = jax.ShapeDtypeStruct((1, tokens, width), BF16)
    both = whole(2, tokens, width)
    return pl.pallas_call(
        ffn_b_kernel,
        grid_spec=pltpu.PrefetchScalarGridSpec(
            num_scalar_prefetch=1,
            grid=(2, 2),
            in_specs=[both, both, late, early, early, whole(*vecs.shape)] + weights,
            out_specs=[whole(1, tokens, width)] * 2
            + [grads, late, late, whole(8, width), whole(1, hidden)],
            scratch_shapes=[turned, turned, high, high, low, low],
        ),
        out_shape=[single, single, jax.ShapeDtypeStruct((2, 2, width, width), BF16)]
        + [shape(BF16)] * 2
        + [jax.ShapeDtypeStruct((8, width), F32), jax.ShapeDtypeStruct((1, hidden), F32)],
        compiler_params=params(2),
        cost_estimate=cost(4 * tokens * width * (width + 3 * hidden), 40e6),
        name="ffn_b",
    )(meta, n2, seed, mid, outacc, dn2acc, vecs, ub, wp, wu, wd)


def back_through(grads, w):
    width = w.shape[0]
    total, first = None, 0
    for grad in grads:
        cols = grad.shape[1] // 3
        for n in range(3):
            piece = grad[:, n * cols : (n + 1) * cols]
            part = mm(piece, w[:, n * width + first : n * width + first + cols], NT)
            total = part if total is None else total + part
        first += cols
    return total


def far_grad_kernel(meta_s, *refs):
    count = (len(refs) - 3) // 2
    sources, w, d_o, held, sem = refs[:count], refs[count], refs[count + 1], refs[count + 2 : -1], refs[-1]
    total = held[0].shape[0]
    tokens = total - 2 * HALO
    copies = []
    for n, (source, target) in enumerate(zip(sources, held)):
        copy = pltpu.make_async_copy(source.at[pl.ds(2 * tokens, total), :], target, sem.at[n])
        copy.start()
        copies.append(copy)
    for copy in copies:
        copy.wait()
    full = back_through(held, w)
    d_o[0:tokens, :] = full[0:tokens, :].astype(BF16)
    before = full[tokens : tokens + HALO, :]
    after = full[tokens + HALO :, :]
    d_o[tokens:, :] = jnp.where(meta_s[1] == 1, before, after).astype(BF16)


def far_grad(meta, grads, w, total):
    width = w.shape[0]
    whole = lambda *shape: pl.BlockSpec(shape, lambda i, *_: (0,) * len(shape))
    return pl.pallas_call(
        far_grad_kernel,
        grid_spec=pltpu.PrefetchScalarGridSpec(
            num_scalar_prefetch=1,
            grid=(1,),
            in_specs=[pl.BlockSpec(memory_space=pl.ANY)] * len(grads) + [whole(*w.shape)],
            out_specs=whole(total - HALO, width),
            scratch_shapes=[pltpu.VMEM((total, d.shape[1]), BF16) for d in grads]
            + [pltpu.SemaphoreType.DMA((len(grads),))],
        ),
        out_shape=jax.ShapeDtypeStruct((total - HALO, width), BF16),
        compiler_params=params(),
        cost_estimate=cost(4 * total * width * width, 5e6),
        name="far_grad",
    )(meta, *grads, w)


def near_grad_kernel(meta_s, *refs):
    grads, (w, got, st, dbr, vecs, in_l, in_s, sums, acc) = refs[:-9], refs[-9:]
    b = pl.program_id(0)
    tokens = st.shape[1]
    acc[...] = back_through(grads, w)

    @pl.when(b == 0)
    def _():
        acc[...] += got[0:tokens, :].astype(F32)
        sums[...] = jnp.zeros_like(sums)

    @pl.when(b > 0)
    def _():
        edge = got[tokens:, :].astype(F32)
        acc[0:HALO, :] += jnp.where(meta_s[1] == 1, edge, 0.0)
        acc[tokens - HALO :, :] += jnp.where(meta_s[1] == 0, edge, 0.0)

    dn = acc[...]
    unit, scale = norm_parts(st[0])
    du = dn * vecs[0:1, :]
    back = du - jnp.mean(du, -1, keepdims=True) - unit * jnp.mean(du * unit, -1, keepdims=True)
    result = (back * scale + dbr[0].astype(F32)).astype(BF16)

    @pl.when(b == 0)
    def _():
        in_l[0] = result

    @pl.when(b > 0)
    def _():
        in_s[0] = result

    sums[0:1, :] += jnp.sum(dn * unit, 0, keepdims=True)
    sums[1:2, :] += jnp.sum(dn, 0, keepdims=True)


def near_grad(meta, grads, w, got, st, dbr, vecs):
    tokens, width = st.shape[1], st.shape[2]
    whole = lambda *shape: pl.BlockSpec(shape, lambda b, *_: (0,) * len(shape))
    part = pl.BlockSpec((1, tokens, width), lambda b, *_: (b, 0, 0))
    rows = lambda d: pl.BlockSpec((tokens, d.shape[1]), lambda b, *_: (b, 0))
    single = jax.ShapeDtypeStruct((1, tokens, width), BF16)
    return pl.pallas_call(
        near_grad_kernel,
        grid_spec=pltpu.PrefetchScalarGridSpec(
            num_scalar_prefetch=1,
            grid=(2,),
            in_specs=[
                *map(rows, grads), whole(*w.shape), whole(*got.shape), part, part, whole(*vecs.shape),
            ],
            out_specs=[whole(1, tokens, width), whole(1, tokens, width), whole(8, width)],
            scratch_shapes=[pltpu.VMEM((tokens, width), F32)],
        ),
        out_shape=[single, single, jax.ShapeDtypeStruct((8, width), F32)],
        compiler_params=params(),
        cost_estimate=cost(4 * tokens * width * 3 * width, 15e6),
        name="near_grad",
    )(meta, *grads, w, got, st, dbr, vecs)


def outer(left, right):
    rows = lambda x: x.reshape(-1, x.shape[-1])
    full = jnp.einsum("ni,nj->ij", rows(left), rows(right), preferred_element_type=F32)
    return full.astype(BF16)


def plus(x, y):
    return (x.astype(F32) + y.astype(F32)).astype(BF16)


PLACE = 256


def mlp_place_kernel(meta_s, turned, value, *rest):
    down, up = rest[-2:]
    down[...] = turned[0, 0].T.astype(F32)
    up[...] = value[0, 0].astype(F32)


def mlp_place(meta, theirs, grads, earlier=()):
    width = grads.shape[2]
    per = width // PLACE
    spot = lambda h, m: 2 * (m[2] if theirs else 1 - m[2]) + h
    return pl.pallas_call(
        mlp_place_kernel,
        grid_spec=pltpu.PrefetchScalarGridSpec(
            num_scalar_prefetch=1,
            grid=(2, per),
            in_specs=[
                pl.BlockSpec((1, 1, width, PLACE), lambda h, r, m: (h, 0, 0, r)),
                pl.BlockSpec((1, 1, PLACE, width), lambda h, r, m: (h, 1, r, 0)),
            ]
            + [pl.BlockSpec(memory_space=pl.ANY)] * len(earlier),
            out_specs=[
                pl.BlockSpec((PLACE, width), lambda h, r, m: (spot(h, m) * per + r, 0)),
                pl.BlockSpec((PLACE, width), lambda h, r, m: (r, spot(h, m))),
            ],
        ),
        out_shape=[
            jax.ShapeDtypeStruct((4 * width, width), F32),
            jax.ShapeDtypeStruct((width, 4 * width), F32),
        ],
        input_output_aliases={3 + n: n for n in range(len(earlier))},
        compiler_params=params(2),
        cost_estimate=cost(1e6, 14e6),
        name="mlp_place",
    )(meta, grads, grads, *earlier)


GROUPS = 3


def att_place_kernel(meta_s, *refs):
    parts, last, (qkv, proj) = refs[:GROUPS], refs[GROUPS], refs[-2:]
    cols = parts[0].shape[1]

    @pl.when(pl.program_id(0) < 3)
    def _():
        for n, part in enumerate(parts):
            qkv[:, n * cols : (n + 1) * cols] = part[...].astype(F32)

    @pl.when(pl.program_id(0) == 3)
    def _():
        proj[...] = last[...].astype(F32)


def att_place(meta, theirs, grads, earlier=()):
    half, width = grads.shape[0], 2 * grads.shape[0]
    spot = lambda m: m[2] if theirs else 1 - m[2]
    group = lambda n: pl.BlockSpec(
        (half, width // GROUPS), lambda j, m: (0, 3 * n + jnp.minimum(j, 2))
    )
    return pl.pallas_call(
        att_place_kernel,
        grid_spec=pltpu.PrefetchScalarGridSpec(
            num_scalar_prefetch=1,
            grid=(4,),
            in_specs=[group(n) for n in range(GROUPS)]
            + [pl.BlockSpec((half, width), lambda j, m: (0, 3))]
            + [pl.BlockSpec(memory_space=pl.ANY)] * len(earlier),
            out_specs=[
                pl.BlockSpec((half, width), lambda j, m: (spot(m), jnp.minimum(j, 2))),
                pl.BlockSpec((half, width), lambda j, m: (spot(m), 0)),
            ],
        ),
        out_shape=[
            jax.ShapeDtypeStruct((width, 3 * width), F32),
            jax.ShapeDtypeStruct((width, width), F32),
        ],
        input_output_aliases={2 + GROUPS + n: n for n in range(len(earlier))},
        compiler_params=params(),
        cost_estimate=cost(1e6, 14e6),
        name="att_place",
    )(meta, *[grads] * (GROUPS + 1), *earlier)


def swap_with(x, axis, bit=1):
    count = lax.axis_size(axis)
    return lax.ppermute(x, axis, [(i, i ^ bit) for i in range(count)])


ALL = ("chips", "core", "ulysses")


def chains():
    count = lax.axis_size("chips") * 4
    bits = [1] + [1 << n for n in range(2, count.bit_length() - 1)]
    swapped = list(bits)
    for n in range(0, len(bits) - 1, 2):
        swapped[n], swapped[n + 1] = bits[n + 1], bits[n]
    return count, bits, swapped


class Chain:
    def __init__(self, x, more, axis):
        self.x, self.more, self.axis, self.at = x, more, axis, 0
        self.count, *self.orders = chains()
        self.hops = len(self.orders[0])

    def swap(self, x, hop):
        pairs = [(i, i ^ self.orders[(i >> 1) & 1][hop]) for i in range(self.count)]
        return lax.ppermute(x, ALL, pairs)

    def bit(self, hop):
        place = lax.axis_index(ALL)
        step = jnp.where(lax.axis_index("core") == 0, self.orders[0][hop], self.orders[1][hop])
        return jnp.minimum(place & step, 1)

    def cut(self, x, which):
        half = x.shape[self.axis] // 2
        return lax.dynamic_slice_in_dim(x, which * half, half, self.axis)

    def piece(self, which):
        part = self.cut(self.x, which).astype(F32)
        return part if self.more is None else part + self.cut(self.more, which).astype(F32)

    def add(self, hop):
        self.x = (self.piece(self.bit(hop)) + self.got.astype(F32)).astype(BF16)
        self.more = None

    def join(self, hop):
        first = self.bit(hop) == 0
        low = jnp.where(first, self.x, self.got)
        high = jnp.where(first, self.got, self.x)
        self.x = jnp.concatenate([low, high], self.axis)

    @property
    def plan(self):
        wide = min(2, self.hops)
        steps = [("halve", hop) for hop in range(wide)]
        steps += [("whole", hop) for hop in range(wide, self.hops)]
        return steps + [("gather", hop) for hop in range(wide - 1, -1, -1)]

    @property
    def done(self):
        return self.at > len(self.plan)

    def prepare(self):
        plan, at = self.plan, self.at
        self.at += 1
        if at:
            kind, hop = plan[at - 1]
            if kind == "halve":
                self.add(hop)
            elif kind == "whole":
                self.x = plus(self.x, self.got)
            else:
                self.join(hop)
        if at == len(plan):
            self.out = None
            return
        kind, self.hop = plan[at]
        self.out = self.x
        if kind == "halve":
            self.out = self.piece(1 - self.bit(self.hop)).astype(BF16)

    def fire(self):
        self.got = self.swap(self.out, self.hop)


class Butterfly:
    def __init__(self, x):
        self.x, self.at = x, 0
        self.count = lax.axis_size("chips") * 4
        self.hops = self.count.bit_length() - 1

    @property
    def done(self):
        return self.at > self.hops

    def prepare(self):
        if self.at:
            self.x = self.x + self.got
        self.out = self.x if self.at < self.hops else None
        self.at += 1

    def fire(self):
        bit = 1 << (self.at - 1)
        self.got = lax.ppermute(self.out, ALL, [(i, i ^ bit) for i in range(self.count)])


def advance(values, *running):
    running = [chain for chain in running if not chain.done]
    for chain in running:
        chain.prepare()
    outs = [chain.x if chain.out is None else chain.out for chain in running]
    tied = tie(*outs, *values)
    for chain, out in zip(running, tied):
        if chain.out is None:
            chain.x = out
        else:
            if chain.out is chain.x:
                chain.x = out
            chain.out = out
            chain.fire()
    return tied[len(running) :]


def tie(*values):
    return lax.optimization_barrier(values)


def body(
    inputs_long,
    inputs_short,
    steps_long,
    steps_short,
    lengths,
    time_table,
    attngain,
    attnshift,
    qkvweight,
    querybias,
    valuebias,
    projweight,
    projbias,
    mlpgain,
    mlpshift,
    upweight,
    upbias,
    downweight,
    downbias,
    upstream_long,
    upstream_short,
):
    tokens, width = inputs_long.shape[1], inputs_long.shape[2]
    side = lax.axis_index("ulysses")
    core = lax.axis_index("core")
    meta = jnp.stack([side * tokens, side, 1 - core]).astype(jnp.int32)
    vecs, ub = pack(
        (attngain, attnshift, querybias, valuebias, projbias, mlpgain, mlpshift, downbias), upbias
    )

    edge = lax.dynamic_slice_in_dim(inputs_short[0], (1 - side) * (tokens - HALO), HALO, 0)
    across = jnp.concatenate([inputs_long[0], edge], axis=0)
    across = swap_with(across, "ulysses")

    q, ko, vo, start, rows, norm_s, norm_k = own_tokens(
        lengths, steps_short, steps_long, meta, inputs_long, inputs_short, time_table, vecs, qkvweight
    )
    kr, vr, norm_s, norm_k = far_tokens(lengths, meta, across, rows, vecs, qkvweight, norm_s, norm_k)
    att, lse, bias = attend(lengths, meta, q, ko, vo, kr, vr)
    core_swap = lambda x: swap_with(x, "core")
    send, n2, seed, mid, outacc, dn2acc, att_s, att_k, ub_a = ffn_a(
        meta, att, start, upstream_long, upstream_short, vecs, ub, projweight, upweight, downweight
    )
    send, n2 = tie(send, n2)
    got = core_swap(send)
    out_long, out_short, keep, dbr, datt, sums_mlp, ub_b = ffn_b(
        meta, n2, seed, mid, outacc, dn2acc, vecs, ub, projweight, upweight, downweight
    )
    mlp = Chain(keep, got, 2)
    (datt,) = advance((datt,), mlp)

    count = width // PAIR // GROUPS
    grads, head_sums = [], []
    for n in range(GROUPS):
        d, sums = attend_back(n * count, count, q, ko, vo, kr, vr, datt, lse, bias)
        grads.append(d)
        head_sums.append(sums[0:2])
        if n:
            datt, *grads = advance((datt, *grads), mlp)
        else:
            datt, *grads = tie(datt, *grads)
    shares = lambda norm, att_half: jnp.concatenate(
        [outer(norm, d) for d in grads] + [outer(att_half, dbr)], 1
    )
    send = shares(norm_s, att_s)
    send, *grads = tie(send, *grads)
    got = core_swap(send)
    rest = Chain(shares(norm_k, att_k), got, 0)
    grads = advance(grads, rest)
    grads = advance(grads, mlp, rest)
    back = far_grad(meta, grads, qkvweight, kr.shape[0])
    (back,) = advance((back,), rest)
    back = swap_with(back, "ulysses")
    grads = advance(grads, mlp)
    in_long, in_short, sums_in = near_grad(meta, grads, qkvweight, back, start, dbr, vecs)
    small = Butterfly(
        jnp.concatenate(
            [
                sums_in[0:2],
                jnp.concatenate(head_sums, 1),
                sums_mlp[0:4],
                (ub_a + ub_b).reshape(-1, width),
            ],
            0,
        )
    )
    advance((), mlp, small)
    advance((), rest, small)
    advance((), rest, small)
    while not mlp.done:
        advance((), mlp)
    mlp_other = core_swap(mlp.x)
    held = mlp_place(meta, False, mlp.x)
    while not (rest.done and small.done):
        advance((), rest, small)
    rest_other = core_swap(rest.x)
    held = mlp_place(meta, True, mlp_other, held)
    rest_x, *held = tie(rest.x, *held)
    placed = att_place(meta, False, rest_x)
    g_down, g_up = held
    g_qkv, g_proj = att_place(meta, True, rest_other, placed)
    small = small.x
    return (
        out_long,
        out_short,
        in_long,
        in_short,
        small[0],
        small[1],
        g_qkv,
        small[2],
        small[3],
        g_proj,
        small[4],
        small[5],
        small[6],
        g_up,
        small[8:].reshape(-1),
        g_down,
        small[7],
    )


def solution(mesh):
    seq, pair = mesh.shape["seq"], mesh.shape["ulysses"]
    split = jax.sharding.Mesh(mesh.devices.reshape(seq // 2, 2, pair), ("chips", "core", "ulysses"))
    rows = ("chips", "core")
    tokens = P(rows, "ulysses", None)
    placed = (tokens, tokens, P(rows), P(rows, None), P(rows, None)) + (P(),) * 14 + (tokens,) * 2
    return jax.shard_map(
        body,
        mesh=split,
        in_specs=placed,
        out_specs=(tokens,) * 4 + (P(),) * 13,
        check_vma=False,
    )
```

```python
import functools

import jax
import jax.numpy as jnp
from jax import lax
from jax.experimental import pallas as pl
from jax.experimental.pallas import tpu as pltpu
from jax.sharding import PartitionSpec as P

HEAD = 64
PAIR = 2 * HEAD
HALO = 64
EPS = 1e-05
GROUP = 16
F32 = jnp.float32
BF16 = jnp.bfloat16
VMEM_LIMIT = 56 * 1024 * 1024

NT = (((1,), (1,)), ((), ()))
NN = (((1,), (0,)), ((), ()))


def mm(left, right, dims=NN):
    return lax.dot_general(left, right, dims, preferred_element_type=F32)


def params(steps=1):
    return pltpu.CompilerParams(
        vmem_limit_bytes=VMEM_LIMIT, dimension_semantics=("arbitrary",) * steps
    )


def cost(flops, moved, scale=1):
    return pl.CostEstimate(flops=int(flops * scale), bytes_accessed=int(moved * scale), transcendentals=0)


def norm_parts(values_in):
    centre = values_in - jnp.mean(values_in, -1, keepdims=True)
    spread = jnp.mean(centre * centre, -1, keepdims=True)
    scale = lax.rsqrt(spread + EPS)
    return centre * scale, scale


def bounds_rows(lengths_s, segs, width):
    lane = lax.broadcasted_iota(jnp.int32, (1, width), 1)
    low = jnp.zeros((1, width), jnp.int32)
    high = jnp.zeros((1, width), jnp.int32)
    at = jnp.int32(0)
    for k in range(segs):
        low = jnp.where(lane == k, at, low)
        at = at + lengths_s[0, k]
        high = jnp.where(lane == k, at, high)
    return lane, low, high


def pack_kernel(*refs):
    vecs, ub = refs[-2:]
    for n, ref in enumerate(refs[:-3]):
        vecs[n : n + 1, :] = ref[...].astype(F32).reshape(1, -1)
    ub[...] = refs[-3][...].astype(F32).reshape(1, -1)


def pack(vectors, wide):
    width = vectors[0].shape[0]
    return pl.pallas_call(
        pack_kernel,
        out_shape=[
            jax.ShapeDtypeStruct((len(vectors), width), F32),
            jax.ShapeDtypeStruct((1, wide.shape[0]), F32),
        ],
        cost_estimate=cost(1e6, 1e5),
        name="pack",
    )(*vectors, wide)


def own_kernel(
    lengths_s, steps_short_s, steps_long_s, meta_s,
    xl, xs, table, vecs, w,
    q_o, k_o, v_o, st_o, rows_o, ns_o, nk_o,
    buf, sem,
):
    b = pl.program_id(0)
    segs = lengths_s.shape[1]
    tokens, width = xl.shape[1], xl.shape[2]

    @pl.when(b == 0)
    def _():
        copies = []
        target = jnp.zeros((32, buf.shape[0]), jnp.int32) - 1
        sub = lax.broadcasted_iota(jnp.int32, (32, buf.shape[0]), 0)
        for k in range(segs + 1):
            step = steps_short_s[0, k] if k < segs else steps_long_s[0]
            base = pl.multiple_of((step // GROUP) * GROUP, GROUP)
            copy = pltpu.make_async_copy(
                table.at[pl.ds(base, GROUP), :], buf.at[pl.ds(k * GROUP, GROUP), :], sem.at[k]
            )
            copy.start()
            copies.append(copy)
            target = jnp.where(sub == k, k * GROUP + step - base, target)
        rest = buf.shape[0] - (segs + 1) * GROUP
        if rest:
            buf[pl.ds((segs + 1) * GROUP, rest), :] = jnp.zeros((rest, width), BF16)
        for copy in copies:
            copy.wait()
        lane = lax.broadcasted_iota(jnp.int32, (32, buf.shape[0]), 1)
        pick = jnp.where(lane == target, 1.0, 0.0).astype(BF16)
        rows_o[...] = mm(pick, buf[...]).astype(BF16)

    lane, low, high = bounds_rows(lengths_s, segs, 32)
    whole = lane == segs
    low = jnp.where(b == 0, 0, low)
    high = jnp.where(b == 0, jnp.where(whole, 1 << 30, 0), high)
    place = meta_s[0] + lax.broadcasted_iota(jnp.int32, (tokens, 1), 0)
    pick = jnp.where((place >= low) & (place < high), 1.0, 0.0).astype(BF16)
    embed = mm(pick, rows_o[...])
    start = jnp.where(b == 0, xl[0], xs[0]).astype(F32) + embed
    st_o[0] = start
    unit, _ = norm_parts(start)
    normed = (unit * vecs[0:1, :] + vecs[1:2, :]).astype(BF16)
    left, right = normed[:, : width // 2], normed[:, width // 2 :]
    ns_o[...] = jnp.where(meta_s[2] == 1, right, left)
    nk_o[...] = jnp.where(meta_s[2] == 1, left, right)
    q_o[0] = ((mm(normed, w[:, :width]) + vecs[2:3, :]) * HEAD ** (-0.5)).astype(BF16)
    k_o[0] = mm(normed, w[:, width : 2 * width]).astype(BF16)
    v_o[0] = (mm(normed, w[:, 2 * width :]) + vecs[3:4, :]).astype(BF16)


def own_tokens(lengths, steps_short, steps_long, meta, xl, xs, table, vecs, w):
    tokens, width = xl.shape[1], xl.shape[2]
    segs = lengths.shape[1]
    spots = -(-(segs + 1) * GROUP // 128) * 128
    whole = lambda *shape: pl.BlockSpec(shape, lambda b, *_: (0,) * len(shape))
    part = pl.BlockSpec((1, tokens, width), lambda b, *_: (b, 0, 0))
    half = pl.BlockSpec((tokens, width // 2), lambda b, *_: (b, 0))
    stacked = jax.ShapeDtypeStruct((2, tokens, width), BF16)
    return pl.pallas_call(
        own_kernel,
        grid_spec=pltpu.PrefetchScalarGridSpec(
            num_scalar_prefetch=4,
            grid=(2,),
            in_specs=[
                whole(1, tokens, width),
                whole(1, tokens, width),
                pl.BlockSpec(memory_space=pl.ANY),
                whole(*vecs.shape),
                whole(*w.shape),
            ],
            out_specs=[part] * 4 + [whole(32, width)] + [half, half],
            scratch_shapes=[pltpu.VMEM((spots, width), BF16), pltpu.SemaphoreType.DMA((segs + 1,))],
        ),
        out_shape=[stacked] * 3
        + [jax.ShapeDtypeStruct((2, tokens, width), F32), jax.ShapeDtypeStruct((32, width), BF16)]
        + [jax.ShapeDtypeStruct((3 * tokens + 2 * HALO, width // 2), BF16)] * 2,
        compiler_params=params(),
        cost_estimate=cost(4 * tokens * width * 3 * width, 14e6),
        name="own_tokens",
    )(lengths, steps_short, steps_long, meta, xl, xs, table, vecs, w)


def far_kernel(
    lengths_s, meta_s, xr, xe, rows, vecs, wk, wv, ns_i, nk_i, k_o, v_o, ns_o, nk_o, ns, nk, sem
):
    segs = lengths_s.shape[1]
    total, width = k_o.shape
    tokens = total - 2 * HALO
    side = meta_s[1]
    edge = xe[...].astype(F32)
    before = jnp.where(side == 1, edge, 0.0)
    after = jnp.where(side == 0, edge, 0.0)
    x = jnp.concatenate([xr[...].astype(F32), before, after], axis=0)
    lane, low, high = bounds_rows(lengths_s, segs, 32)
    row = lax.broadcasted_iota(jnp.int32, (total, 1), 0)
    place = meta_s[0] + row - HALO - jnp.where(row < tokens + HALO, tokens, 0)
    inside = (place >= low) & (place < high)
    story = jnp.where(lane == segs, 1.0, 0.0)
    pick = jnp.where(row < tokens, story, jnp.where(inside, 1.0, 0.0)).astype(BF16)
    start = x + mm(pick, rows[...])
    unit, _ = norm_parts(start)
    normed = (unit * vecs[0:1, :] + vecs[1:2, :]).astype(BF16)
    left, right = normed[:, : width // 2], normed[:, width // 2 :]
    ns[...] = jnp.where(meta_s[2] == 1, right, left)
    nk[...] = jnp.where(meta_s[2] == 1, left, right)
    rest = pl.ds(2 * tokens, total)
    copy_s = pltpu.make_async_copy(ns, ns_o.at[rest, :], sem.at[0])
    copy_k = pltpu.make_async_copy(nk, nk_o.at[rest, :], sem.at[1])
    copy_s.start()
    copy_k.start()
    k_o[...] = mm(normed, wk[...]).astype(BF16)
    v_o[...] = (mm(normed, wv[...]) + vecs[3:4, :]).astype(BF16)
    copy_s.wait()
    copy_k.wait()


def far_tokens(lengths, meta, xr, xe, rows, vecs, w, ns, nk):
    width = xr.shape[1]
    total = xr.shape[0] + 2 * HALO
    whole = lambda *shape: pl.BlockSpec(shape, lambda i, *_: (0,) * len(shape))
    out = jax.ShapeDtypeStruct((total, width), BF16)
    return pl.pallas_call(
        far_kernel,
        grid_spec=pltpu.PrefetchScalarGridSpec(
            num_scalar_prefetch=2,
            grid=(1,),
            in_specs=[
                whole(*xr.shape),
                whole(*xe.shape),
                whole(*rows.shape),
                whole(*vecs.shape),
                pl.BlockSpec((width, width), lambda i, *_: (0, 1)),
                pl.BlockSpec((width, width), lambda i, *_: (0, 2)),
                pl.BlockSpec(memory_space=pl.ANY),
                pl.BlockSpec(memory_space=pl.ANY),
            ],
            out_specs=[whole(total, width)] * 2 + [pl.BlockSpec(memory_space=pl.ANY)] * 2,
            scratch_shapes=[pltpu.VMEM((total, width // 2), BF16)] * 2
            + [pltpu.SemaphoreType.DMA((2,))],
        ),
        out_shape=[out] * 2 + [jax.ShapeDtypeStruct(ns.shape, BF16)] * 2,
        input_output_aliases={8: 2, 9: 3},
        compiler_params=params(),
        cost_estimate=cost(2 * total * width * 2 * width, 6e6),
        name="far_tokens",
    )(lengths, meta, xr, xe, rows, vecs, w, w, ns, nk)


def seg_of(lengths_s, place):
    segs = lengths_s.shape[1]
    at = jnp.int32(0)
    seg = jnp.zeros(place.shape, jnp.int32)
    for k in range(segs - 1):
        at = at + lengths_s[0, k]
        seg = seg + jnp.where(place >= at, 1, 0)
    at = at + lengths_s[0, segs - 1]
    return jnp.where(place < 0, -1, jnp.where(place >= at, -2, seg))


def halves():
    lane = lax.broadcasted_iota(jnp.int32, (1, PAIR), 1)
    return (lane < HEAD, lane >= HEAD)


def attend_kernel(lengths_s, meta_s, q, ko, vo, kr, vr, o, lse, bias_t, bias, kx, vx):
    tokens = q.shape[1]
    blocks = tokens // 128
    span = 128 + 2 * HALO

    @pl.when(pl.program_id(0) == 0)
    def _():
        seg_q = seg_of(lengths_s, meta_s[0] + lax.broadcasted_iota(jnp.int32, (tokens, 1), 0))
        seg_k = seg_of(
            lengths_s, meta_s[0] - HALO + lax.broadcasted_iota(jnp.int32, (1, tokens + 2 * HALO), 1)
        )
        for i in range(blocks):
            same = seg_q[i * 128 : (i + 1) * 128, :] == seg_k[:, i * 128 : i * 128 + span]
            bias[i] = jnp.where(same, 0.0, -1e30)
            bias_t[i] = bias[i].T

    for ext, own, far in ((kx, ko, kr), (vx, vo, vr)):
        ext[0:HALO, :] = far[tokens : tokens + HALO, :]
        ext[HALO : HALO + tokens, :] = own[1]
        ext[HALO + tokens :, :] = far[tokens + HALO :, :]

    lane = lax.broadcasted_iota(jnp.int32, (1, PAIR), 1)
    stats = jnp.zeros((tokens, 128), F32)
    step = 256
    for h, half in enumerate(halves()):
        logs = []
        for i in range(tokens // step):
            rows = pl.ds(i * step, step)
            qh = jnp.where(half, q[0, rows, :], 0)
            s1 = mm(qh, ko[0], NT)
            s2 = mm(qh, kr[:tokens, :], NT)
            top = jnp.maximum(jnp.max(s1, -1, keepdims=True), jnp.max(s2, -1, keepdims=True))
            e1 = jnp.exp(s1 - top)
            e2 = jnp.exp(s2 - top)
            total = jnp.sum(e1, -1, keepdims=True) + jnp.sum(e2, -1, keepdims=True)
            r = mm(e1.astype(BF16), vo[0]) + mm(e2.astype(BF16), vr[:tokens, :])
            r = (r / total).astype(BF16)
            o[0, rows, :] = r if h == 0 else jnp.where(half, r, o[0, rows, :])
            logs.append(top + jnp.log(total))
        stats = jnp.where(lane == h, jnp.concatenate(logs, 0), stats)
        logs = []
        for i in range(blocks):
            rows = pl.ds(i * 128, 128)
            keys = pl.ds(i * 128, span)
            qh = jnp.where(half, q[1, rows, :], 0)
            s1 = mm(qh, kx[keys, :], NT) + bias[i]
            top = jnp.max(s1, -1, keepdims=True)
            e1 = jnp.exp(s1 - top)
            total = jnp.sum(e1, -1, keepdims=True)
            r = (mm(e1.astype(BF16), vx[keys, :]) / total).astype(BF16)
            o[1, rows, :] = r if h == 0 else jnp.where(half, r, o[1, rows, :])
            logs.append(top + jnp.log(total))
        stats = jnp.where(lane == 2 + h, jnp.concatenate(logs, 0), stats)
    lse[0] = stats.T[0:8, :]


def head_specs(tokens):
    own = pl.BlockSpec((2, tokens, PAIR), lambda i, *_: (0, 0, i))
    far = pl.BlockSpec((tokens + 2 * HALO, PAIR), lambda i, *_: (0, i))
    row = pl.BlockSpec((1, 8, tokens), lambda i, *_: (i, 0, 0))
    return own, far, row


def attend(lengths, meta, q, ko, vo, kr, vr):
    tokens, width = q.shape[1], q.shape[2]
    pairs = width // PAIR
    own, far, row = head_specs(tokens)
    ext = pltpu.VMEM((tokens + 2 * HALO, PAIR), BF16)
    return pl.pallas_call(
        attend_kernel,
        grid_spec=pltpu.PrefetchScalarGridSpec(
            num_scalar_prefetch=2,
            grid=(pairs,),
            in_specs=[own, own, own, far, far],
            out_specs=[
                own, row, pl.BlockSpec((tokens // 128, 128 + 2 * HALO, 128), lambda i, *_: (0, 0, 0)),
            ],
            scratch_shapes=[pltpu.VMEM((tokens // 128, 128, 128 + 2 * HALO), F32), ext, ext],
        ),
        out_shape=[
            jax.ShapeDtypeStruct(q.shape, BF16),
            jax.ShapeDtypeStruct((pairs, 8, tokens), F32),
            jax.ShapeDtypeStruct((tokens // 128, 128 + 2 * HALO, 128), F32),
        ],
        compiler_params=params(),
        cost_estimate=cost(4 * tokens * 2.5 * tokens * 256 * 2 * pairs, 8e6),
        name="attend",
    )(lengths, meta, q, ko, vo, kr, vr)


def attend_back_kernel(
    q, ko, vo, kr, vr, go, lse, bias, grad, sums, kx, vx, kt, dkx, dvx, dqt
):
    tokens = q.shape[1]
    far_at = 2 * tokens
    third = grad.shape[1] // 3
    at = [
        pl.ds(pl.multiple_of(n * third + pl.program_id(0) * PAIR, PAIR), PAIR) for n in range(3)
    ]
    grad[far_at:, at[0]] = jnp.zeros((grad.shape[0] - far_at, PAIR), BF16)
    blocks = tokens // 128
    span = 128 + 2 * HALO

    for ext, own, far in ((kx, ko, kr), (vx, vo, vr)):
        ext[0:HALO, :] = far[tokens : tokens + HALO, :]
        ext[HALO : HALO + tokens, :] = own[1]
        ext[HALO + tokens :, :] = far[tokens + HALO :, :]

    shift = HEAD ** (-0.5)
    sum_q = jnp.zeros((1, PAIR), F32)
    sum_v = jnp.zeros((1, PAIR), F32)

    k_parts = (ko[0], kr[:tokens, :])
    v_parts = (vo[0], vr[:tokens, :])
    for n in range(2):
        kt[n, :, :tokens] = k_parts[n].T
    dk_sums = [jnp.zeros((tokens, PAIR), F32)] * 2
    dv_sums = [jnp.zeros((tokens, PAIR), F32)] * 2
    for h, half in enumerate(halves()):
        rows = pl.ds(h * HEAD, HEAD)
        qh = jnp.where(half, q[0], 0)
        gh = jnp.where(half, go[0], 0)
        log = lse[0, h : h + 1, :]
        pts = [jnp.exp(mm(k_parts[n], qh, NT) - log) for n in range(2)]
        dpts = [mm(v_parts[n], gh, NT) for n in range(2)]
        delta = jnp.sum(pts[0] * dpts[0], 0, keepdims=True)
        delta += jnp.sum(pts[1] * dpts[1], 0, keepdims=True)
        part = None
        for n in range(2):
            dst = (pts[n] * (dpts[n] - delta)).astype(BF16)
            dv_sums[n] = dv_sums[n] + mm(pts[n].astype(BF16), gh)
            dk_sums[n] = dk_sums[n] + mm(dst, qh)
            turned = mm(kt[n, rows, :tokens], dst)
            part = turned if n == 0 else part + turned
        dqt[rows, :] = part
    for n, row in enumerate((0, far_at)):
        grad[row : row + tokens, at[1]] = dk_sums[n].astype(BF16)
        grad[row : row + tokens, at[2]] = dv_sums[n].astype(BF16)
    for n in range(2):
        sum_v += jnp.sum(dv_sums[n], 0, keepdims=True)
    out = dqt[...].T * shift
    grad[:tokens, at[0]] = out.astype(BF16)
    sum_q += jnp.sum(out, 0, keepdims=True)

    kt[0] = kx[...].T
    dkx[...] = jnp.zeros_like(dkx)
    dvx[...] = jnp.zeros_like(dvx)
    for i in range(blocks):
        cols = slice(i * 128, (i + 1) * 128)
        keys = slice(i * 128, i * 128 + span)
        dk_sum = jnp.zeros((span, PAIR), F32)
        dv_sum = jnp.zeros((span, PAIR), F32)
        for h, half in enumerate(halves()):
            rows = slice(h * HEAD, (h + 1) * HEAD)
            qh = jnp.where(half, q[1, cols, :], 0)
            gh = jnp.where(half, go[1, cols, :], 0)
            st = mm(kx[keys, :], qh, NT) + bias[i]
            pt = jnp.exp(st - lse[0, 2 + h : 3 + h, cols])
            dpt = mm(vx[keys, :], gh, NT)
            delta = jnp.sum(pt * dpt, 0, keepdims=True)
            dst = (pt * (dpt - delta)).astype(BF16)
            dv_sum += mm(pt.astype(BF16), gh)
            dk_sum += mm(dst, qh)
            dqt[rows, cols] = mm(kt[0, rows, keys], dst)
        dkx[keys, :] += dk_sum
        dvx[keys, :] += dv_sum
    out = dqt[...].T * shift
    grad[tokens:far_at, at[0]] = out.astype(BF16)
    sum_q += jnp.sum(out, 0, keepdims=True)
    sum_v += jnp.sum(dvx[...], 0, keepdims=True)
    edge = far_at + tokens
    for ext, cols in ((dkx, at[1]), (dvx, at[2])):
        grad[tokens:far_at, cols] = ext[HALO : HALO + tokens, :].astype(BF16)
        grad[edge : edge + HALO, cols] = ext[0:HALO, :].astype(BF16)
        grad[edge + HALO :, cols] = ext[HALO + tokens :, :].astype(BF16)
    sums[...] = jnp.concatenate([sum_q, sum_v, jnp.zeros((6, PAIR), F32)], 0)


def attend_back(first, count, q, ko, vo, kr, vr, go, lse, bias):
    tokens, width = q.shape[1], q.shape[2]
    wide = tokens + 2 * HALO
    own = pl.BlockSpec((2, tokens, PAIR), lambda i: (0, 0, i + first))
    far = pl.BlockSpec((wide, PAIR), lambda i: (0, i + first))
    row = pl.BlockSpec((1, 8, tokens), lambda i: (i + first, 0, 0))
    ext = pltpu.VMEM((wide, PAIR), BF16)
    ext32 = pltpu.VMEM((wide, PAIR), F32)
    rows, cols = 2 * tokens + wide, 3 * count * PAIR
    return pl.pallas_call(
        attend_back_kernel,
        grid=(count,),
        in_specs=[own, own, own, far, far, own, row]
        + [pl.BlockSpec(bias.shape, lambda i: (0, 0, 0))],
        out_specs=[
            pl.BlockSpec((rows, cols), lambda i: (0, 0)),
            pl.BlockSpec((8, PAIR), lambda i: (0, i)),
        ],
        scratch_shapes=[
            ext,
            ext,
            pltpu.VMEM((2, PAIR, wide), BF16),
            ext32,
            ext32,
            pltpu.VMEM((PAIR, tokens), F32),
        ],
        out_shape=[
            jax.ShapeDtypeStruct((rows, cols), BF16),
            jax.ShapeDtypeStruct((8, count * PAIR), F32),
        ],
        compiler_params=params(),
        cost_estimate=cost(10 * tokens * 2.5 * tokens * 256 * 2 * count, 2e6 * count),
        name="attend_back",
    )(q, ko, vo, kr, vr, go, lse, bias)


def chunk_spot(c, part, meta_s):
    return 2 * jnp.where(part == 0, meta_s[2], 1 - meta_s[2]) + c


def ffn_chunk(spot, first, n2, seed, ub, wu, wd, act, dh, sums_ub):
    chunk = wu.shape[1]
    k0 = 0.7978845608028654
    piece = 256

    @pl.when(first)
    def _():
        sums_ub[...] = jnp.zeros_like(sums_ub)

    for j in range(chunk // piece):
        cols = slice(j * piece, (j + 1) * piece)
        hid = mm(n2, wu[:, cols]) + ub[0:1, cols]
        square = hid * hid
        t = jnp.tanh(hid * (k0 + k0 * 0.044715 * square))
        half = 0.5 + 0.5 * t
        act[:, cols] = (hid * half).astype(BF16)
        slope = half + (hid * (0.5 - 0.5 * (t * t))) * (k0 + 3 * k0 * 0.044715 * square)
        dh32 = mm(seed, wd[cols, :], NT) * slope
        dh[:, cols] = dh32.astype(BF16)
        at = pl.ds(pl.multiple_of(spot * chunk + j * piece, piece), piece)
        sums_ub[0:1, at] += jnp.sum(dh32, 0, keepdims=True)


def ffn_a_kernel(
    meta_s, att, st, ul, us, vecs, ub, wp, wu, wd,
    g_o, n2_o, seed_o, mid_o, out_o, dn2_o, as_o, ak_o, sums_ub,
    n2, seed, n2t, seedt, outacc, dn2acc, act, dh,
):
    c, b = pl.program_id(0), pl.program_id(1)
    half = wp.shape[0] // 2
    tokens = mid_o.shape[1]
    rows = pl.ds(pl.multiple_of(b * tokens, tokens), tokens)

    @pl.when(c == 0)
    def _():
        up = jnp.where(b == 0, ul[0], us[0])
        seed[rows, :] = up
        seed_o[0] = up
        seedt[:, rows] = up.T
        whole = att[0]
        as_o[...] = jnp.where(meta_s[2] == 1, whole[:, half:], whole[:, :half])
        ak_o[...] = jnp.where(meta_s[2] == 1, whole[:, :half], whole[:, half:])
        middle = st[0] + mm(whole, wp[...]) + vecs[4:5, :]
        mid_o[0] = middle
        unit, _ = norm_parts(middle)
        normed = (unit * vecs[5:6, :] + vecs[6:7, :]).astype(BF16)
        n2[rows, :] = normed
        n2_o[0] = normed
        n2t[:, rows] = normed.T

    spot = chunk_spot(c, 0, meta_s)
    act_b, dh_b = act.at[rows, :], dh.at[rows, :]
    ffn_chunk(spot, (b == 0) & (c == 0), n2[rows, :], seed[rows, :], ub, wu, wd, act_b, dh_b, sums_ub)
    out = mm(act_b[...], wd[...])
    dn2 = mm(dh_b[...], wu[...], NT)

    @pl.when(c == 0)
    def _():
        outacc[rows, :] = mid_o[0] + vecs[7:8, :] + out
        dn2acc[rows, :] = dn2

    @pl.when(c == 1)
    def _():
        out_o[0] = outacc[rows, :] + out
        dn2_o[0] = dn2acc[rows, :] + dn2

    @pl.when(b == 1)
    def _():
        g_o[0, 0] = mm(seedt[...], act[...]).astype(BF16)
        g_o[0, 1] = mm(n2t[...], dh[...]).astype(BF16)


def ffn_b_kernel(
    meta_s, n2, seed, mid, out_i, dn2_i, vecs, ub, wp, wu, wd,
    out_l, out_s, g_o, dbr_o, datt_o, sums, sums_ub,
    n2t, seedt, outacc, dn2acc, act, dh,
):
    c, b = pl.program_id(0), pl.program_id(1)
    tokens = mid.shape[1]
    rows = pl.ds(pl.multiple_of(b * tokens, tokens), tokens)

    @pl.when(c == 0)
    def _():
        seedt[:, rows] = seed[b].T
        n2t[:, rows] = n2[b].T

    spot = chunk_spot(c, 1, meta_s)
    act_b, dh_b = act.at[rows, :], dh.at[rows, :]
    ffn_chunk(spot, (b == 0) & (c == 0), n2[b], seed[b], ub, wu, wd, act_b, dh_b, sums_ub)
    out = mm(act_b[...], wd[...])
    dn2 = mm(dh_b[...], wu[...], NT)

    @pl.when(c == 0)
    def _():
        outacc[rows, :] = out_i[0] + out
        dn2acc[rows, :] = dn2_i[0] + dn2

    @pl.when(c == 1)
    def _():
        result = (outacc[rows, :] + out).astype(BF16)

        @pl.when(b == 0)
        def _():
            out_l[0] = result
            sums[...] = jnp.zeros_like(sums)

        @pl.when(b > 0)
        def _():
            out_s[0] = result

        unit, scale = norm_parts(mid[0])
        whole = dn2acc[rows, :] + dn2
        seed32 = seed[b].astype(F32)
        du = whole * vecs[5:6, :]
        back = du - jnp.mean(du, -1, keepdims=True) - unit * jnp.mean(du * unit, -1, keepdims=True)
        dmid = back * scale + seed32
        dbr = dmid.astype(BF16)
        dbr_o[0] = dbr
        datt_o[0] = mm(dbr, wp[...], NT).astype(BF16)
        sums[0:1, :] += jnp.sum(dmid, 0, keepdims=True)
        sums[1:2, :] += jnp.sum(whole * unit, 0, keepdims=True)
        sums[2:3, :] += jnp.sum(whole, 0, keepdims=True)
        sums[3:4, :] += jnp.sum(seed32, 0, keepdims=True)

    @pl.when(b == 1)
    def _():
        g_o[0, 0] = mm(seedt[...], act[...]).astype(BF16)
        g_o[0, 1] = mm(n2t[...], dh[...]).astype(BF16)


def ffn_specs(tokens, width, part):
    whole = lambda *shape: pl.BlockSpec(shape, lambda c, b, m: (0,) * len(shape))
    early = pl.BlockSpec((1, tokens, width), lambda c, b, m: (jnp.where(c == 0, b, 1), 0, 0))
    late = pl.BlockSpec((1, tokens, width), lambda c, b, m: (jnp.where(c == 0, 0, b), 0, 0))
    grads = pl.BlockSpec((1, 2, width, width), lambda c, b, m: (c, 0, 0, 0))
    weights = [
        pl.BlockSpec((1, width), lambda c, b, m: (0, chunk_spot(c, part, m))),
        whole(width, width),
        pl.BlockSpec((width, width), lambda c, b, m: (0, chunk_spot(c, part, m))),
        pl.BlockSpec((width, width), lambda c, b, m: (chunk_spot(c, part, m), 0)),
    ]
    shape = lambda kind: jax.ShapeDtypeStruct((2, tokens, width), kind)
    low, high = pltpu.VMEM((2 * tokens, width), BF16), pltpu.VMEM((2 * tokens, width), F32)
    turned = pltpu.VMEM((width, 2 * tokens), BF16)
    return whole, early, late, grads, weights, shape, low, high, turned


def ffn_a(meta, att, st, ul, us, vecs, ub, wp, wu, wd):
    tokens, width = ul.shape[1], ul.shape[2]
    hidden = wu.shape[1]
    whole, early, late, grads, weights, shape, low, high, turned = ffn_specs(tokens, width, 0)
    single = whole(1, tokens, width)
    half = pl.BlockSpec((tokens, width // 2), lambda c, b, m: (jnp.where(c == 0, b, 1), 0))
    return pl.pallas_call(
        ffn_a_kernel,
        grid_spec=pltpu.PrefetchScalarGridSpec(
            num_scalar_prefetch=1,
            grid=(2, 2),
            in_specs=[early, early, single, single, whole(*vecs.shape)] + weights,
            out_specs=[grads, early, early, early, late, late, half, half, whole(1, hidden)],
            scratch_shapes=[low, low, turned, turned, high, high, low, low],
        ),
        out_shape=[jax.ShapeDtypeStruct((2, 2, width, width), BF16)]
        + [shape(BF16)] * 2
        + [shape(F32)] * 3
        + [jax.ShapeDtypeStruct((2 * tokens, width // 2), BF16)] * 2
        + [jax.ShapeDtypeStruct((1, hidden), F32)],
        compiler_params=params(2),
        cost_estimate=cost(4 * tokens * width * (width + 3 * hidden), 40e6),
        name="ffn_a",
    )(meta, att, st, ul, us, vecs, ub, wp, wu, wd)


def ffn_b(meta, n2, seed, mid, outacc, dn2acc, vecs, ub, wp, wu, wd):
    tokens, width = mid.shape[1], mid.shape[2]
    hidden = wu.shape[1]
    whole, early, late, grads, weights, shape, low, high, turned = ffn_specs(tokens, width, 1)
    single = jax.ShapeDtypeStruct((1, tokens, width), BF16)
    both = whole(2, tokens, width)
    return pl.pallas_call(
        ffn_b_kernel,
        grid_spec=pltpu.PrefetchScalarGridSpec(
            num_scalar_prefetch=1,
            grid=(2, 2),
            in_specs=[both, both, late, early, early, whole(*vecs.shape)] + weights,
            out_specs=[whole(1, tokens, width)] * 2
            + [grads, late, late, whole(8, width), whole(1, hidden)],
            scratch_shapes=[turned, turned, high, high, low, low],
        ),
        out_shape=[single, single, jax.ShapeDtypeStruct((2, 2, width, width), BF16)]
        + [shape(BF16)] * 2
        + [jax.ShapeDtypeStruct((8, width), F32), jax.ShapeDtypeStruct((1, hidden), F32)],
        compiler_params=params(2),
        cost_estimate=cost(4 * tokens * width * (width + 3 * hidden), 40e6),
        name="ffn_b",
    )(meta, n2, seed, mid, outacc, dn2acc, vecs, ub, wp, wu, wd)


def back_through(grads, w):
    width = w.shape[0]
    total, first = None, 0
    for grad in grads:
        cols = grad.shape[1] // 3
        for n in range(3):
            piece = grad[:, n * cols : (n + 1) * cols]
            part = mm(piece, w[:, n * width + first : n * width + first + cols], NT)
            total = part if total is None else total + part
        first += cols
    return total


def far_grad_kernel(meta_s, *refs):
    count = (len(refs) - 3) // 2
    sources, w, d_o, held, sem = refs[:count], refs[count], refs[count + 1], refs[count + 2 : -1], refs[-1]
    total = held[0].shape[0]
    tokens = total - 2 * HALO
    copies = []
    for n, (source, target) in enumerate(zip(sources, held)):
        copy = pltpu.make_async_copy(source.at[pl.ds(2 * tokens, total), :], target, sem.at[n])
        copy.start()
        copies.append(copy)
    for copy in copies:
        copy.wait()
    full = back_through(held, w)
    d_o[0:tokens, :] = full[0:tokens, :].astype(BF16)
    before = full[tokens : tokens + HALO, :]
    after = full[tokens + HALO :, :]
    d_o[tokens:, :] = jnp.where(meta_s[1] == 1, before, after).astype(BF16)


def far_grad(meta, grads, w, total):
    width = w.shape[0]
    whole = lambda *shape: pl.BlockSpec(shape, lambda i, *_: (0,) * len(shape))
    return pl.pallas_call(
        far_grad_kernel,
        grid_spec=pltpu.PrefetchScalarGridSpec(
            num_scalar_prefetch=1,
            grid=(1,),
            in_specs=[pl.BlockSpec(memory_space=pl.ANY)] * len(grads) + [whole(*w.shape)],
            out_specs=whole(total - HALO, width),
            scratch_shapes=[pltpu.VMEM((total, d.shape[1]), BF16) for d in grads]
            + [pltpu.SemaphoreType.DMA((len(grads),))],
        ),
        out_shape=jax.ShapeDtypeStruct((total - HALO, width), BF16),
        compiler_params=params(),
        cost_estimate=cost(4 * total * width * width, 5e6),
        name="far_grad",
    )(meta, *grads, w)


def near_grad_kernel(meta_s, *refs):
    grads, (w, got, st, dbr, vecs, in_l, in_s, sums, acc) = refs[:-9], refs[-9:]
    b = pl.program_id(0)
    tokens = st.shape[1]
    acc[...] = back_through(grads, w)

    @pl.when(b == 0)
    def _():
        acc[...] += got[0:tokens, :].astype(F32)
        sums[...] = jnp.zeros_like(sums)

    @pl.when(b > 0)
    def _():
        edge = got[tokens:, :].astype(F32)
        acc[0:HALO, :] += jnp.where(meta_s[1] == 1, edge, 0.0)
        acc[tokens - HALO :, :] += jnp.where(meta_s[1] == 0, edge, 0.0)

    dn = acc[...]
    unit, scale = norm_parts(st[0])
    du = dn * vecs[0:1, :]
    back = du - jnp.mean(du, -1, keepdims=True) - unit * jnp.mean(du * unit, -1, keepdims=True)
    result = (back * scale + dbr[0].astype(F32)).astype(BF16)

    @pl.when(b == 0)
    def _():
        in_l[0] = result

    @pl.when(b > 0)
    def _():
        in_s[0] = result

    sums[0:1, :] += jnp.sum(dn * unit, 0, keepdims=True)
    sums[1:2, :] += jnp.sum(dn, 0, keepdims=True)


def near_grad(meta, grads, w, got, st, dbr, vecs):
    tokens, width = st.shape[1], st.shape[2]
    whole = lambda *shape: pl.BlockSpec(shape, lambda b, *_: (0,) * len(shape))
    part = pl.BlockSpec((1, tokens, width), lambda b, *_: (b, 0, 0))
    rows = lambda d: pl.BlockSpec((tokens, d.shape[1]), lambda b, *_: (b, 0))
    single = jax.ShapeDtypeStruct((1, tokens, width), BF16)
    return pl.pallas_call(
        near_grad_kernel,
        grid_spec=pltpu.PrefetchScalarGridSpec(
            num_scalar_prefetch=1,
            grid=(2,),
            in_specs=[
                *map(rows, grads), whole(*w.shape), whole(*got.shape), part, part, whole(*vecs.shape),
            ],
            out_specs=[whole(1, tokens, width), whole(1, tokens, width), whole(8, width)],
            scratch_shapes=[pltpu.VMEM((tokens, width), F32)],
        ),
        out_shape=[single, single, jax.ShapeDtypeStruct((8, width), F32)],
        compiler_params=params(),
        cost_estimate=cost(4 * tokens * width * 3 * width, 15e6),
        name="near_grad",
    )(meta, *grads, w, got, st, dbr, vecs)


def outer(left, right):
    rows = lambda x: x.reshape(-1, x.shape[-1])
    full = jnp.einsum("ni,nj->ij", rows(left), rows(right), preferred_element_type=F32)
    return full.astype(BF16)


def plus(x, y):
    return (x.astype(F32) + y.astype(F32)).astype(BF16)


PLACE = 384


def mlp_place_kernel(meta_s, turned, value, *rest):
    down, up = rest[-2:]
    down[...] = turned[0, 0].T.astype(F32)
    up[...] = value[0, 0].astype(F32)


def mlp_place(meta, theirs, grads, earlier=()):
    width = grads.shape[2]
    per = width // PLACE
    spot = lambda h, m: 2 * (m[2] if theirs else 1 - m[2]) + h
    return pl.pallas_call(
        mlp_place_kernel,
        grid_spec=pltpu.PrefetchScalarGridSpec(
            num_scalar_prefetch=1,
            grid=(2, per),
            in_specs=[
                pl.BlockSpec((1, 1, width, PLACE), lambda h, r, m: (h, 0, 0, r)),
                pl.BlockSpec((1, 1, PLACE, width), lambda h, r, m: (h, 1, r, 0)),
            ]
            + [pl.BlockSpec(memory_space=pl.ANY)] * len(earlier),
            out_specs=[
                pl.BlockSpec((PLACE, width), lambda h, r, m: (spot(h, m) * per + r, 0)),
                pl.BlockSpec((PLACE, width), lambda h, r, m: (r, spot(h, m))),
            ],
        ),
        out_shape=[
            jax.ShapeDtypeStruct((4 * width, width), F32),
            jax.ShapeDtypeStruct((width, 4 * width), F32),
        ],
        input_output_aliases={3 + n: n for n in range(len(earlier))},
        compiler_params=params(2),
        cost_estimate=cost(1e6, 14e6),
        name="mlp_place",
    )(meta, grads, grads, *earlier)


GROUPS = 3


def att_place_kernel(meta_s, *refs):
    parts, last, (qkv, proj) = refs[:GROUPS], refs[GROUPS], refs[-2:]
    cols = parts[0].shape[1]

    @pl.when(pl.program_id(0) < 3)
    def _():
        for n, part in enumerate(parts):
            qkv[:, n * cols : (n + 1) * cols] = part[...].astype(F32)

    @pl.when(pl.program_id(0) == 3)
    def _():
        proj[...] = last[...].astype(F32)


def att_place(meta, theirs, grads, earlier=()):
    half, width = grads.shape[0], 2 * grads.shape[0]
    spot = lambda m: m[2] if theirs else 1 - m[2]
    group = lambda n: pl.BlockSpec(
        (half, width // GROUPS), lambda j, m: (0, 3 * n + jnp.minimum(j, 2))
    )
    return pl.pallas_call(
        att_place_kernel,
        grid_spec=pltpu.PrefetchScalarGridSpec(
            num_scalar_prefetch=1,
            grid=(4,),
            in_specs=[group(n) for n in range(GROUPS)]
            + [pl.BlockSpec((half, width), lambda j, m: (0, 3))]
            + [pl.BlockSpec(memory_space=pl.ANY)] * len(earlier),
            out_specs=[
                pl.BlockSpec((half, width), lambda j, m: (spot(m), jnp.minimum(j, 2))),
                pl.BlockSpec((half, width), lambda j, m: (spot(m), 0)),
            ],
        ),
        out_shape=[
            jax.ShapeDtypeStruct((width, 3 * width), F32),
            jax.ShapeDtypeStruct((width, width), F32),
        ],
        input_output_aliases={2 + GROUPS + n: n for n in range(len(earlier))},
        compiler_params=params(),
        cost_estimate=cost(1e6, 14e6),
        name="att_place",
    )(meta, *[grads] * (GROUPS + 1), *earlier)


def swap_with(x, axis, bit=1):
    count = lax.axis_size(axis)
    return lax.ppermute(x, axis, [(i, i ^ bit) for i in range(count)])


ALL = ("chips", "core", "ulysses")


def chains():
    count = lax.axis_size("chips") * 4
    bits = [1] + [1 << n for n in range(2, count.bit_length() - 1)]
    swapped = list(bits)
    for n in range(0, len(bits) - 1, 2):
        swapped[n], swapped[n + 1] = bits[n + 1], bits[n]
    return count, bits, swapped


class Chain:
    def __init__(self, x, more, axis):
        self.x, self.more, self.axis, self.at = x, more, axis, 0
        self.count, *self.orders = chains()
        self.hops = len(self.orders[0])

    def swap(self, x, hop):
        pairs = [(i, i ^ self.orders[(i >> 1) & 1][hop]) for i in range(self.count)]
        return lax.ppermute(x, ALL, pairs)

    def bit(self, hop):
        place = lax.axis_index(ALL)
        step = jnp.where(lax.axis_index("core") == 0, self.orders[0][hop], self.orders[1][hop])
        return jnp.minimum(place & step, 1)

    def cut(self, x, which):
        half = x.shape[self.axis] // 2
        return lax.dynamic_slice_in_dim(x, which * half, half, self.axis)

    def piece(self, which):
        part = self.cut(self.x, which).astype(F32)
        return part if self.more is None else part + self.cut(self.more, which).astype(F32)

    def add(self, hop):
        self.x = (self.piece(self.bit(hop)) + self.got.astype(F32)).astype(BF16)
        self.more = None

    def join(self, hop):
        first = self.bit(hop) == 0
        low = jnp.where(first, self.x, self.got)
        high = jnp.where(first, self.got, self.x)
        self.x = jnp.concatenate([low, high], self.axis)

    @property
    def plan(self):
        wide = min(2, self.hops)
        steps = [("halve", hop) for hop in range(wide)]
        steps += [("whole", hop) for hop in range(wide, self.hops)]
        return steps + [("gather", hop) for hop in range(wide - 1, -1, -1)]

    @property
    def done(self):
        return self.at > len(self.plan)

    def prepare(self):
        plan, at = self.plan, self.at
        self.at += 1
        if at:
            kind, hop = plan[at - 1]
            if kind == "halve":
                self.add(hop)
            elif kind == "whole":
                self.x = plus(self.x, self.got)
            else:
                self.join(hop)
        if at == len(plan):
            self.out = None
            return
        kind, self.hop = plan[at]
        self.out = self.x
        if kind == "halve":
            self.out = self.piece(1 - self.bit(self.hop)).astype(BF16)

    def fire(self):
        self.got = self.swap(self.out, self.hop)


class Butterfly:
    def __init__(self, x):
        self.x, self.at = x, 0
        self.count = lax.axis_size("chips") * 4
        self.hops = self.count.bit_length() - 1

    @property
    def done(self):
        return self.at > self.hops

    def prepare(self):
        if self.at:
            self.x = self.x + self.got
        self.out = self.x if self.at < self.hops else None
        self.at += 1

    def fire(self):
        bit = 1 << (self.at - 1)
        self.got = lax.ppermute(self.out, ALL, [(i, i ^ bit) for i in range(self.count)])


def advance(values, *running):
    running = [chain for chain in running if not chain.done]
    for chain in running:
        chain.prepare()
    outs = [chain.x if chain.out is None else chain.out for chain in running]
    tied = tie(*outs, *values)
    for chain, out in zip(running, tied):
        if chain.out is None:
            chain.x = out
        else:
            if chain.out is chain.x:
                chain.x = out
            chain.out = out
            chain.fire()
    return tied[len(running) :]


def tie(*values):
    return lax.optimization_barrier(values)


def body(
    inputs_long,
    inputs_short,
    steps_long,
    steps_short,
    lengths,
    time_table,
    attngain,
    attnshift,
    qkvweight,
    querybias,
    valuebias,
    projweight,
    projbias,
    mlpgain,
    mlpshift,
    upweight,
    upbias,
    downweight,
    downbias,
    upstream_long,
    upstream_short,
):
    tokens, width = inputs_long.shape[1], inputs_long.shape[2]
    side = lax.axis_index("ulysses")
    core = lax.axis_index("core")
    meta = jnp.stack([side * tokens, side, 1 - core]).astype(jnp.int32)
    vecs, ub = pack(
        (attngain, attnshift, querybias, valuebias, projbias, mlpgain, mlpshift, downbias), upbias
    )

    edge = lax.dynamic_slice_in_dim(inputs_short[0], (1 - side) * (tokens - HALO), HALO, 0)
    across = (swap_with(inputs_long[0], "ulysses"), swap_with(edge, "ulysses"))

    q, ko, vo, start, rows, norm_s, norm_k = own_tokens(
        lengths, steps_short, steps_long, meta, inputs_long, inputs_short, time_table, vecs, qkvweight
    )
    kr, vr, norm_s, norm_k = far_tokens(lengths, meta, *across, rows, vecs, qkvweight, norm_s, norm_k)
    att, lse, bias = attend(lengths, meta, q, ko, vo, kr, vr)
    core_swap = lambda x: swap_with(x, "core")
    send, n2, seed, mid, outacc, dn2acc, att_s, att_k, ub_a = ffn_a(
        meta, att, start, upstream_long, upstream_short, vecs, ub, projweight, upweight, downweight
    )
    send, n2 = tie(send, n2)
    got = core_swap(send)
    out_long, out_short, keep, dbr, datt, sums_mlp, ub_b = ffn_b(
        meta, n2, seed, mid, outacc, dn2acc, vecs, ub, projweight, upweight, downweight
    )
    mlp = Chain(keep, got, 2)
    (datt,) = advance((datt,), mlp)

    count = width // PAIR // GROUPS
    grads, head_sums = [], []
    for n in range(GROUPS):
        d, sums = attend_back(n * count, count, q, ko, vo, kr, vr, datt, lse, bias)
        grads.append(d)
        head_sums.append(sums[0:2])
        if n:
            datt, *grads = advance((datt, *grads), mlp)
        else:
            datt, *grads = tie(datt, *grads)
    shares = lambda norm, att_half: jnp.concatenate(
        [outer(norm, d) for d in grads] + [outer(att_half, dbr)], 1
    )
    send = shares(norm_s, att_s)
    send, *grads = tie(send, *grads)
    got = core_swap(send)
    rest = Chain(shares(norm_k, att_k), got, 0)
    grads = advance(grads, rest)
    grads = advance(grads, mlp, rest)
    back = far_grad(meta, grads, qkvweight, kr.shape[0])
    (back,) = advance((back,), rest)
    back = swap_with(back, "ulysses")
    grads = advance(grads, mlp)
    in_long, in_short, sums_in = near_grad(meta, grads, qkvweight, back, start, dbr, vecs)
    small = Butterfly(
        jnp.concatenate(
            [
                sums_in[0:2],
                jnp.concatenate(head_sums, 1),
                sums_mlp[0:4],
                (ub_a + ub_b).reshape(-1, width),
            ],
            0,
        )
    )
    advance((), mlp, small)
    advance((), rest, small)
    advance((), rest, small)
    while not mlp.done:
        advance((), mlp)
    mlp_other = core_swap(mlp.x)
    held = mlp_place(meta, False, mlp.x)
    turn = 0
    while not (rest.done and small.done):
        live = not rest.done
        if turn == 1:
            held = advance(held, rest, small)
        else:
            advance((), rest, small)
        turn += 1
        if live and rest.done:
            rest_other = core_swap(rest.x)
            placed = att_place(meta, False, rest.x)
    *placed, mlp_other = tie(*placed, mlp_other)
    held = mlp_place(meta, True, mlp_other, held)
    g_down, g_up, rest_other = tie(*held, rest_other)
    g_qkv, g_proj = att_place(meta, True, rest_other, placed)
    small = small.x
    return (
        out_long,
        out_short,
        in_long,
        in_short,
        small[0],
        small[1],
        g_qkv,
        small[2],
        small[3],
        g_proj,
        small[4],
        small[5],
        small[6],
        g_up,
        small[8:].reshape(-1),
        g_down,
        small[7],
    )


def solution(mesh):
    seq, pair = mesh.shape["seq"], mesh.shape["ulysses"]
    split = jax.sharding.Mesh(mesh.devices.reshape(seq // 2, 2, pair), ("chips", "core", "ulysses"))
    rows = ("chips", "core")
    tokens = P(rows, "ulysses", None)
    placed = (tokens, tokens, P(rows), P(rows, None), P(rows, None)) + (P(),) * 14 + (tokens,) * 2
    return jax.shard_map(
        body,
        mesh=split,
        in_specs=placed,
        out_specs=(tokens,) * 4 + (P(),) * 13,
        check_vma=False,
    )
```

```python
import functools

import jax
import jax.numpy as jnp
from jax import lax
from jax.experimental import pallas as pl
from jax.experimental.pallas import tpu as pltpu
from jax.sharding import PartitionSpec as P

HEAD = 64
PAIR = 2 * HEAD
HALO = 64
EPS = 1e-05
GROUP = 16
F32 = jnp.float32
BF16 = jnp.bfloat16
VMEM_LIMIT = 56 * 1024 * 1024

NT = (((1,), (1,)), ((), ()))
NN = (((1,), (0,)), ((), ()))


def mm(left, right, dims=NN):
    return lax.dot_general(left, right, dims, preferred_element_type=F32)


def params(steps=1):
    return pltpu.CompilerParams(
        vmem_limit_bytes=VMEM_LIMIT, dimension_semantics=("arbitrary",) * steps
    )


def cost(flops, moved, scale=1):
    return pl.CostEstimate(flops=int(flops * scale), bytes_accessed=int(moved * scale), transcendentals=0)


def norm_parts(values_in):
    centre = values_in - jnp.mean(values_in, -1, keepdims=True)
    spread = jnp.mean(centre * centre, -1, keepdims=True)
    scale = lax.rsqrt(spread + EPS)
    return centre * scale, scale


def bounds_rows(lengths_s, segs, width):
    lane = lax.broadcasted_iota(jnp.int32, (1, width), 1)
    low = jnp.zeros((1, width), jnp.int32)
    high = jnp.zeros((1, width), jnp.int32)
    at = jnp.int32(0)
    for k in range(segs):
        low = jnp.where(lane == k, at, low)
        at = at + lengths_s[0, k]
        high = jnp.where(lane == k, at, high)
    return lane, low, high


def pack_kernel(*refs):
    vecs, ub = refs[-2:]
    for n, ref in enumerate(refs[:-3]):
        vecs[n : n + 1, :] = ref[...].astype(F32).reshape(1, -1)
    ub[...] = refs[-3][...].astype(F32).reshape(1, -1)


def pack(vectors, wide):
    width = vectors[0].shape[0]
    return pl.pallas_call(
        pack_kernel,
        out_shape=[
            jax.ShapeDtypeStruct((len(vectors), width), F32),
            jax.ShapeDtypeStruct((1, wide.shape[0]), F32),
        ],
        cost_estimate=cost(1e6, 1e5),
        name="pack",
    )(*vectors, wide)


def own_kernel(
    lengths_s, steps_short_s, steps_long_s, meta_s,
    xl, xs, table, vecs, w,
    q_o, k_o, v_o, st_o, rows_o, ns_o, nk_o,
    buf, sem,
):
    b = pl.program_id(0)
    segs = lengths_s.shape[1]
    tokens, width = xl.shape[1], xl.shape[2]

    @pl.when(b == 0)
    def _():
        copies = []
        target = jnp.zeros((32, buf.shape[0]), jnp.int32) - 1
        sub = lax.broadcasted_iota(jnp.int32, (32, buf.shape[0]), 0)
        for k in range(segs + 1):
            step = steps_short_s[0, k] if k < segs else steps_long_s[0]
            base = pl.multiple_of((step // GROUP) * GROUP, GROUP)
            copy = pltpu.make_async_copy(
                table.at[pl.ds(base, GROUP), :], buf.at[pl.ds(k * GROUP, GROUP), :], sem.at[k]
            )
            copy.start()
            copies.append(copy)
            target = jnp.where(sub == k, k * GROUP + step - base, target)
        rest = buf.shape[0] - (segs + 1) * GROUP
        if rest:
            buf[pl.ds((segs + 1) * GROUP, rest), :] = jnp.zeros((rest, width), BF16)
        for copy in copies:
            copy.wait()
        lane = lax.broadcasted_iota(jnp.int32, (32, buf.shape[0]), 1)
        pick = jnp.where(lane == target, 1.0, 0.0).astype(BF16)
        rows_o[...] = mm(pick, buf[...]).astype(BF16)

    lane, low, high = bounds_rows(lengths_s, segs, 32)
    whole = lane == segs
    low = jnp.where(b == 0, 0, low)
    high = jnp.where(b == 0, jnp.where(whole, 1 << 30, 0), high)
    place = meta_s[0] + lax.broadcasted_iota(jnp.int32, (tokens, 1), 0)
    pick = jnp.where((place >= low) & (place < high), 1.0, 0.0).astype(BF16)
    embed = mm(pick, rows_o[...])
    start = jnp.where(b == 0, xl[0], xs[0]).astype(F32) + embed
    st_o[0] = start
    unit, _ = norm_parts(start)
    normed = (unit * vecs[0:1, :] + vecs[1:2, :]).astype(BF16)
    left, right = normed[:, : width // 2], normed[:, width // 2 :]
    ns_o[...] = jnp.where(meta_s[2] == 1, right, left)
    nk_o[...] = jnp.where(meta_s[2] == 1, left, right)
    q_o[0] = ((mm(normed, w[:, :width]) + vecs[2:3, :]) * HEAD ** (-0.5)).astype(BF16)
    k_o[0] = mm(normed, w[:, width : 2 * width]).astype(BF16)
    v_o[0] = (mm(normed, w[:, 2 * width :]) + vecs[3:4, :]).astype(BF16)


def own_tokens(lengths, steps_short, steps_long, meta, xl, xs, table, vecs, w):
    tokens, width = xl.shape[1], xl.shape[2]
    segs = lengths.shape[1]
    spots = -(-(segs + 1) * GROUP // 128) * 128
    whole = lambda *shape: pl.BlockSpec(shape, lambda b, *_: (0,) * len(shape))
    part = pl.BlockSpec((1, tokens, width), lambda b, *_: (b, 0, 0))
    half = pl.BlockSpec((tokens, width // 2), lambda b, *_: (b, 0))
    stacked = jax.ShapeDtypeStruct((2, tokens, width), BF16)
    return pl.pallas_call(
        own_kernel,
        grid_spec=pltpu.PrefetchScalarGridSpec(
            num_scalar_prefetch=4,
            grid=(2,),
            in_specs=[
                whole(1, tokens, width),
                whole(1, tokens, width),
                pl.BlockSpec(memory_space=pl.ANY),
                whole(*vecs.shape),
                whole(*w.shape),
            ],
            out_specs=[part] * 4 + [whole(32, width)] + [half, half],
            scratch_shapes=[pltpu.VMEM((spots, width), BF16), pltpu.SemaphoreType.DMA((segs + 1,))],
        ),
        out_shape=[stacked] * 3
        + [jax.ShapeDtypeStruct((2, tokens, width), F32), jax.ShapeDtypeStruct((32, width), BF16)]
        + [jax.ShapeDtypeStruct((3 * tokens + 2 * HALO, width // 2), BF16)] * 2,
        compiler_params=params(),
        cost_estimate=cost(4 * tokens * width * 3 * width, 14e6),
        name="own_tokens",
    )(lengths, steps_short, steps_long, meta, xl, xs, table, vecs, w)


def far_kernel(
    lengths_s, meta_s, xr, xe, rows, vecs, wk, wv, ns_i, nk_i, k_o, v_o, ns_o, nk_o, ns, nk, sem
):
    segs = lengths_s.shape[1]
    total, width = k_o.shape
    tokens = total - 2 * HALO
    side = meta_s[1]
    edge = xe[...].astype(F32)
    before = jnp.where(side == 1, edge, 0.0)
    after = jnp.where(side == 0, edge, 0.0)
    x = jnp.concatenate([xr[...].astype(F32), before, after], axis=0)
    lane, low, high = bounds_rows(lengths_s, segs, 32)
    row = lax.broadcasted_iota(jnp.int32, (total, 1), 0)
    place = meta_s[0] + row - HALO - jnp.where(row < tokens + HALO, tokens, 0)
    inside = (place >= low) & (place < high)
    story = jnp.where(lane == segs, 1.0, 0.0)
    pick = jnp.where(row < tokens, story, jnp.where(inside, 1.0, 0.0)).astype(BF16)
    start = x + mm(pick, rows[...])
    unit, _ = norm_parts(start)
    normed = (unit * vecs[0:1, :] + vecs[1:2, :]).astype(BF16)
    left, right = normed[:, : width // 2], normed[:, width // 2 :]
    ns[...] = jnp.where(meta_s[2] == 1, right, left)
    nk[...] = jnp.where(meta_s[2] == 1, left, right)
    rest = pl.ds(2 * tokens, total)
    copy_s = pltpu.make_async_copy(ns, ns_o.at[rest, :], sem.at[0])
    copy_k = pltpu.make_async_copy(nk, nk_o.at[rest, :], sem.at[1])
    copy_s.start()
    copy_k.start()
    k_o[...] = mm(normed, wk[...]).astype(BF16)
    v_o[...] = (mm(normed, wv[...]) + vecs[3:4, :]).astype(BF16)
    copy_s.wait()
    copy_k.wait()


def far_tokens(lengths, meta, xr, xe, rows, vecs, w, ns, nk):
    width = xr.shape[1]
    total = xr.shape[0] + 2 * HALO
    whole = lambda *shape: pl.BlockSpec(shape, lambda i, *_: (0,) * len(shape))
    out = jax.ShapeDtypeStruct((total, width), BF16)
    return pl.pallas_call(
        far_kernel,
        grid_spec=pltpu.PrefetchScalarGridSpec(
            num_scalar_prefetch=2,
            grid=(1,),
            in_specs=[
                whole(*xr.shape),
                whole(*xe.shape),
                whole(*rows.shape),
                whole(*vecs.shape),
                pl.BlockSpec((width, width), lambda i, *_: (0, 1)),
                pl.BlockSpec((width, width), lambda i, *_: (0, 2)),
                pl.BlockSpec(memory_space=pl.ANY),
                pl.BlockSpec(memory_space=pl.ANY),
            ],
            out_specs=[whole(total, width)] * 2 + [pl.BlockSpec(memory_space=pl.ANY)] * 2,
            scratch_shapes=[pltpu.VMEM((total, width // 2), BF16)] * 2
            + [pltpu.SemaphoreType.DMA((2,))],
        ),
        out_shape=[out] * 2 + [jax.ShapeDtypeStruct(ns.shape, BF16)] * 2,
        input_output_aliases={8: 2, 9: 3},
        compiler_params=params(),
        cost_estimate=cost(2 * total * width * 2 * width, 6e6),
        name="far_tokens",
    )(lengths, meta, xr, xe, rows, vecs, w, w, ns, nk)


def seg_of(lengths_s, place):
    segs = lengths_s.shape[1]
    at = jnp.int32(0)
    seg = jnp.zeros(place.shape, jnp.int32)
    for k in range(segs - 1):
        at = at + lengths_s[0, k]
        seg = seg + jnp.where(place >= at, 1, 0)
    at = at + lengths_s[0, segs - 1]
    return jnp.where(place < 0, -1, jnp.where(place >= at, -2, seg))


def halves():
    lane = lax.broadcasted_iota(jnp.int32, (1, PAIR), 1)
    return (lane < HEAD, lane >= HEAD)


def attend_kernel(lengths_s, meta_s, q, ko, vo, kr, vr, o, lse, bias_t, bias, kx, vx):
    tokens = q.shape[1]
    blocks = tokens // 128
    span = 128 + 2 * HALO

    @pl.when(pl.program_id(0) == 0)
    def _():
        seg_q = seg_of(lengths_s, meta_s[0] + lax.broadcasted_iota(jnp.int32, (tokens, 1), 0))
        seg_k = seg_of(
            lengths_s, meta_s[0] - HALO + lax.broadcasted_iota(jnp.int32, (1, tokens + 2 * HALO), 1)
        )
        for i in range(blocks):
            same = seg_q[i * 128 : (i + 1) * 128, :] == seg_k[:, i * 128 : i * 128 + span]
            bias[i] = jnp.where(same, 0.0, -1e30)
            bias_t[i] = bias[i].T

    for ext, own, far in ((kx, ko, kr), (vx, vo, vr)):
        ext[0:HALO, :] = far[tokens : tokens + HALO, :]
        ext[HALO : HALO + tokens, :] = own[1]
        ext[HALO + tokens :, :] = far[tokens + HALO :, :]

    lane = lax.broadcasted_iota(jnp.int32, (1, PAIR), 1)
    stats = jnp.zeros((tokens, 128), F32)
    step = tokens
    for h, half in enumerate(halves()):
        logs = []
        for i in range(tokens // step):
            rows = pl.ds(i * step, step)
            qh = jnp.where(half, q[0, rows, :], 0)
            s1 = mm(qh, ko[0], NT)
            s2 = mm(qh, kr[:tokens, :], NT)
            top = jnp.maximum(jnp.max(s1, -1, keepdims=True), jnp.max(s2, -1, keepdims=True))
            e1 = jnp.exp(s1 - top)
            e2 = jnp.exp(s2 - top)
            total = jnp.sum(e1, -1, keepdims=True) + jnp.sum(e2, -1, keepdims=True)
            r = mm(e1.astype(BF16), vo[0]) + mm(e2.astype(BF16), vr[:tokens, :])
            r = (r / total).astype(BF16)
            o[0, rows, :] = r if h == 0 else jnp.where(half, r, o[0, rows, :])
            logs.append(top + jnp.log(total))
        stats = jnp.where(lane == h, jnp.concatenate(logs, 0), stats)
        logs = []
        for i in range(blocks):
            rows = pl.ds(i * 128, 128)
            keys = pl.ds(i * 128, span)
            qh = jnp.where(half, q[1, rows, :], 0)
            s1 = mm(qh, kx[keys, :], NT) + bias[i]
            top = jnp.max(s1, -1, keepdims=True)
            e1 = jnp.exp(s1 - top)
            total = jnp.sum(e1, -1, keepdims=True)
            r = (mm(e1.astype(BF16), vx[keys, :]) / total).astype(BF16)
            o[1, rows, :] = r if h == 0 else jnp.where(half, r, o[1, rows, :])
            logs.append(top + jnp.log(total))
        stats = jnp.where(lane == 2 + h, jnp.concatenate(logs, 0), stats)
    lse[0] = stats.T[0:8, :]


def head_specs(tokens):
    own = pl.BlockSpec((2, tokens, PAIR), lambda i, *_: (0, 0, i))
    far = pl.BlockSpec((tokens + 2 * HALO, PAIR), lambda i, *_: (0, i))
    row = pl.BlockSpec((1, 8, tokens), lambda i, *_: (i, 0, 0))
    return own, far, row


def attend(lengths, meta, q, ko, vo, kr, vr):
    tokens, width = q.shape[1], q.shape[2]
    pairs = width // PAIR
    own, far, row = head_specs(tokens)
    ext = pltpu.VMEM((tokens + 2 * HALO, PAIR), BF16)
    return pl.pallas_call(
        attend_kernel,
        grid_spec=pltpu.PrefetchScalarGridSpec(
            num_scalar_prefetch=2,
            grid=(pairs,),
            in_specs=[own, own, own, far, far],
            out_specs=[
                own, row, pl.BlockSpec((tokens // 128, 128 + 2 * HALO, 128), lambda i, *_: (0, 0, 0)),
            ],
            scratch_shapes=[pltpu.VMEM((tokens // 128, 128, 128 + 2 * HALO), F32), ext, ext],
        ),
        out_shape=[
            jax.ShapeDtypeStruct(q.shape, BF16),
            jax.ShapeDtypeStruct((pairs, 8, tokens), F32),
            jax.ShapeDtypeStruct((tokens // 128, 128 + 2 * HALO, 128), F32),
        ],
        compiler_params=params(),
        cost_estimate=cost(4 * tokens * 2.5 * tokens * 256 * 2 * pairs, 8e6),
        name="attend",
    )(lengths, meta, q, ko, vo, kr, vr)


def attend_back_kernel(
    q, ko, vo, kr, vr, go, lse, bias, grad, sums, kx, vx, kt, dkx, dvx, dqt
):
    tokens = q.shape[1]
    far_at = 2 * tokens
    third = grad.shape[1] // 3
    at = [
        pl.ds(pl.multiple_of(n * third + pl.program_id(0) * PAIR, PAIR), PAIR) for n in range(3)
    ]
    grad[far_at:, at[0]] = jnp.zeros((grad.shape[0] - far_at, PAIR), BF16)
    blocks = tokens // 128
    span = 128 + 2 * HALO

    for ext, own, far in ((kx, ko, kr), (vx, vo, vr)):
        ext[0:HALO, :] = far[tokens : tokens + HALO, :]
        ext[HALO : HALO + tokens, :] = own[1]
        ext[HALO + tokens :, :] = far[tokens + HALO :, :]

    shift = HEAD ** (-0.5)
    sum_q = jnp.zeros((1, PAIR), F32)
    sum_v = jnp.zeros((1, PAIR), F32)

    k_parts = (ko[0], kr[:tokens, :])
    v_parts = (vo[0], vr[:tokens, :])
    for n in range(2):
        kt[n, :, :tokens] = k_parts[n].T
    dk_sums = [jnp.zeros((tokens, PAIR), F32)] * 2
    dv_sums = [jnp.zeros((tokens, PAIR), F32)] * 2
    for h, half in enumerate(halves()):
        rows = pl.ds(h * HEAD, HEAD)
        qh = jnp.where(half, q[0], 0)
        gh = jnp.where(half, go[0], 0)
        log = lse[0, h : h + 1, :]
        pts = [jnp.exp(mm(k_parts[n], qh, NT) - log) for n in range(2)]
        dpts = [mm(v_parts[n], gh, NT) for n in range(2)]
        delta = jnp.sum(pts[0] * dpts[0], 0, keepdims=True)
        delta += jnp.sum(pts[1] * dpts[1], 0, keepdims=True)
        part = None
        for n in range(2):
            dst = (pts[n] * (dpts[n] - delta)).astype(BF16)
            dv_sums[n] = dv_sums[n] + mm(pts[n].astype(BF16), gh)
            dk_sums[n] = dk_sums[n] + mm(dst, qh)
            turned = mm(kt[n, rows, :tokens], dst)
            part = turned if n == 0 else part + turned
        dqt[rows, :] = part
    for n, row in enumerate((0, far_at)):
        grad[row : row + tokens, at[1]] = dk_sums[n].astype(BF16)
        grad[row : row + tokens, at[2]] = dv_sums[n].astype(BF16)
    for n in range(2):
        sum_v += jnp.sum(dv_sums[n], 0, keepdims=True)
    out = dqt[...].T * shift
    grad[:tokens, at[0]] = out.astype(BF16)
    sum_q += jnp.sum(out, 0, keepdims=True)

    kt[0] = kx[...].T
    dkx[...] = jnp.zeros_like(dkx)
    dvx[...] = jnp.zeros_like(dvx)
    for i in range(blocks):
        cols = slice(i * 128, (i + 1) * 128)
        keys = slice(i * 128, i * 128 + span)
        dk_sum = jnp.zeros((span, PAIR), F32)
        dv_sum = jnp.zeros((span, PAIR), F32)
        for h, half in enumerate(halves()):
            rows = slice(h * HEAD, (h + 1) * HEAD)
            qh = jnp.where(half, q[1, cols, :], 0)
            gh = jnp.where(half, go[1, cols, :], 0)
            st = mm(kx[keys, :], qh, NT) + bias[i]
            pt = jnp.exp(st - lse[0, 2 + h : 3 + h, cols])
            dpt = mm(vx[keys, :], gh, NT)
            delta = jnp.sum(pt * dpt, 0, keepdims=True)
            dst = (pt * (dpt - delta)).astype(BF16)
            dv_sum += mm(pt.astype(BF16), gh)
            dk_sum += mm(dst, qh)
            dqt[rows, cols] = mm(kt[0, rows, keys], dst)
        dkx[keys, :] += dk_sum
        dvx[keys, :] += dv_sum
    out = dqt[...].T * shift
    grad[tokens:far_at, at[0]] = out.astype(BF16)
    sum_q += jnp.sum(out, 0, keepdims=True)
    sum_v += jnp.sum(dvx[...], 0, keepdims=True)
    edge = far_at + tokens
    for ext, cols in ((dkx, at[1]), (dvx, at[2])):
        grad[tokens:far_at, cols] = ext[HALO : HALO + tokens, :].astype(BF16)
        grad[edge : edge + HALO, cols] = ext[0:HALO, :].astype(BF16)
        grad[edge + HALO :, cols] = ext[HALO + tokens :, :].astype(BF16)
    sums[...] = jnp.concatenate([sum_q, sum_v, jnp.zeros((6, PAIR), F32)], 0)


def attend_back(first, count, q, ko, vo, kr, vr, go, lse, bias):
    tokens, width = q.shape[1], q.shape[2]
    wide = tokens + 2 * HALO
    own = pl.BlockSpec((2, tokens, PAIR), lambda i: (0, 0, i + first))
    far = pl.BlockSpec((wide, PAIR), lambda i: (0, i + first))
    row = pl.BlockSpec((1, 8, tokens), lambda i: (i + first, 0, 0))
    ext = pltpu.VMEM((wide, PAIR), BF16)
    ext32 = pltpu.VMEM((wide, PAIR), F32)
    rows, cols = 2 * tokens + wide, 3 * count * PAIR
    return pl.pallas_call(
        attend_back_kernel,
        grid=(count,),
        in_specs=[own, own, own, far, far, own, row]
        + [pl.BlockSpec(bias.shape, lambda i: (0, 0, 0))],
        out_specs=[
            pl.BlockSpec((rows, cols), lambda i: (0, 0)),
            pl.BlockSpec((8, PAIR), lambda i: (0, i)),
        ],
        scratch_shapes=[
            ext,
            ext,
            pltpu.VMEM((2, PAIR, wide), BF16),
            ext32,
            ext32,
            pltpu.VMEM((PAIR, tokens), F32),
        ],
        out_shape=[
            jax.ShapeDtypeStruct((rows, cols), BF16),
            jax.ShapeDtypeStruct((8, count * PAIR), F32),
        ],
        compiler_params=params(),
        cost_estimate=cost(10 * tokens * 2.5 * tokens * 256 * 2 * count, 2e6 * count),
        name="attend_back",
    )(q, ko, vo, kr, vr, go, lse, bias)


def chunk_spot(c, part, meta_s):
    return 2 * jnp.where(part == 0, meta_s[2], 1 - meta_s[2]) + c


def ffn_chunk(spot, first, n2, seed, ub, wu, wd, act, dh, sums_ub):
    chunk = wu.shape[1]
    k0 = 0.7978845608028654
    piece = 256

    @pl.when(first)
    def _():
        sums_ub[...] = jnp.zeros_like(sums_ub)

    for j in range(chunk // piece):
        cols = slice(j * piece, (j + 1) * piece)
        hid = mm(n2, wu[:, cols]) + ub[0:1, cols]
        square = hid * hid
        t = jnp.tanh(hid * (k0 + k0 * 0.044715 * square))
        half = 0.5 + 0.5 * t
        act[:, cols] = (hid * half).astype(BF16)
        slope = half + (hid * (0.5 - 0.5 * (t * t))) * (k0 + 3 * k0 * 0.044715 * square)
        dh32 = mm(seed, wd[cols, :], NT) * slope
        dh[:, cols] = dh32.astype(BF16)
        at = pl.ds(pl.multiple_of(spot * chunk + j * piece, piece), piece)
        sums_ub[0:1, at] += jnp.sum(dh32, 0, keepdims=True)


def ffn_a_kernel(
    meta_s, att, st, ul, us, vecs, ub, wp, wu, wd,
    g_o, n2_o, seed_o, mid_o, out_o, dn2_o, as_o, ak_o, sums_ub,
    n2, seed, n2t, seedt, outacc, dn2acc, act, dh,
):
    c, b = pl.program_id(0), pl.program_id(1)
    half = wp.shape[0] // 2
    tokens = mid_o.shape[1]
    rows = pl.ds(pl.multiple_of(b * tokens, tokens), tokens)

    @pl.when(c == 0)
    def _():
        up = jnp.where(b == 0, ul[0], us[0])
        seed[rows, :] = up
        seed_o[0] = up
        seedt[:, rows] = up.T
        whole = att[0]
        as_o[...] = jnp.where(meta_s[2] == 1, whole[:, half:], whole[:, :half])
        ak_o[...] = jnp.where(meta_s[2] == 1, whole[:, :half], whole[:, half:])
        middle = st[0] + mm(whole, wp[...]) + vecs[4:5, :]
        mid_o[0] = middle
        unit, _ = norm_parts(middle)
        normed = (unit * vecs[5:6, :] + vecs[6:7, :]).astype(BF16)
        n2[rows, :] = normed
        n2_o[0] = normed
        n2t[:, rows] = normed.T

    spot = chunk_spot(c, 0, meta_s)
    act_b, dh_b = act.at[rows, :], dh.at[rows, :]
    ffn_chunk(spot, (b == 0) & (c == 0), n2[rows, :], seed[rows, :], ub, wu, wd, act_b, dh_b, sums_ub)
    out = mm(act_b[...], wd[...])
    dn2 = mm(dh_b[...], wu[...], NT)

    @pl.when(c == 0)
    def _():
        outacc[rows, :] = mid_o[0] + vecs[7:8, :] + out
        dn2acc[rows, :] = dn2

    @pl.when(c == 1)
    def _():
        out_o[0] = outacc[rows, :] + out
        dn2_o[0] = dn2acc[rows, :] + dn2

    @pl.when(b == 1)
    def _():
        g_o[0, 0] = mm(seedt[...], act[...]).astype(BF16)
        g_o[0, 1] = mm(n2t[...], dh[...]).astype(BF16)


def ffn_b_kernel(
    meta_s, n2, seed, mid, out_i, dn2_i, vecs, ub, wp, wu, wd,
    out_l, out_s, g_o, dbr_o, datt_o, sums, sums_ub,
    n2t, seedt, outacc, dn2acc, act, dh,
):
    c, b = pl.program_id(0), pl.program_id(1)
    tokens = mid.shape[1]
    rows = pl.ds(pl.multiple_of(b * tokens, tokens), tokens)

    @pl.when(c == 0)
    def _():
        seedt[:, rows] = seed[b].T
        n2t[:, rows] = n2[b].T

    spot = chunk_spot(c, 1, meta_s)
    act_b, dh_b = act.at[rows, :], dh.at[rows, :]
    ffn_chunk(spot, (b == 0) & (c == 0), n2[b], seed[b], ub, wu, wd, act_b, dh_b, sums_ub)
    out = mm(act_b[...], wd[...])
    dn2 = mm(dh_b[...], wu[...], NT)

    @pl.when(c == 0)
    def _():
        outacc[rows, :] = out_i[0] + out
        dn2acc[rows, :] = dn2_i[0] + dn2

    @pl.when(c == 1)
    def _():
        result = (outacc[rows, :] + out).astype(BF16)

        @pl.when(b == 0)
        def _():
            out_l[0] = result
            sums[...] = jnp.zeros_like(sums)

        @pl.when(b > 0)
        def _():
            out_s[0] = result

        unit, scale = norm_parts(mid[0])
        whole = dn2acc[rows, :] + dn2
        seed32 = seed[b].astype(F32)
        du = whole * vecs[5:6, :]
        back = du - jnp.mean(du, -1, keepdims=True) - unit * jnp.mean(du * unit, -1, keepdims=True)
        dmid = back * scale + seed32
        dbr = dmid.astype(BF16)
        dbr_o[0] = dbr
        datt_o[0] = mm(dbr, wp[...], NT).astype(BF16)
        sums[0:1, :] += jnp.sum(dmid, 0, keepdims=True)
        sums[1:2, :] += jnp.sum(whole * unit, 0, keepdims=True)
        sums[2:3, :] += jnp.sum(whole, 0, keepdims=True)
        sums[3:4, :] += jnp.sum(seed32, 0, keepdims=True)

    @pl.when(b == 1)
    def _():
        g_o[0, 0] = mm(seedt[...], act[...]).astype(BF16)
        g_o[0, 1] = mm(n2t[...], dh[...]).astype(BF16)


def ffn_specs(tokens, width, part):
    whole = lambda *shape: pl.BlockSpec(shape, lambda c, b, m: (0,) * len(shape))
    early = pl.BlockSpec((1, tokens, width), lambda c, b, m: (jnp.where(c == 0, b, 1), 0, 0))
    late = pl.BlockSpec((1, tokens, width), lambda c, b, m: (jnp.where(c == 0, 0, b), 0, 0))
    grads = pl.BlockSpec((1, 2, width, width), lambda c, b, m: (c, 0, 0, 0))
    weights = [
        pl.BlockSpec((1, width), lambda c, b, m: (0, chunk_spot(c, part, m))),
        whole(width, width),
        pl.BlockSpec((width, width), lambda c, b, m: (0, chunk_spot(c, part, m))),
        pl.BlockSpec((width, width), lambda c, b, m: (chunk_spot(c, part, m), 0)),
    ]
    shape = lambda kind: jax.ShapeDtypeStruct((2, tokens, width), kind)
    low, high = pltpu.VMEM((2 * tokens, width), BF16), pltpu.VMEM((2 * tokens, width), F32)
    turned = pltpu.VMEM((width, 2 * tokens), BF16)
    return whole, early, late, grads, weights, shape, low, high, turned


def ffn_a(meta, att, st, ul, us, vecs, ub, wp, wu, wd):
    tokens, width = ul.shape[1], ul.shape[2]
    hidden = wu.shape[1]
    whole, early, late, grads, weights, shape, low, high, turned = ffn_specs(tokens, width, 0)
    single = whole(1, tokens, width)
    half = pl.BlockSpec((tokens, width // 2), lambda c, b, m: (jnp.where(c == 0, b, 1), 0))
    return pl.pallas_call(
        ffn_a_kernel,
        grid_spec=pltpu.PrefetchScalarGridSpec(
            num_scalar_prefetch=1,
            grid=(2, 2),
            in_specs=[early, early, single, single, whole(*vecs.shape)] + weights,
            out_specs=[grads, early, early, early, late, late, half, half, whole(1, hidden)],
            scratch_shapes=[low, low, turned, turned, high, high, low, low],
        ),
        out_shape=[jax.ShapeDtypeStruct((2, 2, width, width), BF16)]
        + [shape(BF16)] * 2
        + [shape(F32)] * 3
        + [jax.ShapeDtypeStruct((2 * tokens, width // 2), BF16)] * 2
        + [jax.ShapeDtypeStruct((1, hidden), F32)],
        compiler_params=params(2),
        cost_estimate=cost(4 * tokens * width * (width + 3 * hidden), 40e6),
        name="ffn_a",
    )(meta, att, st, ul, us, vecs, ub, wp, wu, wd)


def ffn_b(meta, n2, seed, mid, outacc, dn2acc, vecs, ub, wp, wu, wd):
    tokens, width = mid.shape[1], mid.shape[2]
    hidden = wu.shape[1]
    whole, early, late, grads, weights, shape, low, high, turned = ffn_specs(tokens, width, 1)
    single = jax.ShapeDtypeStruct((1, tokens, width), BF16)
    both = whole(2, tokens, width)
    return pl.pallas_call(
        ffn_b_kernel,
        grid_spec=pltpu.PrefetchScalarGridSpec(
            num_scalar_prefetch=1,
            grid=(2, 2),
            in_specs=[both, both, late, early, early, whole(*vecs.shape)] + weights,
            out_specs=[whole(1, tokens, width)] * 2
            + [grads, late, late, whole(8, width), whole(1, hidden)],
            scratch_shapes=[turned, turned, high, high, low, low],
        ),
        out_shape=[single, single, jax.ShapeDtypeStruct((2, 2, width, width), BF16)]
        + [shape(BF16)] * 2
        + [jax.ShapeDtypeStruct((8, width), F32), jax.ShapeDtypeStruct((1, hidden), F32)],
        compiler_params=params(2),
        cost_estimate=cost(4 * tokens * width * (width + 3 * hidden), 40e6),
        name="ffn_b",
    )(meta, n2, seed, mid, outacc, dn2acc, vecs, ub, wp, wu, wd)


def back_through(grads, w):
    width = w.shape[0]
    total, first = None, 0
    for grad in grads:
        cols = grad.shape[1] // 3
        for n in range(3):
            piece = grad[:, n * cols : (n + 1) * cols]
            part = mm(piece, w[:, n * width + first : n * width + first + cols], NT)
            total = part if total is None else total + part
        first += cols
    return total


def far_grad_kernel(meta_s, *refs):
    count = (len(refs) - 3) // 2
    sources, w, d_o, held, sem = refs[:count], refs[count], refs[count + 1], refs[count + 2 : -1], refs[-1]
    total = held[0].shape[0]
    tokens = total - 2 * HALO
    copies = []
    for n, (source, target) in enumerate(zip(sources, held)):
        copy = pltpu.make_async_copy(source.at[pl.ds(2 * tokens, total), :], target, sem.at[n])
        copy.start()
        copies.append(copy)
    for copy in copies:
        copy.wait()
    full = back_through(held, w)
    d_o[0:tokens, :] = full[0:tokens, :].astype(BF16)
    before = full[tokens : tokens + HALO, :]
    after = full[tokens + HALO :, :]
    d_o[tokens:, :] = jnp.where(meta_s[1] == 1, before, after).astype(BF16)


def far_grad(meta, grads, w, total):
    width = w.shape[0]
    whole = lambda *shape: pl.BlockSpec(shape, lambda i, *_: (0,) * len(shape))
    return pl.pallas_call(
        far_grad_kernel,
        grid_spec=pltpu.PrefetchScalarGridSpec(
            num_scalar_prefetch=1,
            grid=(1,),
            in_specs=[pl.BlockSpec(memory_space=pl.ANY)] * len(grads) + [whole(*w.shape)],
            out_specs=whole(total - HALO, width),
            scratch_shapes=[pltpu.VMEM((total, d.shape[1]), BF16) for d in grads]
            + [pltpu.SemaphoreType.DMA((len(grads),))],
        ),
        out_shape=jax.ShapeDtypeStruct((total - HALO, width), BF16),
        compiler_params=params(),
        cost_estimate=cost(4 * total * width * width, 5e6),
        name="far_grad",
    )(meta, *grads, w)


def near_grad_kernel(meta_s, *refs):
    grads, (w, got, st, dbr, vecs, in_l, in_s, sums, acc) = refs[:-9], refs[-9:]
    b = pl.program_id(0)
    tokens = st.shape[1]
    acc[...] = back_through(grads, w)

    @pl.when(b == 0)
    def _():
        acc[...] += got[0:tokens, :].astype(F32)
        sums[...] = jnp.zeros_like(sums)

    @pl.when(b > 0)
    def _():
        edge = got[tokens:, :].astype(F32)
        acc[0:HALO, :] += jnp.where(meta_s[1] == 1, edge, 0.0)
        acc[tokens - HALO :, :] += jnp.where(meta_s[1] == 0, edge, 0.0)

    dn = acc[...]
    unit, scale = norm_parts(st[0])
    du = dn * vecs[0:1, :]
    back = du - jnp.mean(du, -1, keepdims=True) - unit * jnp.mean(du * unit, -1, keepdims=True)
    result = (back * scale + dbr[0].astype(F32)).astype(BF16)

    @pl.when(b == 0)
    def _():
        in_l[0] = result

    @pl.when(b > 0)
    def _():
        in_s[0] = result

    sums[0:1, :] += jnp.sum(dn * unit, 0, keepdims=True)
    sums[1:2, :] += jnp.sum(dn, 0, keepdims=True)


def near_grad(meta, grads, w, got, st, dbr, vecs):
    tokens, width = st.shape[1], st.shape[2]
    whole = lambda *shape: pl.BlockSpec(shape, lambda b, *_: (0,) * len(shape))
    part = pl.BlockSpec((1, tokens, width), lambda b, *_: (b, 0, 0))
    rows = lambda d: pl.BlockSpec((tokens, d.shape[1]), lambda b, *_: (b, 0))
    single = jax.ShapeDtypeStruct((1, tokens, width), BF16)
    return pl.pallas_call(
        near_grad_kernel,
        grid_spec=pltpu.PrefetchScalarGridSpec(
            num_scalar_prefetch=1,
            grid=(2,),
            in_specs=[
                *map(rows, grads), whole(*w.shape), whole(*got.shape), part, part, whole(*vecs.shape),
            ],
            out_specs=[whole(1, tokens, width), whole(1, tokens, width), whole(8, width)],
            scratch_shapes=[pltpu.VMEM((tokens, width), F32)],
        ),
        out_shape=[single, single, jax.ShapeDtypeStruct((8, width), F32)],
        compiler_params=params(),
        cost_estimate=cost(4 * tokens * width * 3 * width, 15e6),
        name="near_grad",
    )(meta, *grads, w, got, st, dbr, vecs)


def outer(left, right):
    rows = lambda x: x.reshape(-1, x.shape[-1])
    full = jnp.einsum("ni,nj->ij", rows(left), rows(right), preferred_element_type=F32)
    return full.astype(BF16)


def plus(x, y):
    return (x.astype(F32) + y.astype(F32)).astype(BF16)


PLACE = 384


def mlp_place_kernel(meta_s, turned, value, *rest):
    down, up = rest[-2:]
    down[...] = turned[0, 0].T.astype(F32)
    up[...] = value[0, 0].astype(F32)


def mlp_place(meta, theirs, grads, earlier=()):
    width = grads.shape[2]
    per = width // PLACE
    spot = lambda h, m: 2 * (m[2] if theirs else 1 - m[2]) + h
    return pl.pallas_call(
        mlp_place_kernel,
        grid_spec=pltpu.PrefetchScalarGridSpec(
            num_scalar_prefetch=1,
            grid=(2, per),
            in_specs=[
                pl.BlockSpec((1, 1, width, PLACE), lambda h, r, m: (h, 0, 0, r)),
                pl.BlockSpec((1, 1, PLACE, width), lambda h, r, m: (h, 1, r, 0)),
            ]
            + [pl.BlockSpec(memory_space=pl.ANY)] * len(earlier),
            out_specs=[
                pl.BlockSpec((PLACE, width), lambda h, r, m: (spot(h, m) * per + r, 0)),
                pl.BlockSpec((PLACE, width), lambda h, r, m: (r, spot(h, m))),
            ],
        ),
        out_shape=[
            jax.ShapeDtypeStruct((4 * width, width), F32),
            jax.ShapeDtypeStruct((width, 4 * width), F32),
        ],
        input_output_aliases={3 + n: n for n in range(len(earlier))},
        compiler_params=params(2),
        cost_estimate=cost(1e6, 14e6),
        name="mlp_place",
    )(meta, grads, grads, *earlier)


GROUPS = 3


def att_place_kernel(meta_s, *refs):
    parts, last, (qkv, proj) = refs[:GROUPS], refs[GROUPS], refs[-2:]
    cols = parts[0].shape[1]

    @pl.when(pl.program_id(0) < 3)
    def _():
        for n, part in enumerate(parts):
            qkv[:, n * cols : (n + 1) * cols] = part[...].astype(F32)

    @pl.when(pl.program_id(0) == 3)
    def _():
        proj[...] = last[...].astype(F32)


def att_place(meta, theirs, grads, earlier=()):
    half, width = grads.shape[0], 2 * grads.shape[0]
    spot = lambda m: m[2] if theirs else 1 - m[2]
    group = lambda n: pl.BlockSpec(
        (half, width // GROUPS), lambda j, m: (0, 3 * n + jnp.minimum(j, 2))
    )
    return pl.pallas_call(
        att_place_kernel,
        grid_spec=pltpu.PrefetchScalarGridSpec(
            num_scalar_prefetch=1,
            grid=(4,),
            in_specs=[group(n) for n in range(GROUPS)]
            + [pl.BlockSpec((half, width), lambda j, m: (0, 3))]
            + [pl.BlockSpec(memory_space=pl.ANY)] * len(earlier),
            out_specs=[
                pl.BlockSpec((half, width), lambda j, m: (spot(m), jnp.minimum(j, 2))),
                pl.BlockSpec((half, width), lambda j, m: (spot(m), 0)),
            ],
        ),
        out_shape=[
            jax.ShapeDtypeStruct((width, 3 * width), F32),
            jax.ShapeDtypeStruct((width, width), F32),
        ],
        input_output_aliases={2 + GROUPS + n: n for n in range(len(earlier))},
        compiler_params=params(),
        cost_estimate=cost(1e6, 14e6),
        name="att_place",
    )(meta, *[grads] * (GROUPS + 1), *earlier)


def swap_with(x, axis, bit=1):
    count = lax.axis_size(axis)
    return lax.ppermute(x, axis, [(i, i ^ bit) for i in range(count)])


ALL = ("chips", "core", "ulysses")


def chains():
    count = lax.axis_size("chips") * 4
    bits = [1] + [1 << n for n in range(2, count.bit_length() - 1)]
    swapped = list(bits)
    for n in range(0, len(bits) - 1, 2):
        swapped[n], swapped[n + 1] = bits[n + 1], bits[n]
    return count, bits, swapped


class Chain:
    def __init__(self, x, more, axis):
        self.x, self.more, self.axis, self.at = x, more, axis, 0
        self.count, *self.orders = chains()
        self.hops = len(self.orders[0])

    def swap(self, x, hop):
        pairs = [(i, i ^ self.orders[(i >> 1) & 1][hop]) for i in range(self.count)]
        return lax.ppermute(x, ALL, pairs)

    def bit(self, hop):
        place = lax.axis_index(ALL)
        step = jnp.where(lax.axis_index("core") == 0, self.orders[0][hop], self.orders[1][hop])
        return jnp.minimum(place & step, 1)

    def cut(self, x, which):
        half = x.shape[self.axis] // 2
        return lax.dynamic_slice_in_dim(x, which * half, half, self.axis)

    def piece(self, which):
        part = self.cut(self.x, which).astype(F32)
        return part if self.more is None else part + self.cut(self.more, which).astype(F32)

    def add(self, hop):
        self.x = (self.piece(self.bit(hop)) + self.got.astype(F32)).astype(BF16)
        self.more = None

    def join(self, hop):
        first = self.bit(hop) == 0
        low = jnp.where(first, self.x, self.got)
        high = jnp.where(first, self.got, self.x)
        self.x = jnp.concatenate([low, high], self.axis)

    @property
    def plan(self):
        wide = min(2, self.hops)
        steps = [("halve", hop) for hop in range(wide)]
        steps += [("whole", hop) for hop in range(wide, self.hops)]
        return steps + [("gather", hop) for hop in range(wide - 1, -1, -1)]

    @property
    def done(self):
        return self.at > len(self.plan)

    def prepare(self):
        plan, at = self.plan, self.at
        self.at += 1
        if at:
            kind, hop = plan[at - 1]
            if kind == "halve":
                self.add(hop)
            elif kind == "whole":
                self.x = plus(self.x, self.got)
            else:
                self.join(hop)
        if at == len(plan):
            self.out = None
            return
        kind, self.hop = plan[at]
        self.out = self.x
        if kind == "halve":
            self.out = self.piece(1 - self.bit(self.hop)).astype(BF16)

    def fire(self):
        self.got = self.swap(self.out, self.hop)


class Butterfly:
    def __init__(self, x):
        self.x, self.at = x, 0
        self.count = lax.axis_size("chips") * 4
        self.hops = self.count.bit_length() - 1

    @property
    def done(self):
        return self.at > self.hops

    def prepare(self):
        if self.at:
            self.x = self.x + self.got
        self.out = self.x if self.at < self.hops else None
        self.at += 1

    def fire(self):
        bit = 1 << (self.at - 1)
        self.got = lax.ppermute(self.out, ALL, [(i, i ^ bit) for i in range(self.count)])


def advance(values, *running):
    running = [chain for chain in running if not chain.done]
    for chain in running:
        chain.prepare()
    outs = [chain.x if chain.out is None else chain.out for chain in running]
    tied = tie(*outs, *values)
    for chain, out in zip(running, tied):
        if chain.out is None:
            chain.x = out
        else:
            if chain.out is chain.x:
                chain.x = out
            chain.out = out
            chain.fire()
    return tied[len(running) :]


def tie(*values):
    return lax.optimization_barrier(values)


def body(
    inputs_long,
    inputs_short,
    steps_long,
    steps_short,
    lengths,
    time_table,
    attngain,
    attnshift,
    qkvweight,
    querybias,
    valuebias,
    projweight,
    projbias,
    mlpgain,
    mlpshift,
    upweight,
    upbias,
    downweight,
    downbias,
    upstream_long,
    upstream_short,
):
    tokens, width = inputs_long.shape[1], inputs_long.shape[2]
    side = lax.axis_index("ulysses")
    core = lax.axis_index("core")
    meta = jnp.stack([side * tokens, side, 1 - core]).astype(jnp.int32)
    vecs, ub = pack(
        (attngain, attnshift, querybias, valuebias, projbias, mlpgain, mlpshift, downbias), upbias
    )

    edge = lax.dynamic_slice_in_dim(inputs_short[0], (1 - side) * (tokens - HALO), HALO, 0)
    across = (swap_with(inputs_long[0], "ulysses"), swap_with(edge, "ulysses"))

    q, ko, vo, start, rows, norm_s, norm_k = own_tokens(
        lengths, steps_short, steps_long, meta, inputs_long, inputs_short, time_table, vecs, qkvweight
    )
    kr, vr, norm_s, norm_k = far_tokens(lengths, meta, *across, rows, vecs, qkvweight, norm_s, norm_k)
    att, lse, bias = attend(lengths, meta, q, ko, vo, kr, vr)
    core_swap = lambda x: swap_with(x, "core")
    send, n2, seed, mid, outacc, dn2acc, att_s, att_k, ub_a = ffn_a(
        meta, att, start, upstream_long, upstream_short, vecs, ub, projweight, upweight, downweight
    )
    send, n2 = tie(send, n2)
    got = core_swap(send)
    out_long, out_short, keep, dbr, datt, sums_mlp, ub_b = ffn_b(
        meta, n2, seed, mid, outacc, dn2acc, vecs, ub, projweight, upweight, downweight
    )
    mlp = Chain(keep, got, 2)
    (datt,) = advance((datt,), mlp)

    count = width // PAIR // GROUPS
    grads, head_sums = [], []
    for n in range(GROUPS):
        d, sums = attend_back(n * count, count, q, ko, vo, kr, vr, datt, lse, bias)
        grads.append(d)
        head_sums.append(sums[0:2])
        if n:
            datt, *grads = advance((datt, *grads), mlp)
        else:
            datt, *grads = tie(datt, *grads)
    shares = lambda norm, att_half: jnp.concatenate(
        [outer(norm, d) for d in grads] + [outer(att_half, dbr)], 1
    )
    send = shares(norm_s, att_s)
    send, *grads = tie(send, *grads)
    got = core_swap(send)
    rest = Chain(shares(norm_k, att_k), got, 0)
    grads = advance(grads, rest)
    grads = advance(grads, mlp, rest)
    back = far_grad(meta, grads, qkvweight, kr.shape[0])
    (back,) = advance((back,), rest)
    back = swap_with(back, "ulysses")
    grads = advance(grads, mlp)
    in_long, in_short, sums_in = near_grad(meta, grads, qkvweight, back, start, dbr, vecs)
    small = Butterfly(
        jnp.concatenate(
            [
                sums_in[0:2],
                jnp.concatenate(head_sums, 1),
                sums_mlp[0:4],
                (ub_a + ub_b).reshape(-1, width),
            ],
            0,
        )
    )
    advance((), mlp, small)
    advance((), rest, small)
    advance((), rest, small)
    while not mlp.done:
        advance((), mlp)
    mlp_other = core_swap(mlp.x)
    held = mlp_place(meta, False, mlp.x)
    turn = 0
    while not (rest.done and small.done):
        live = not rest.done
        if turn == 1:
            held = advance(held, rest, small)
        else:
            advance((), rest, small)
        turn += 1
        if live and rest.done:
            rest_other = core_swap(rest.x)
            placed = att_place(meta, False, rest.x)
    *placed, mlp_other = tie(*placed, mlp_other)
    held = mlp_place(meta, True, mlp_other, held)
    g_down, g_up, rest_other = tie(*held, rest_other)
    g_qkv, g_proj = att_place(meta, True, rest_other, placed)
    small = small.x
    return (
        out_long,
        out_short,
        in_long,
        in_short,
        small[0],
        small[1],
        g_qkv,
        small[2],
        small[3],
        g_proj,
        small[4],
        small[5],
        small[6],
        g_up,
        small[8:].reshape(-1),
        g_down,
        small[7],
    )


def solution(mesh):
    seq, pair = mesh.shape["seq"], mesh.shape["ulysses"]
    split = jax.sharding.Mesh(mesh.devices.reshape(seq // 2, 2, pair), ("chips", "core", "ulysses"))
    rows = ("chips", "core")
    tokens = P(rows, "ulysses", None)
    placed = (tokens, tokens, P(rows), P(rows, None), P(rows, None)) + (P(),) * 14 + (tokens,) * 2
    return jax.shard_map(
        body,
        mesh=split,
        in_specs=placed,
        out_specs=(tokens,) * 4 + (P(),) * 13,
        check_vma=False,
    )
```

```python
import functools

import jax
import jax.numpy as jnp
from jax import lax
from jax.experimental import pallas as pl
from jax.experimental.pallas import tpu as pltpu
from jax.sharding import PartitionSpec as P

HEAD = 64
PAIR = 2 * HEAD
HALO = 64
EPS = 1e-05
GROUP = 16
F32 = jnp.float32
BF16 = jnp.bfloat16
VMEM_LIMIT = 56 * 1024 * 1024

NT = (((1,), (1,)), ((), ()))
NN = (((1,), (0,)), ((), ()))


def mm(left, right, dims=NN):
    return lax.dot_general(left, right, dims, preferred_element_type=F32)


def params(steps=1):
    return pltpu.CompilerParams(
        vmem_limit_bytes=VMEM_LIMIT, dimension_semantics=("arbitrary",) * steps
    )


def cost(flops, moved, scale=1):
    return pl.CostEstimate(flops=int(flops * scale), bytes_accessed=int(moved * scale), transcendentals=0)


def norm_parts(values_in):
    centre = values_in - jnp.mean(values_in, -1, keepdims=True)
    spread = jnp.mean(centre * centre, -1, keepdims=True)
    scale = lax.rsqrt(spread + EPS)
    return centre * scale, scale


def bounds_rows(lengths_s, segs, width):
    lane = lax.broadcasted_iota(jnp.int32, (1, width), 1)
    low = jnp.zeros((1, width), jnp.int32)
    high = jnp.zeros((1, width), jnp.int32)
    at = jnp.int32(0)
    for k in range(segs):
        low = jnp.where(lane == k, at, low)
        at = at + lengths_s[0, k]
        high = jnp.where(lane == k, at, high)
    return lane, low, high


def pack_kernel(*refs):
    vecs, ub = refs[-2:]
    for n, ref in enumerate(refs[:-3]):
        vecs[n : n + 1, :] = ref[...].astype(F32).reshape(1, -1)
    ub[...] = refs[-3][...].astype(F32).reshape(1, -1)


def pack(vectors, wide):
    width = vectors[0].shape[0]
    return pl.pallas_call(
        pack_kernel,
        out_shape=[
            jax.ShapeDtypeStruct((len(vectors), width), F32),
            jax.ShapeDtypeStruct((1, wide.shape[0]), F32),
        ],
        cost_estimate=cost(1e6, 1e5),
        name="pack",
    )(*vectors, wide)


def own_kernel(
    lengths_s, steps_short_s, steps_long_s, meta_s,
    xl, xs, table, vecs, w,
    q_o, k_o, v_o, st_o, rows_o, ns_o, nk_o,
    buf, sem,
):
    b = pl.program_id(0)
    segs = lengths_s.shape[1]
    tokens, width = xl.shape[1], xl.shape[2]

    @pl.when(b == 0)
    def _():
        copies = []
        target = jnp.zeros((32, buf.shape[0]), jnp.int32) - 1
        sub = lax.broadcasted_iota(jnp.int32, (32, buf.shape[0]), 0)
        for k in range(segs + 1):
            step = steps_short_s[0, k] if k < segs else steps_long_s[0]
            base = pl.multiple_of((step // GROUP) * GROUP, GROUP)
            copy = pltpu.make_async_copy(
                table.at[pl.ds(base, GROUP), :], buf.at[pl.ds(k * GROUP, GROUP), :], sem.at[k]
            )
            copy.start()
            copies.append(copy)
            target = jnp.where(sub == k, k * GROUP + step - base, target)
        rest = buf.shape[0] - (segs + 1) * GROUP
        if rest:
            buf[pl.ds((segs + 1) * GROUP, rest), :] = jnp.zeros((rest, width), BF16)
        for copy in copies:
            copy.wait()
        lane = lax.broadcasted_iota(jnp.int32, (32, buf.shape[0]), 1)
        pick = jnp.where(lane == target, 1.0, 0.0).astype(BF16)
        rows_o[...] = mm(pick, buf[...]).astype(BF16)

    lane, low, high = bounds_rows(lengths_s, segs, 32)
    whole = lane == segs
    low = jnp.where(b == 0, 0, low)
    high = jnp.where(b == 0, jnp.where(whole, 1 << 30, 0), high)
    place = meta_s[0] + lax.broadcasted_iota(jnp.int32, (tokens, 1), 0)
    pick = jnp.where((place >= low) & (place < high), 1.0, 0.0).astype(BF16)
    embed = mm(pick, rows_o[...])
    start = jnp.where(b == 0, xl[0], xs[0]).astype(F32) + embed
    st_o[0] = start
    unit, _ = norm_parts(start)
    normed = (unit * vecs[0:1, :] + vecs[1:2, :]).astype(BF16)
    left, right = normed[:, : width // 2], normed[:, width // 2 :]
    ns_o[...] = jnp.where(meta_s[2] == 1, right, left)
    nk_o[...] = jnp.where(meta_s[2] == 1, left, right)
    q_o[0] = ((mm(normed, w[:, :width]) + vecs[2:3, :]) * HEAD ** (-0.5)).astype(BF16)
    k_o[0] = mm(normed, w[:, width : 2 * width]).astype(BF16)
    v_o[0] = (mm(normed, w[:, 2 * width :]) + vecs[3:4, :]).astype(BF16)


def own_tokens(lengths, steps_short, steps_long, meta, xl, xs, table, vecs, w):
    tokens, width = xl.shape[1], xl.shape[2]
    segs = lengths.shape[1]
    spots = -(-(segs + 1) * GROUP // 128) * 128
    whole = lambda *shape: pl.BlockSpec(shape, lambda b, *_: (0,) * len(shape))
    part = pl.BlockSpec((1, tokens, width), lambda b, *_: (b, 0, 0))
    half = pl.BlockSpec((tokens, width // 2), lambda b, *_: (b, 0))
    stacked = jax.ShapeDtypeStruct((2, tokens, width), BF16)
    return pl.pallas_call(
        own_kernel,
        grid_spec=pltpu.PrefetchScalarGridSpec(
            num_scalar_prefetch=4,
            grid=(2,),
            in_specs=[
                whole(1, tokens, width),
                whole(1, tokens, width),
                pl.BlockSpec(memory_space=pl.ANY),
                whole(*vecs.shape),
                whole(*w.shape),
            ],
            out_specs=[part] * 4 + [whole(32, width)] + [half, half],
            scratch_shapes=[pltpu.VMEM((spots, width), BF16), pltpu.SemaphoreType.DMA((segs + 1,))],
        ),
        out_shape=[stacked] * 3
        + [jax.ShapeDtypeStruct((2, tokens, width), F32), jax.ShapeDtypeStruct((32, width), BF16)]
        + [jax.ShapeDtypeStruct((3 * tokens + 2 * HALO, width // 2), BF16)] * 2,
        compiler_params=params(),
        cost_estimate=cost(4 * tokens * width * 3 * width, 14e6),
        name="own_tokens",
    )(lengths, steps_short, steps_long, meta, xl, xs, table, vecs, w)


def far_kernel(
    lengths_s, meta_s, xr, xe, rows, vecs, wk, wv, ns_i, nk_i, k_o, v_o, ns_o, nk_o, ns, nk, sem
):
    segs = lengths_s.shape[1]
    total, width = k_o.shape
    tokens = total - 2 * HALO
    side = meta_s[1]
    edge = xe[...].astype(F32)
    before = jnp.where(side == 1, edge, 0.0)
    after = jnp.where(side == 0, edge, 0.0)
    x = jnp.concatenate([xr[...].astype(F32), before, after], axis=0)
    lane, low, high = bounds_rows(lengths_s, segs, 32)
    row = lax.broadcasted_iota(jnp.int32, (total, 1), 0)
    place = meta_s[0] + row - HALO - jnp.where(row < tokens + HALO, tokens, 0)
    inside = (place >= low) & (place < high)
    story = jnp.where(lane == segs, 1.0, 0.0)
    pick = jnp.where(row < tokens, story, jnp.where(inside, 1.0, 0.0)).astype(BF16)
    start = x + mm(pick, rows[...])
    unit, _ = norm_parts(start)
    normed = (unit * vecs[0:1, :] + vecs[1:2, :]).astype(BF16)
    left, right = normed[:, : width // 2], normed[:, width // 2 :]
    ns[...] = jnp.where(meta_s[2] == 1, right, left)
    nk[...] = jnp.where(meta_s[2] == 1, left, right)
    rest = pl.ds(2 * tokens, total)
    copy_s = pltpu.make_async_copy(ns, ns_o.at[rest, :], sem.at[0])
    copy_k = pltpu.make_async_copy(nk, nk_o.at[rest, :], sem.at[1])
    copy_s.start()
    copy_k.start()
    k_o[...] = mm(normed, wk[...]).astype(BF16)
    v_o[...] = (mm(normed, wv[...]) + vecs[3:4, :]).astype(BF16)
    copy_s.wait()
    copy_k.wait()


def far_tokens(lengths, meta, xr, xe, rows, vecs, w, ns, nk):
    width = xr.shape[1]
    total = xr.shape[0] + 2 * HALO
    whole = lambda *shape: pl.BlockSpec(shape, lambda i, *_: (0,) * len(shape))
    out = jax.ShapeDtypeStruct((total, width), BF16)
    return pl.pallas_call(
        far_kernel,
        grid_spec=pltpu.PrefetchScalarGridSpec(
            num_scalar_prefetch=2,
            grid=(1,),
            in_specs=[
                whole(*xr.shape),
                whole(*xe.shape),
                whole(*rows.shape),
                whole(*vecs.shape),
                pl.BlockSpec((width, width), lambda i, *_: (0, 1)),
                pl.BlockSpec((width, width), lambda i, *_: (0, 2)),
                pl.BlockSpec(memory_space=pl.ANY),
                pl.BlockSpec(memory_space=pl.ANY),
            ],
            out_specs=[whole(total, width)] * 2 + [pl.BlockSpec(memory_space=pl.ANY)] * 2,
            scratch_shapes=[pltpu.VMEM((total, width // 2), BF16)] * 2
            + [pltpu.SemaphoreType.DMA((2,))],
        ),
        out_shape=[out] * 2 + [jax.ShapeDtypeStruct(ns.shape, BF16)] * 2,
        input_output_aliases={8: 2, 9: 3},
        compiler_params=params(),
        cost_estimate=cost(2 * total * width * 2 * width, 6e6),
        name="far_tokens",
    )(lengths, meta, xr, xe, rows, vecs, w, w, ns, nk)


def seg_of(lengths_s, place):
    segs = lengths_s.shape[1]
    at = jnp.int32(0)
    seg = jnp.zeros(place.shape, jnp.int32)
    for k in range(segs - 1):
        at = at + lengths_s[0, k]
        seg = seg + jnp.where(place >= at, 1, 0)
    at = at + lengths_s[0, segs - 1]
    return jnp.where(place < 0, -1, jnp.where(place >= at, -2, seg))


def halves():
    lane = lax.broadcasted_iota(jnp.int32, (1, PAIR), 1)
    return (lane < HEAD, lane >= HEAD)


def attend_kernel(lengths_s, meta_s, q, ko, vo, kr, vr, o, lse, bias_t, bias, kx, vx):
    tokens = q.shape[1]
    blocks = tokens // 128
    span = 128 + 2 * HALO

    @pl.when(pl.program_id(0) == 0)
    def _():
        seg_q = seg_of(lengths_s, meta_s[0] + lax.broadcasted_iota(jnp.int32, (tokens, 1), 0))
        seg_k = seg_of(
            lengths_s, meta_s[0] - HALO + lax.broadcasted_iota(jnp.int32, (1, tokens + 2 * HALO), 1)
        )
        for i in range(blocks):
            same = seg_q[i * 128 : (i + 1) * 128, :] == seg_k[:, i * 128 : i * 128 + span]
            bias[i] = jnp.where(same, 0.0, -1e30)
            bias_t[i] = bias[i].T

    for ext, own, far in ((kx, ko, kr), (vx, vo, vr)):
        ext[0:HALO, :] = far[tokens : tokens + HALO, :]
        ext[HALO : HALO + tokens, :] = own[1]
        ext[HALO + tokens :, :] = far[tokens + HALO :, :]

    lane = lax.broadcasted_iota(jnp.int32, (1, PAIR), 1)
    stats = jnp.zeros((tokens, 128), F32)
    step = tokens
    for h, half in enumerate(halves()):
        logs = []
        for i in range(tokens // step):
            rows = pl.ds(i * step, step)
            qh = jnp.where(half, q[0, rows, :], 0)
            s1 = mm(qh, ko[0], NT)
            s2 = mm(qh, kr[:tokens, :], NT)
            top = jnp.maximum(jnp.max(s1, -1, keepdims=True), jnp.max(s2, -1, keepdims=True))
            e1 = jnp.exp(s1 - top)
            e2 = jnp.exp(s2 - top)
            total = jnp.sum(e1, -1, keepdims=True) + jnp.sum(e2, -1, keepdims=True)
            r = mm(e1.astype(BF16), vo[0]) + mm(e2.astype(BF16), vr[:tokens, :])
            r = (r / total).astype(BF16)
            o[0, rows, :] = r if h == 0 else jnp.where(half, r, o[0, rows, :])
            logs.append(top + jnp.log(total))
        stats = jnp.where(lane == h, jnp.concatenate(logs, 0), stats)
        logs = []
        for i in range(blocks):
            rows = pl.ds(i * 128, 128)
            keys = pl.ds(i * 128, span)
            qh = jnp.where(half, q[1, rows, :], 0)
            s1 = mm(qh, kx[keys, :], NT) + bias[i]
            top = jnp.max(s1, -1, keepdims=True)
            e1 = jnp.exp(s1 - top)
            total = jnp.sum(e1, -1, keepdims=True)
            r = (mm(e1.astype(BF16), vx[keys, :]) / total).astype(BF16)
            o[1, rows, :] = r if h == 0 else jnp.where(half, r, o[1, rows, :])
            logs.append(top + jnp.log(total))
        stats = jnp.where(lane == 2 + h, jnp.concatenate(logs, 0), stats)
    lse[0] = stats.T[0:8, :]


def head_specs(tokens):
    own = pl.BlockSpec((2, tokens, PAIR), lambda i, *_: (0, 0, i))
    far = pl.BlockSpec((tokens + 2 * HALO, PAIR), lambda i, *_: (0, i))
    row = pl.BlockSpec((1, 8, tokens), lambda i, *_: (i, 0, 0))
    return own, far, row


def attend(lengths, meta, q, ko, vo, kr, vr):
    tokens, width = q.shape[1], q.shape[2]
    pairs = width // PAIR
    own, far, row = head_specs(tokens)
    ext = pltpu.VMEM((tokens + 2 * HALO, PAIR), BF16)
    return pl.pallas_call(
        attend_kernel,
        grid_spec=pltpu.PrefetchScalarGridSpec(
            num_scalar_prefetch=2,
            grid=(pairs,),
            in_specs=[own, own, own, far, far],
            out_specs=[
                own, row, pl.BlockSpec((tokens // 128, 128 + 2 * HALO, 128), lambda i, *_: (0, 0, 0)),
            ],
            scratch_shapes=[pltpu.VMEM((tokens // 128, 128, 128 + 2 * HALO), F32), ext, ext],
        ),
        out_shape=[
            jax.ShapeDtypeStruct(q.shape, BF16),
            jax.ShapeDtypeStruct((pairs, 8, tokens), F32),
            jax.ShapeDtypeStruct((tokens // 128, 128 + 2 * HALO, 128), F32),
        ],
        compiler_params=params(),
        cost_estimate=cost(4 * tokens * 2.5 * tokens * 256 * 2 * pairs, 8e6),
        name="attend",
    )(lengths, meta, q, ko, vo, kr, vr)


def attend_back_kernel(
    q, ko, vo, kr, vr, go, lse, bias, grad, sums, kx, vx, kt, dkx, dvx, dqt
):
    tokens = q.shape[1]
    far_at = 2 * tokens
    third = grad.shape[1] // 3
    at = [
        pl.ds(pl.multiple_of(n * third + pl.program_id(0) * PAIR, PAIR), PAIR) for n in range(3)
    ]
    grad[far_at:, at[0]] = jnp.zeros((grad.shape[0] - far_at, PAIR), BF16)
    blocks = tokens // 128
    span = 128 + 2 * HALO

    for ext, own, far in ((kx, ko, kr), (vx, vo, vr)):
        ext[0:HALO, :] = far[tokens : tokens + HALO, :]
        ext[HALO : HALO + tokens, :] = own[1]
        ext[HALO + tokens :, :] = far[tokens + HALO :, :]

    shift = HEAD ** (-0.5)
    sum_q = jnp.zeros((1, PAIR), F32)
    sum_v = jnp.zeros((1, PAIR), F32)

    k_parts = (ko[0], kr[:tokens, :])
    v_parts = (vo[0], vr[:tokens, :])
    for n in range(2):
        kt[n, :, :tokens] = k_parts[n].T
    dk_sums = [jnp.zeros((tokens, PAIR), F32)] * 2
    dv_sums = [jnp.zeros((tokens, PAIR), F32)] * 2
    for h, half in enumerate(halves()):
        rows = pl.ds(h * HEAD, HEAD)
        qh = jnp.where(half, q[0], 0)
        gh = jnp.where(half, go[0], 0)
        log = lse[0, h : h + 1, :]
        pts = [jnp.exp(mm(k_parts[n], qh, NT) - log) for n in range(2)]
        dpts = [mm(v_parts[n], gh, NT) for n in range(2)]
        delta = jnp.sum(pts[0] * dpts[0], 0, keepdims=True)
        delta += jnp.sum(pts[1] * dpts[1], 0, keepdims=True)
        part = None
        for n in range(2):
            dst = (pts[n] * (dpts[n] - delta)).astype(BF16)
            dv_sums[n] = dv_sums[n] + mm(pts[n].astype(BF16), gh)
            dk_sums[n] = dk_sums[n] + mm(dst, qh)
            turned = mm(kt[n, rows, :tokens], dst)
            part = turned if n == 0 else part + turned
        dqt[rows, :] = part
    for n, row in enumerate((0, far_at)):
        grad[row : row + tokens, at[1]] = dk_sums[n].astype(BF16)
        grad[row : row + tokens, at[2]] = dv_sums[n].astype(BF16)
    for n in range(2):
        sum_v += jnp.sum(dv_sums[n], 0, keepdims=True)
    out = dqt[...].T * shift
    grad[:tokens, at[0]] = out.astype(BF16)
    sum_q += jnp.sum(out, 0, keepdims=True)

    kt[0] = kx[...].T
    dkx[...] = jnp.zeros_like(dkx)
    dvx[...] = jnp.zeros_like(dvx)
    for i in range(blocks):
        cols = slice(i * 128, (i + 1) * 128)
        keys = slice(i * 128, i * 128 + span)
        dk_sum = jnp.zeros((span, PAIR), F32)
        dv_sum = jnp.zeros((span, PAIR), F32)
        for h, half in enumerate(halves()):
            rows = slice(h * HEAD, (h + 1) * HEAD)
            qh = jnp.where(half, q[1, cols, :], 0)
            gh = jnp.where(half, go[1, cols, :], 0)
            st = mm(kx[keys, :], qh, NT) + bias[i]
            pt = jnp.exp(st - lse[0, 2 + h : 3 + h, cols])
            dpt = mm(vx[keys, :], gh, NT)
            delta = jnp.sum(pt * dpt, 0, keepdims=True)
            dst = (pt * (dpt - delta)).astype(BF16)
            dv_sum += mm(pt.astype(BF16), gh)
            dk_sum += mm(dst, qh)
            dqt[rows, cols] = mm(kt[0, rows, keys], dst)
        dkx[keys, :] += dk_sum
        dvx[keys, :] += dv_sum
    out = dqt[...].T * shift
    grad[tokens:far_at, at[0]] = out.astype(BF16)
    sum_q += jnp.sum(out, 0, keepdims=True)
    sum_v += jnp.sum(dvx[...], 0, keepdims=True)
    edge = far_at + tokens
    for ext, cols in ((dkx, at[1]), (dvx, at[2])):
        grad[tokens:far_at, cols] = ext[HALO : HALO + tokens, :].astype(BF16)
        grad[edge : edge + HALO, cols] = ext[0:HALO, :].astype(BF16)
        grad[edge + HALO :, cols] = ext[HALO + tokens :, :].astype(BF16)
    sums[...] = jnp.concatenate([sum_q, sum_v, jnp.zeros((6, PAIR), F32)], 0)


def attend_back(first, count, q, ko, vo, kr, vr, go, lse, bias):
    tokens, width = q.shape[1], q.shape[2]
    wide = tokens + 2 * HALO
    own = pl.BlockSpec((2, tokens, PAIR), lambda i: (0, 0, i + first))
    far = pl.BlockSpec((wide, PAIR), lambda i: (0, i + first))
    row = pl.BlockSpec((1, 8, tokens), lambda i: (i + first, 0, 0))
    ext = pltpu.VMEM((wide, PAIR), BF16)
    ext32 = pltpu.VMEM((wide, PAIR), F32)
    rows, cols = 2 * tokens + wide, 3 * count * PAIR
    return pl.pallas_call(
        attend_back_kernel,
        grid=(count,),
        in_specs=[own, own, own, far, far, own, row]
        + [pl.BlockSpec(bias.shape, lambda i: (0, 0, 0))],
        out_specs=[
            pl.BlockSpec((rows, cols), lambda i: (0, 0)),
            pl.BlockSpec((8, PAIR), lambda i: (0, i)),
        ],
        scratch_shapes=[
            ext,
            ext,
            pltpu.VMEM((2, PAIR, wide), BF16),
            ext32,
            ext32,
            pltpu.VMEM((PAIR, tokens), F32),
        ],
        out_shape=[
            jax.ShapeDtypeStruct((rows, cols), BF16),
            jax.ShapeDtypeStruct((8, count * PAIR), F32),
        ],
        compiler_params=params(),
        cost_estimate=cost(10 * tokens * 2.5 * tokens * 256 * 2 * count, 2e6 * count),
        name="attend_back",
    )(q, ko, vo, kr, vr, go, lse, bias)


def chunk_spot(c, part, meta_s):
    return 2 * jnp.where(part == 0, meta_s[2], 1 - meta_s[2]) + c


def ffn_chunk(spot, first, n2, seed, ub, wu, wd, act, dh, sums_ub):
    chunk = wu.shape[1]
    k0 = 0.7978845608028654
    piece = 256

    @pl.when(first)
    def _():
        sums_ub[...] = jnp.zeros_like(sums_ub)

    for j in range(chunk // piece):
        cols = slice(j * piece, (j + 1) * piece)
        hid = mm(n2, wu[:, cols]) + ub[0:1, cols]
        square = hid * hid
        t = jnp.tanh(hid * (k0 + k0 * 0.044715 * square))
        half = 0.5 + 0.5 * t
        act[:, cols] = (hid * half).astype(BF16)
        slope = half + (hid * (0.5 - 0.5 * (t * t))) * (k0 + 3 * k0 * 0.044715 * square)
        dh32 = mm(seed, wd[cols, :], NT) * slope
        dh[:, cols] = dh32.astype(BF16)
        at = pl.ds(pl.multiple_of(spot * chunk + j * piece, piece), piece)
        sums_ub[0:1, at] += jnp.sum(dh32, 0, keepdims=True)


def ffn_a_kernel(
    meta_s, att, st, ul, us, vecs, ub, wp, wu, wd,
    g_o, n2_o, seed_o, mid_o, out_o, dn2_o, as_o, ak_o, sums_ub,
    n2, seed, n2t, seedt, outacc, dn2acc, act, dh,
):
    c, b = pl.program_id(0), pl.program_id(1)
    half = wp.shape[0] // 2
    tokens = mid_o.shape[1]
    rows = pl.ds(pl.multiple_of(b * tokens, tokens), tokens)

    @pl.when(c == 0)
    def _():
        up = jnp.where(b == 0, ul[0], us[0])
        seed[rows, :] = up
        seed_o[0] = up
        seedt[:, rows] = up.T
        whole = att[0]
        as_o[...] = jnp.where(meta_s[2] == 1, whole[:, half:], whole[:, :half])
        ak_o[...] = jnp.where(meta_s[2] == 1, whole[:, :half], whole[:, half:])
        middle = st[0] + mm(whole, wp[...]) + vecs[4:5, :]
        mid_o[0] = middle
        unit, _ = norm_parts(middle)
        normed = (unit * vecs[5:6, :] + vecs[6:7, :]).astype(BF16)
        n2[rows, :] = normed
        n2_o[0] = normed
        n2t[:, rows] = normed.T

    spot = chunk_spot(c, 0, meta_s)
    act_b, dh_b = act.at[rows, :], dh.at[rows, :]
    ffn_chunk(spot, (b == 0) & (c == 0), n2[rows, :], seed[rows, :], ub, wu, wd, act_b, dh_b, sums_ub)
    out = mm(act_b[...], wd[...])
    dn2 = mm(dh_b[...], wu[...], NT)

    @pl.when(c == 0)
    def _():
        outacc[rows, :] = mid_o[0] + vecs[7:8, :] + out
        dn2acc[rows, :] = dn2

    @pl.when(c == 1)
    def _():
        out_o[0] = outacc[rows, :] + out
        dn2_o[0] = dn2acc[rows, :] + dn2

    @pl.when(b == 1)
    def _():
        g_o[0, 0] = mm(seedt[...], act[...]).astype(BF16)
        g_o[0, 1] = mm(n2t[...], dh[...]).astype(BF16)


def ffn_b_kernel(
    meta_s, n2, seed, mid, out_i, dn2_i, vecs, ub, wp, wu, wd,
    out_l, out_s, g_o, dbr_o, datt_o, sums, sums_ub,
    n2t, seedt, outacc, dn2acc, act, dh,
):
    c, b = pl.program_id(0), pl.program_id(1)
    tokens = mid.shape[1]
    rows = pl.ds(pl.multiple_of(b * tokens, tokens), tokens)

    @pl.when(c == 0)
    def _():
        seedt[:, rows] = seed[b].T
        n2t[:, rows] = n2[b].T

    spot = chunk_spot(c, 1, meta_s)
    act_b, dh_b = act.at[rows, :], dh.at[rows, :]
    ffn_chunk(spot, (b == 0) & (c == 0), n2[b], seed[b], ub, wu, wd, act_b, dh_b, sums_ub)
    out = mm(act_b[...], wd[...])
    dn2 = mm(dh_b[...], wu[...], NT)

    @pl.when(c == 0)
    def _():
        outacc[rows, :] = out_i[0] + out
        dn2acc[rows, :] = dn2_i[0] + dn2

    @pl.when(c == 1)
    def _():
        result = (outacc[rows, :] + out).astype(BF16)

        @pl.when(b == 0)
        def _():
            out_l[0] = result
            sums[...] = jnp.zeros_like(sums)

        @pl.when(b > 0)
        def _():
            out_s[0] = result

        unit, scale = norm_parts(mid[0])
        whole = dn2acc[rows, :] + dn2
        seed32 = seed[b].astype(F32)
        du = whole * vecs[5:6, :]
        back = du - jnp.mean(du, -1, keepdims=True) - unit * jnp.mean(du * unit, -1, keepdims=True)
        dmid = back * scale + seed32
        dbr = dmid.astype(BF16)
        dbr_o[0] = dbr
        datt_o[0] = mm(dbr, wp[...], NT).astype(BF16)
        sums[0:1, :] += jnp.sum(dmid, 0, keepdims=True)
        sums[1:2, :] += jnp.sum(whole * unit, 0, keepdims=True)
        sums[2:3, :] += jnp.sum(whole, 0, keepdims=True)
        sums[3:4, :] += jnp.sum(seed32, 0, keepdims=True)

    @pl.when(b == 1)
    def _():
        g_o[0, 0] = mm(seedt[...], act[...]).astype(BF16)
        g_o[0, 1] = mm(n2t[...], dh[...]).astype(BF16)


def ffn_specs(tokens, width, part):
    whole = lambda *shape: pl.BlockSpec(shape, lambda c, b, m: (0,) * len(shape))
    early = pl.BlockSpec((1, tokens, width), lambda c, b, m: (jnp.where(c == 0, b, 1), 0, 0))
    late = pl.BlockSpec((1, tokens, width), lambda c, b, m: (jnp.where(c == 0, 0, b), 0, 0))
    grads = pl.BlockSpec((1, 2, width, width), lambda c, b, m: (c, 0, 0, 0))
    weights = [
        pl.BlockSpec((1, width), lambda c, b, m: (0, chunk_spot(c, part, m))),
        whole(width, width),
        pl.BlockSpec((width, width), lambda c, b, m: (0, chunk_spot(c, part, m))),
        pl.BlockSpec((width, width), lambda c, b, m: (chunk_spot(c, part, m), 0)),
    ]
    shape = lambda kind: jax.ShapeDtypeStruct((2, tokens, width), kind)
    low, high = pltpu.VMEM((2 * tokens, width), BF16), pltpu.VMEM((2 * tokens, width), F32)
    turned = pltpu.VMEM((width, 2 * tokens), BF16)
    return whole, early, late, grads, weights, shape, low, high, turned


def ffn_a(meta, att, st, ul, us, vecs, ub, wp, wu, wd):
    tokens, width = ul.shape[1], ul.shape[2]
    hidden = wu.shape[1]
    whole, early, late, grads, weights, shape, low, high, turned = ffn_specs(tokens, width, 0)
    single = whole(1, tokens, width)
    half = pl.BlockSpec((tokens, width // 2), lambda c, b, m: (jnp.where(c == 0, b, 1), 0))
    return pl.pallas_call(
        ffn_a_kernel,
        grid_spec=pltpu.PrefetchScalarGridSpec(
            num_scalar_prefetch=1,
            grid=(2, 2),
            in_specs=[early, early, single, single, whole(*vecs.shape)] + weights,
            out_specs=[grads, early, early, early, late, late, half, half, whole(1, hidden)],
            scratch_shapes=[low, low, turned, turned, high, high, low, low],
        ),
        out_shape=[jax.ShapeDtypeStruct((2, 2, width, width), BF16)]
        + [shape(BF16)] * 2
        + [shape(F32)] * 3
        + [jax.ShapeDtypeStruct((2 * tokens, width // 2), BF16)] * 2
        + [jax.ShapeDtypeStruct((1, hidden), F32)],
        compiler_params=params(2),
        cost_estimate=cost(4 * tokens * width * (width + 3 * hidden), 40e6),
        name="ffn_a",
    )(meta, att, st, ul, us, vecs, ub, wp, wu, wd)


def ffn_b(meta, n2, seed, mid, outacc, dn2acc, vecs, ub, wp, wu, wd):
    tokens, width = mid.shape[1], mid.shape[2]
    hidden = wu.shape[1]
    whole, early, late, grads, weights, shape, low, high, turned = ffn_specs(tokens, width, 1)
    single = jax.ShapeDtypeStruct((1, tokens, width), BF16)
    both = whole(2, tokens, width)
    return pl.pallas_call(
        ffn_b_kernel,
        grid_spec=pltpu.PrefetchScalarGridSpec(
            num_scalar_prefetch=1,
            grid=(2, 2),
            in_specs=[both, both, late, early, early, whole(*vecs.shape)] + weights,
            out_specs=[whole(1, tokens, width)] * 2
            + [grads, late, late, whole(8, width), whole(1, hidden)],
            scratch_shapes=[turned, turned, high, high, low, low],
        ),
        out_shape=[single, single, jax.ShapeDtypeStruct((2, 2, width, width), BF16)]
        + [shape(BF16)] * 2
        + [jax.ShapeDtypeStruct((8, width), F32), jax.ShapeDtypeStruct((1, hidden), F32)],
        compiler_params=params(2),
        cost_estimate=cost(4 * tokens * width * (width + 3 * hidden), 40e6),
        name="ffn_b",
    )(meta, n2, seed, mid, outacc, dn2acc, vecs, ub, wp, wu, wd)


def back_through(grads, w):
    cols = [grad.shape[1] // 3 for grad in grads]
    pieces = [
        grad[:, n * col : (n + 1) * col] for n in range(3) for grad, col in zip(grads, cols)
    ]
    return mm(jnp.concatenate(pieces, 1), w[...], NT)


def far_grad_kernel(meta_s, *refs):
    count = (len(refs) - 3) // 2
    sources, w, d_o, held, sem = refs[:count], refs[count], refs[count + 1], refs[count + 2 : -1], refs[-1]
    total = held[0].shape[0]
    tokens = total - 2 * HALO
    copies = []
    for n, (source, target) in enumerate(zip(sources, held)):
        copy = pltpu.make_async_copy(source.at[pl.ds(2 * tokens, total), :], target, sem.at[n])
        copy.start()
        copies.append(copy)
    for copy in copies:
        copy.wait()
    full = back_through(held, w)
    d_o[0:tokens, :] = full[0:tokens, :].astype(BF16)
    before = full[tokens : tokens + HALO, :]
    after = full[tokens + HALO :, :]
    d_o[tokens:, :] = jnp.where(meta_s[1] == 1, before, after).astype(BF16)


def far_grad(meta, grads, w, total):
    width = w.shape[0]
    whole = lambda *shape: pl.BlockSpec(shape, lambda i, *_: (0,) * len(shape))
    return pl.pallas_call(
        far_grad_kernel,
        grid_spec=pltpu.PrefetchScalarGridSpec(
            num_scalar_prefetch=1,
            grid=(1,),
            in_specs=[pl.BlockSpec(memory_space=pl.ANY)] * len(grads) + [whole(*w.shape)],
            out_specs=whole(total - HALO, width),
            scratch_shapes=[pltpu.VMEM((total, d.shape[1]), BF16) for d in grads]
            + [pltpu.SemaphoreType.DMA((len(grads),))],
        ),
        out_shape=jax.ShapeDtypeStruct((total - HALO, width), BF16),
        compiler_params=params(),
        cost_estimate=cost(4 * total * width * width, 5e6),
        name="far_grad",
    )(meta, *grads, w)


def near_grad_kernel(meta_s, *refs):
    grads, (w, got, st, dbr, vecs, in_l, in_s, sums, acc) = refs[:-9], refs[-9:]
    b = pl.program_id(0)
    tokens = st.shape[1]
    acc[...] = back_through(grads, w)

    @pl.when(b == 0)
    def _():
        acc[...] += got[0:tokens, :].astype(F32)
        sums[...] = jnp.zeros_like(sums)

    @pl.when(b > 0)
    def _():
        edge = got[tokens:, :].astype(F32)
        acc[0:HALO, :] += jnp.where(meta_s[1] == 1, edge, 0.0)
        acc[tokens - HALO :, :] += jnp.where(meta_s[1] == 0, edge, 0.0)

    dn = acc[...]
    unit, scale = norm_parts(st[0])
    du = dn * vecs[0:1, :]
    back = du - jnp.mean(du, -1, keepdims=True) - unit * jnp.mean(du * unit, -1, keepdims=True)
    result = (back * scale + dbr[0].astype(F32)).astype(BF16)

    @pl.when(b == 0)
    def _():
        in_l[0] = result

    @pl.when(b > 0)
    def _():
        in_s[0] = result

    sums[0:1, :] += jnp.sum(dn * unit, 0, keepdims=True)
    sums[1:2, :] += jnp.sum(dn, 0, keepdims=True)


def near_grad(meta, grads, w, got, st, dbr, vecs):
    tokens, width = st.shape[1], st.shape[2]
    whole = lambda *shape: pl.BlockSpec(shape, lambda b, *_: (0,) * len(shape))
    part = pl.BlockSpec((1, tokens, width), lambda b, *_: (b, 0, 0))
    rows = lambda d: pl.BlockSpec((tokens, d.shape[1]), lambda b, *_: (b, 0))
    single = jax.ShapeDtypeStruct((1, tokens, width), BF16)
    return pl.pallas_call(
        near_grad_kernel,
        grid_spec=pltpu.PrefetchScalarGridSpec(
            num_scalar_prefetch=1,
            grid=(2,),
            in_specs=[
                *map(rows, grads), whole(*w.shape), whole(*got.shape), part, part, whole(*vecs.shape),
            ],
            out_specs=[whole(1, tokens, width), whole(1, tokens, width), whole(8, width)],
            scratch_shapes=[pltpu.VMEM((tokens, width), F32)],
        ),
        out_shape=[single, single, jax.ShapeDtypeStruct((8, width), F32)],
        compiler_params=params(),
        cost_estimate=cost(4 * tokens * width * 3 * width, 15e6),
        name="near_grad",
    )(meta, *grads, w, got, st, dbr, vecs)


def outer(left, right):
    rows = lambda x: x.reshape(-1, x.shape[-1])
    full = jnp.einsum("ni,nj->ij", rows(left), rows(right), preferred_element_type=F32)
    return full.astype(BF16)


def plus(x, y):
    return (x.astype(F32) + y.astype(F32)).astype(BF16)


PLACE = 384


def mlp_place_kernel(meta_s, turned, value, *rest):
    down, up = rest[-2:]
    down[...] = turned[0, 0].T.astype(F32)
    up[...] = value[0, 0].astype(F32)


def mlp_place(meta, theirs, grads, earlier=()):
    width = grads.shape[2]
    per = width // PLACE
    spot = lambda h, m: 2 * (m[2] if theirs else 1 - m[2]) + h
    return pl.pallas_call(
        mlp_place_kernel,
        grid_spec=pltpu.PrefetchScalarGridSpec(
            num_scalar_prefetch=1,
            grid=(2, per),
            in_specs=[
                pl.BlockSpec((1, 1, width, PLACE), lambda h, r, m: (h, 0, 0, r)),
                pl.BlockSpec((1, 1, PLACE, width), lambda h, r, m: (h, 1, r, 0)),
            ]
            + [pl.BlockSpec(memory_space=pl.ANY)] * len(earlier),
            out_specs=[
                pl.BlockSpec((PLACE, width), lambda h, r, m: (spot(h, m) * per + r, 0)),
                pl.BlockSpec((PLACE, width), lambda h, r, m: (r, spot(h, m))),
            ],
        ),
        out_shape=[
            jax.ShapeDtypeStruct((4 * width, width), F32),
            jax.ShapeDtypeStruct((width, 4 * width), F32),
        ],
        input_output_aliases={3 + n: n for n in range(len(earlier))},
        compiler_params=params(2),
        cost_estimate=cost(1e6, 14e6),
        name="mlp_place",
    )(meta, grads, grads, *earlier)


GROUPS = 3


def att_place_kernel(meta_s, *refs):
    parts, last, (qkv, proj) = refs[:GROUPS], refs[GROUPS], refs[-2:]
    cols = parts[0].shape[1]

    @pl.when(pl.program_id(0) < 3)
    def _():
        for n, part in enumerate(parts):
            qkv[:, n * cols : (n + 1) * cols] = part[...].astype(F32)

    @pl.when(pl.program_id(0) == 3)
    def _():
        proj[...] = last[...].astype(F32)


def att_place(meta, theirs, grads, earlier=()):
    half, width = grads.shape[0], 2 * grads.shape[0]
    spot = lambda m: m[2] if theirs else 1 - m[2]
    group = lambda n: pl.BlockSpec(
        (half, width // GROUPS), lambda j, m: (0, 3 * n + jnp.minimum(j, 2))
    )
    return pl.pallas_call(
        att_place_kernel,
        grid_spec=pltpu.PrefetchScalarGridSpec(
            num_scalar_prefetch=1,
            grid=(4,),
            in_specs=[group(n) for n in range(GROUPS)]
            + [pl.BlockSpec((half, width), lambda j, m: (0, 3))]
            + [pl.BlockSpec(memory_space=pl.ANY)] * len(earlier),
            out_specs=[
                pl.BlockSpec((half, width), lambda j, m: (spot(m), jnp.minimum(j, 2))),
                pl.BlockSpec((half, width), lambda j, m: (spot(m), 0)),
            ],
        ),
        out_shape=[
            jax.ShapeDtypeStruct((width, 3 * width), F32),
            jax.ShapeDtypeStruct((width, width), F32),
        ],
        input_output_aliases={2 + GROUPS + n: n for n in range(len(earlier))},
        compiler_params=params(),
        cost_estimate=cost(1e6, 14e6),
        name="att_place",
    )(meta, *[grads] * (GROUPS + 1), *earlier)


def swap_with(x, axis, bit=1):
    count = lax.axis_size(axis)
    return lax.ppermute(x, axis, [(i, i ^ bit) for i in range(count)])


ALL = ("chips", "core", "ulysses")


def chains():
    count = lax.axis_size("chips") * 4
    bits = [1] + [1 << n for n in range(2, count.bit_length() - 1)]
    swapped = list(bits)
    for n in range(0, len(bits) - 1, 2):
        swapped[n], swapped[n + 1] = bits[n + 1], bits[n]
    return count, bits, swapped


class Chain:
    def __init__(self, x, more, axis):
        self.x, self.more, self.axis, self.at = x, more, axis, 0
        self.count, *self.orders = chains()
        self.hops = len(self.orders[0])

    def swap(self, x, hop):
        pairs = [(i, i ^ self.orders[(i >> 1) & 1][hop]) for i in range(self.count)]
        return lax.ppermute(x, ALL, pairs)

    def bit(self, hop):
        place = lax.axis_index(ALL)
        step = jnp.where(lax.axis_index("core") == 0, self.orders[0][hop], self.orders[1][hop])
        return jnp.minimum(place & step, 1)

    def cut(self, x, which):
        half = x.shape[self.axis] // 2
        return lax.dynamic_slice_in_dim(x, which * half, half, self.axis)

    def piece(self, which):
        part = self.cut(self.x, which).astype(F32)
        return part if self.more is None else part + self.cut(self.more, which).astype(F32)

    def add(self, hop):
        self.x = (self.piece(self.bit(hop)) + self.got.astype(F32)).astype(BF16)
        self.more = None

    def join(self, hop):
        first = self.bit(hop) == 0
        low = jnp.where(first, self.x, self.got)
        high = jnp.where(first, self.got, self.x)
        self.x = jnp.concatenate([low, high], self.axis)

    @property
    def plan(self):
        wide = min(2, self.hops)
        steps = [("halve", hop) for hop in range(wide)]
        steps += [("whole", hop) for hop in range(wide, self.hops)]
        return steps + [("gather", hop) for hop in range(wide - 1, -1, -1)]

    @property
    def done(self):
        return self.at > len(self.plan)

    def prepare(self):
        plan, at = self.plan, self.at
        self.at += 1
        if at:
            kind, hop = plan[at - 1]
            if kind == "halve":
                self.add(hop)
            elif kind == "whole":
                self.x = plus(self.x, self.got)
            else:
                self.join(hop)
        if at == len(plan):
            self.out = None
            return
        kind, self.hop = plan[at]
        self.out = self.x
        if kind == "halve":
            self.out = self.piece(1 - self.bit(self.hop)).astype(BF16)

    def fire(self):
        self.got = self.swap(self.out, self.hop)


class Butterfly:
    def __init__(self, x):
        self.x, self.at = x, 0
        self.count = lax.axis_size("chips") * 4
        self.hops = self.count.bit_length() - 1

    @property
    def done(self):
        return self.at > self.hops

    def prepare(self):
        if self.at:
            self.x = self.x + self.got
        self.out = self.x if self.at < self.hops else None
        self.at += 1

    def fire(self):
        bit = 1 << (self.at - 1)
        self.got = lax.ppermute(self.out, ALL, [(i, i ^ bit) for i in range(self.count)])


def advance(values, *running):
    running = [chain for chain in running if not chain.done]
    for chain in running:
        chain.prepare()
    outs = [chain.x if chain.out is None else chain.out for chain in running]
    tied = tie(*outs, *values)
    for chain, out in zip(running, tied):
        if chain.out is None:
            chain.x = out
        else:
            if chain.out is chain.x:
                chain.x = out
            chain.out = out
            chain.fire()
    return tied[len(running) :]


def tie(*values):
    return lax.optimization_barrier(values)


def body(
    inputs_long,
    inputs_short,
    steps_long,
    steps_short,
    lengths,
    time_table,
    attngain,
    attnshift,
    qkvweight,
    querybias,
    valuebias,
    projweight,
    projbias,
    mlpgain,
    mlpshift,
    upweight,
    upbias,
    downweight,
    downbias,
    upstream_long,
    upstream_short,
):
    tokens, width = inputs_long.shape[1], inputs_long.shape[2]
    side = lax.axis_index("ulysses")
    core = lax.axis_index("core")
    meta = jnp.stack([side * tokens, side, 1 - core]).astype(jnp.int32)
    vecs, ub = pack(
        (attngain, attnshift, querybias, valuebias, projbias, mlpgain, mlpshift, downbias), upbias
    )

    edge = lax.dynamic_slice_in_dim(inputs_short[0], (1 - side) * (tokens - HALO), HALO, 0)
    across = (swap_with(inputs_long[0], "ulysses"), swap_with(edge, "ulysses"))

    q, ko, vo, start, rows, norm_s, norm_k = own_tokens(
        lengths, steps_short, steps_long, meta, inputs_long, inputs_short, time_table, vecs, qkvweight
    )
    kr, vr, norm_s, norm_k = far_tokens(lengths, meta, *across, rows, vecs, qkvweight, norm_s, norm_k)
    att, lse, bias = attend(lengths, meta, q, ko, vo, kr, vr)
    core_swap = lambda x: swap_with(x, "core")
    send, n2, seed, mid, outacc, dn2acc, att_s, att_k, ub_a = ffn_a(
        meta, att, start, upstream_long, upstream_short, vecs, ub, projweight, upweight, downweight
    )
    send, n2 = tie(send, n2)
    got = core_swap(send)
    out_long, out_short, keep, dbr, datt, sums_mlp, ub_b = ffn_b(
        meta, n2, seed, mid, outacc, dn2acc, vecs, ub, projweight, upweight, downweight
    )
    mlp = Chain(keep, got, 2)
    (datt,) = advance((datt,), mlp)

    count = width // PAIR // GROUPS
    grads, head_sums = [], []
    for n in range(GROUPS):
        d, sums = attend_back(n * count, count, q, ko, vo, kr, vr, datt, lse, bias)
        grads.append(d)
        head_sums.append(sums[0:2])
        if n:
            datt, *grads = advance((datt, *grads), mlp)
        else:
            datt, *grads = tie(datt, *grads)
    shares = lambda norm, att_half: jnp.concatenate(
        [outer(norm, d) for d in grads] + [outer(att_half, dbr)], 1
    )
    send = shares(norm_s, att_s)
    send, *grads = tie(send, *grads)
    got = core_swap(send)
    rest = Chain(shares(norm_k, att_k), got, 0)
    grads = advance(grads, rest)
    grads = advance(grads, mlp, rest)
    back = far_grad(meta, grads, qkvweight, kr.shape[0])
    (back,) = advance((back,), rest)
    back = swap_with(back, "ulysses")
    grads = advance(grads, mlp)
    in_long, in_short, sums_in = near_grad(meta, grads, qkvweight, back, start, dbr, vecs)
    small = Butterfly(
        jnp.concatenate(
            [
                sums_in[0:2],
                jnp.concatenate(head_sums, 1),
                sums_mlp[0:4],
                (ub_a + ub_b).reshape(-1, width),
            ],
            0,
        )
    )
    advance((), mlp, small)
    advance((), rest, small)
    advance((), rest, small)
    while not mlp.done:
        advance((), mlp)
    mlp_other = core_swap(mlp.x)
    held = mlp_place(meta, False, mlp.x)
    turn = 0
    while not (rest.done and small.done):
        live = not rest.done
        if turn == 1:
            held = advance(held, rest, small)
        else:
            advance((), rest, small)
        turn += 1
        if live and rest.done:
            rest_other = core_swap(rest.x)
            placed = att_place(meta, False, rest.x)
    *placed, mlp_other = tie(*placed, mlp_other)
    held = mlp_place(meta, True, mlp_other, held)
    g_down, g_up, rest_other = tie(*held, rest_other)
    g_qkv, g_proj = att_place(meta, True, rest_other, placed)
    small = small.x
    return (
        out_long,
        out_short,
        in_long,
        in_short,
        small[0],
        small[1],
        g_qkv,
        small[2],
        small[3],
        g_proj,
        small[4],
        small[5],
        small[6],
        g_up,
        small[8:].reshape(-1),
        g_down,
        small[7],
    )


def solution(mesh):
    seq, pair = mesh.shape["seq"], mesh.shape["ulysses"]
    split = jax.sharding.Mesh(mesh.devices.reshape(seq // 2, 2, pair), ("chips", "core", "ulysses"))
    rows = ("chips", "core")
    tokens = P(rows, "ulysses", None)
    placed = (tokens, tokens, P(rows), P(rows, None), P(rows, None)) + (P(),) * 14 + (tokens,) * 2
    return jax.shard_map(
        body,
        mesh=split,
        in_specs=placed,
        out_specs=(tokens,) * 4 + (P(),) * 13,
        check_vma=False,
    )
```
